32 devices in a mesh: parts: 2 (over y), gx: 4 (over z), gy: 2 (over x), gz: 2 (over core).
Axes of the slice: x: 2, y: 2, z: 4, core: 2. Of those that a mesh axis runs over, the one named last changes fastest.
Arguments:
- species: int32 [2048], P(('parts', 'gx', 'gy', 'gz')), parts along dimension 0, may hold values from 0 to 1
- send_x: int32 [32, 2, 176], P(('parts', 'gx', 'gy', 'gz')), parts along dimension 0, may hold values from 0 to 295, as said below
- send_y: int32 [32, 2, 80], P(('parts', 'gx', 'gy', 'gz')), parts along dimension 0, may hold values from 0 to 135, as said below
- send_z: int32 [32, 2, 36], P(('parts', 'gx', 'gy', 'gz')), parts along dimension 0, may hold values from 0 to 63, as said below
- edge_first: int32 [32, 1280], P(('parts', 'gx', 'gy', 'gz')), parts along dimension 0, may hold values from 0 to 63
- edge_second: int32 [32, 1280], P(('parts', 'gx', 'gy', 'gz')), parts along dimension 0, may hold values from 0 to 647, as said below
- edge_live: int32 [32, 1280], P(('parts', 'gx', 'gy', 'gz')), parts along dimension 0, may hold values from 0 to 1, as said below
- edge_vec: float32 [3, 40960], P(None, ('parts', 'gx', 'gy', 'gz')), parts along dimension 1, may hold values from -4.9 to 4.9, as said below
- embed: float32 [2, 128], replicated, may hold values from -6 to 6
- radial_in: float32 [2, 8, 64], replicated, may hold values from -6 to 6
- radial_mid: float32 [2, 64, 64], replicated, may hold values from -1.5 to 1.5
- radial_out: float32 [2, 64, 384], replicated, may hold values from -1.5 to 1.5
- mix: float32 [2, 128, 128], replicated, may hold values from -0.5 to 0.5
- update: float32 [2, 384, 128], replicated, may hold values from -0.3125 to 0.3125
- readout: float32 [2, 128], replicated, may hold values from -0.5 to 0.5
Outputs:
- energies: float32 [2048], P(('parts', 'gx', 'gy', 'gz')), parts along dimension 0
- forces: float32 [3, 2048], P(None, ('parts', 'gx', 'gy', 'gz')), parts along dimension 1
The draws below stay inside these ranges and needn't reach their ends.
There are 2 independent parts, one for each index of `parts`. The reference program is written for one: setup_inputs(seed, part) draws one part's arguments, and reference() takes and returns one part's arrays. A program takes and returns all parts, laid end to end along the dimension named above; an argument that names none is the same for every part. Nothing has to cross between parts.
Inputs may be any that keep to these rules, and one draw needn't show every extreme that they name: `send_x`: the entries of one domain and side are distinct. `send_y`: the entries of one domain and side are distinct. `send_z`: the entries of one domain and side are distinct. `edge_second`: in each domain's row the entries below 64 come first, and each of them differs from edge_first's entry. `edge_live`: each domain's row is ones then zeros, with at least 640 ones and at least as many ones as edge_second has entries below 64; some domain's row is all ones. `edge_vec`: every column has length between 1 and 4.9.
All inputs are finite; a program needn't handle non-finite values.
Results may differ from the reference program's by a relative error of at most 0.0003.
Values sent between devices are 32-bit elements; how exact they have to be, the bound alone decides.
No kernel may reach another device: no remote copies, remote signals or barrier semaphores. Data moves between devices by JAX's collectives and lax.ppermute only.
A program may use at most 64 MiB of HBM per device.

```python
import math
import jax
import jax.numpy as jnp
from jax import lax

C = 128
RADIAL = 64
NBASIS = 8
LAYERS = 2
KINDS = 2
A_DEV = 64
E_DEV = 1280
GZ_FACE = 36
GY_FACE = 80
GX_FACE = 176
GHOSTS = 584
DOMAINS = 16
ATOMS = 1024
N_GX = 4
N_GY = 2
N_GZ = 2


def face_lists(key, face, span):
    keys = jax.random.split(key, DOMAINS * 2)

    def one_list(single):
        return jax.random.permutation(single, span)[:face]
    rows = jax.vmap(one_list)(keys)
    return rows.reshape(DOMAINS, 2, face).astype(jnp.int32)


def draw_send_x(key, part):
    key = jax.random.fold_in(key, 11)
    return face_lists(key, GX_FACE, A_DEV + 2 * GZ_FACE + 2 * GY_FACE)


def draw_send_y(key, part):
    key = jax.random.fold_in(key, 12)
    return face_lists(key, GY_FACE, A_DEV + 2 * GZ_FACE)


def draw_send_z(key, part):
    key = jax.random.fold_in(key, 13)
    return face_lists(key, GZ_FACE, A_DEV)


def edge_lists(key):
    keys = jax.random.split(key, 6)
    live_count = jax.random.randint(keys[0], (DOMAINS,), E_DEV // 2, E_DEV + 1)
    fullest = jax.random.randint(keys[1], (), 0, DOMAINS)
    live_count = jnp.where(jnp.arange(DOMAINS) == fullest, E_DEV, live_count)
    eighths = jax.random.randint(keys[2], (DOMAINS,), 2, 5)
    inner_count = live_count * eighths // 8
    position = jnp.arange(E_DEV, dtype=jnp.int32)[None, :]
    first = jax.random.randint(keys[3], (DOMAINS, E_DEV), 0, A_DEV)
    first = jnp.where(position == 0, A_DEV - 1, first)
    first = jnp.where(position == 1, 0, first)
    step_own = jax.random.randint(keys[4], (DOMAINS, E_DEV), 1, A_DEV)
    ghost = jax.random.randint(keys[5], (DOMAINS, E_DEV), 0, GHOSTS)
    ghost = jnp.where(position == E_DEV - 1, GHOSTS - 1, ghost)
    second = jnp.where(position < inner_count[:, None], (first + step_own) % A_DEV, A_DEV + ghost)
    live = (position < live_count[:, None]).astype(jnp.int32)
    return (first.astype(jnp.int32), second.astype(jnp.int32), live)


def draw_edge_first(key, part):
    return edge_lists(key)[0]


def draw_edge_second(key, part):
    return edge_lists(key)[1]


def draw_edge_live(key, part):
    return edge_lists(key)[2]


def draw_edge_vec(key, part):
    key = jax.random.fold_in(key, 17)
    key_polar, key_turn, key_length = jax.random.split(key, 3)
    count = DOMAINS * E_DEV
    cosine = jax.random.uniform(key_polar, (count,), jnp.float32, -1.0, 1.0)
    turn = jax.random.uniform(key_turn, (count,), jnp.float32, -math.pi, math.pi)
    length = jax.random.uniform(key_length, (count,), jnp.float32, 1.0, 4.9)
    sine = jnp.sqrt(jnp.maximum(1.0 - cosine * cosine, 0.0))
    return jnp.stack([length * sine * jnp.cos(turn), length * sine * jnp.sin(turn), length * cosine])


def with_ends(array, stream_key, low, largest):
    extent = array.shape
    place = [jax.random.randint(jax.random.fold_in(stream_key, axis), (), 0, extent[axis]) for axis in range(len(extent))]
    array = array.at[tuple(place)].set(low)
    longest = extent.index(max(extent))
    place[longest] = (place[longest] + 1) % extent[longest]
    return array.at[tuple(place)].set(largest)


def bell_draw(stream_key, shape, scale, reach, kind=jnp.bfloat16):
    drawn = jax.random.normal(stream_key, shape, jnp.float32) * scale
    return jnp.minimum(jnp.maximum(drawn, -reach), reach).astype(kind)


def setup_inputs(seed: int = 0, part: int = 0) -> dict:
    arg_keys = jax.random.split(jax.random.key(seed), 16)
    part_splits = jax.random.split(jax.random.fold_in(arg_keys[15], part), 16)
    species = with_ends(jax.random.randint(part_splits[0], (ATOMS,), 0, KINDS), jax.random.fold_in(part_splits[0], 1), 0, KINDS - 1).astype(jnp.int32)
    send_x = draw_send_x(jax.random.fold_in(jax.random.fold_in(arg_keys[15], part), 71), part)
    send_y = draw_send_y(jax.random.fold_in(jax.random.fold_in(arg_keys[15], part), 71), part)
    send_z = draw_send_z(jax.random.fold_in(jax.random.fold_in(arg_keys[15], part), 71), part)
    edge_first = draw_edge_first(jax.random.fold_in(jax.random.fold_in(arg_keys[15], part), 71), part)
    edge_second = draw_edge_second(jax.random.fold_in(jax.random.fold_in(arg_keys[15], part), 71), part)
    edge_live = draw_edge_live(jax.random.fold_in(jax.random.fold_in(arg_keys[15], part), 71), part)
    edge_vec = draw_edge_vec(jax.random.fold_in(jax.random.fold_in(arg_keys[15], part), 71), part)
    embed = bell_draw(arg_keys[8], (KINDS, C), 1.0, 6.0, jnp.float32)
    radial_in = bell_draw(arg_keys[9], (LAYERS, NBASIS, RADIAL), 1 ** -0.5, 6.0, jnp.float32)
    radial_mid = bell_draw(arg_keys[10], (LAYERS, RADIAL, RADIAL), (RADIAL // 4) ** -0.5, 1.5, jnp.float32)
    radial_out = bell_draw(arg_keys[11], (LAYERS, RADIAL, 3 * C), (RADIAL // 4) ** -0.5, 1.5, jnp.float32)
    mix = bell_draw(arg_keys[12], (LAYERS, C, C), C ** -0.5, 0.5, jnp.float32)
    update = bell_draw(arg_keys[13], (LAYERS, 3 * C, C), (3 * C) ** -0.5, 0.3125, jnp.float32)
    readout = bell_draw(arg_keys[14], (LAYERS, C), C ** -0.5, 0.5, jnp.float32)
    return dict(species=species, send_x=send_x, send_y=send_y, send_z=send_z, edge_first=edge_first, edge_second=edge_second, edge_live=edge_live, edge_vec=edge_vec, embed=embed, radial_in=radial_in, radial_mid=radial_mid, radial_out=radial_out, mix=mix, update=update, readout=readout)


HIGH = lax.Precision.HIGHEST
CUTOFF = 5.0
INV_COUNT = 0.2
ROOT3 = math.sqrt(3.0)
ROOT5 = math.sqrt(5.0)
ROOT15 = math.sqrt(15.0)
DEGREES = (0, 1, 1, 1, 2, 2, 2, 2, 2)

def harmonics(vec):
    dist = jnp.sqrt(vec[0] * vec[0] + vec[1] * vec[1] + vec[2] * vec[2])
    unit_x = vec[0] / dist
    unit_y = vec[1] / dist
    unit_z = vec[2] / dist
    values = [jnp.ones_like(dist), ROOT3 * unit_x, ROOT3 * unit_y, ROOT3 * unit_z, ROOT15 * unit_x * unit_y, ROOT15 * unit_y * unit_z, 0.5 * ROOT5 * (3.0 * unit_z * unit_z - 1.0), ROOT15 * unit_x * unit_z, 0.5 * ROOT15 * (unit_x * unit_x - unit_y * unit_y)]
    return (dist, values)

def radial(dist, live, radial_in, radial_mid, radial_out):
    orders = jnp.arange(1, radial_in.shape[0] + 1, dtype=jnp.float32)
    basis = math.sqrt(2.0 / CUTOFF) * jnp.sin(orders[None, :] * (math.pi / CUTOFF) * dist[:, None]) / dist[:, None]
    scaled = dist / CUTOFF
    envelope = 1.0 - 21.0 * scaled ** 5 + 35.0 * scaled ** 6 - 15.0 * scaled ** 7
    hidden = jax.nn.silu(jnp.dot(basis, radial_in, precision=HIGH))
    hidden = jax.nn.silu(jnp.dot(hidden, radial_mid, precision=HIGH))
    return jnp.dot(hidden, radial_out, precision=HIGH) * (envelope * live)[:, None]

def edge_terms(feat_first, feat_second, vec, live, radial_in, radial_mid, radial_out):
    width = feat_first.shape[1]
    dist, values = harmonics(vec)
    weights = radial(dist, live, radial_in, radial_mid, radial_out)
    to_first = []
    to_second = []
    for order, degree in enumerate(DEGREES):
        factor = weights[:, degree * width:(degree + 1) * width] * values[order][:, None] * INV_COUNT
        parity = -1.0 if degree == 1 else 1.0
        to_first.append(factor * feat_second)
        to_second.append(parity * factor * feat_first)
    return (jnp.concatenate(to_first, axis=1), jnp.concatenate(to_second, axis=1))

def invariants(amat, width):
    count = amat.shape[0]
    vector_part = amat[:, width:4 * width].reshape(count, 3, width)
    tensor_part = amat[:, 4 * width:].reshape(count, 5, width)
    return jnp.concatenate([amat[:, :width], lax.optimization_barrier(jnp.sum(vector_part * vector_part, axis=1)), lax.optimization_barrier(jnp.sum(tensor_part * tensor_part, axis=1))], axis=1)

def node_update(features, amat, update):
    preact = jnp.dot(invariants(amat, features.shape[1]), update, precision=HIGH)
    return (features + jax.nn.silu(preact), preact)

def update_back(d_features, preact, amat, update):
    width = d_features.shape[1]
    gate = jax.nn.sigmoid(preact)
    d_pre = d_features * gate * (1.0 + preact * (1.0 - gate))
    d_inv = jnp.dot(d_pre, update.T, precision=HIGH)
    return jnp.concatenate([d_inv[:, :width], 2.0 * amat[:, width:4 * width] * jnp.tile(d_inv[:, width:2 * width], (1, 3)), 2.0 * amat[:, 4 * width:] * jnp.tile(d_inv[:, 2 * width:], (1, 5))], axis=1)

def neighbour_of(domain, axis, side):
    coord_x = domain // (N_GY * N_GZ)
    coord_y = domain // N_GZ % N_GY
    coord_z = domain % N_GZ
    step = 1 - 2 * side
    if axis == 0:
        coord_x = (coord_x + step) % N_GX
    elif axis == 1:
        coord_y = (coord_y + step) % N_GY
    else:
        coord_z = (coord_z + step) % N_GZ
    return (coord_x * N_GY + coord_y) * N_GZ + coord_z

def gather_sum(mixed, first_global, second_global, vecs, lives, params):

    def step(total, block):
        first_rows, second_rows, vec_block, live_block = block
        to_first, to_second = edge_terms(mixed[first_rows], mixed[second_rows], vec_block, live_block, *params)
        return (total.at[first_rows].add(to_first).at[second_rows].add(to_second), None)
    total = jnp.zeros((mixed.shape[0], 9 * mixed.shape[1]), jnp.float32)
    return lax.scan(step, total, (first_global, second_global, vecs, lives))[0]

def scatter_back(mixed, d_amat, first_global, second_global, vecs, lives, params):

    def step(d_mixed, block):
        first_rows, second_rows, vec_block, live_block = block

        def local(left, right, vec_in):
            return edge_terms(left, right, vec_in, live_block, *params)
        _, back = jax.vjp(local, mixed[first_rows], mixed[second_rows], vec_block)
        d_left, d_right, d_block = back((d_amat[first_rows], d_amat[second_rows]))
        return (d_mixed.at[first_rows].add(d_left).at[second_rows].add(d_right), d_block)
    return lax.scan(step, jnp.zeros_like(mixed), (first_global, second_global, vecs, lives))

def reference(species, send_x, send_y, send_z, edge_first, edge_second, edge_live, edge_vec, embed, radial_in, radial_mid, radial_out, mix, update, readout):
    domain = jnp.arange(DOMAINS, dtype=jnp.int32)
    ext_global = domain[:, None] * A_DEV + jnp.arange(A_DEV, dtype=jnp.int32)[None, :]
    for axis, tables in ((2, send_z), (1, send_y), (0, send_x)):
        pieces = [ext_global]
        for side in range(2):
            neighbour = neighbour_of(domain, axis, side)
            pieces.append(jnp.take_along_axis(ext_global[neighbour], tables[neighbour, 1 - side], axis=1))
        ext_global = jnp.concatenate(pieces, axis=1).astype(jnp.int32)
    second_global = jnp.take_along_axis(ext_global, edge_second, axis=1).astype(jnp.int32)
    first_global = (domain[:, None] * A_DEV + edge_first).astype(jnp.int32)
    vecs = jnp.transpose(edge_vec.reshape(3, DOMAINS, E_DEV), (1, 0, 2))
    lives = edge_live.astype(jnp.float32)
    features = embed[species]
    saved = []
    energies = jnp.zeros((ATOMS,), jnp.float32)
    for layer in range(LAYERS):
        params = (radial_in[layer], radial_mid[layer], radial_out[layer])
        mixed = jnp.dot(features, mix[layer], precision=HIGH)
        amat = gather_sum(mixed, first_global, second_global, vecs, lives, params)
        features, preact = node_update(features, amat, update[layer])
        saved.append((mixed, amat, preact))
        energies = energies + jnp.dot(features, readout[layer], precision=HIGH)
    d_features = jnp.zeros((ATOMS, embed.shape[1]), jnp.float32)
    d_vec_total = jnp.zeros_like(vecs)
    for layer in reversed(range(LAYERS)):
        mixed, amat, preact = saved[layer]
        params = (radial_in[layer], radial_mid[layer], radial_out[layer])
        d_features = d_features + readout[layer][None, :]
        d_amat = update_back(d_features, preact, amat, update[layer])
        d_mixed, d_vec = scatter_back(mixed, d_amat, first_global, second_global, vecs, lives, params)
        d_vec_total = d_vec_total + d_vec
        d_features = d_features + jnp.dot(d_mixed, mix[layer].T, precision=HIGH)
    pulls = jnp.transpose(d_vec_total, (1, 0, 2)).reshape(3, DOMAINS * E_DEV)
    forces = jnp.zeros((3, ATOMS), jnp.float32)
    forces = forces.at[:, first_global.reshape(-1)].add(pulls).at[:, second_global.reshape(-1)].add(-pulls)
    return (energies, forces)
```

```python
import functools
import math

import jax
import jax.numpy as jnp
from jax import lax
from jax.experimental import pallas as pl
from jax.experimental.pallas import tpu as pltpu
from jax.sharding import PartitionSpec as P

HIGH = lax.Precision.HIGHEST
CUTOFF = 5.0
INV_COUNT = 0.2
ROOT3 = math.sqrt(3.0)
ROOT5 = math.sqrt(5.0)
ROOT15 = math.sqrt(15.0)
SPANS = ((0, 1), (1, 3), (4, 5))
LANES = 128
BLOCK = 256
F32 = jnp.float32
BF16 = jnp.bfloat16
NT = (((1,), (1,)), ((), ()))
NN = (((1,), (0,)), ((), ()))


def round_up(value, unit):
    return -(-value // unit) * unit


def dot(left, right, dims=NN):
    return lax.dot_general(left, right, dims, preferred_element_type=F32)


def dot_high(left, right, dims=NN):
    return lax.dot_general(left, right, dims, preferred_element_type=F32, precision=HIGH)


def split(value):
    high = value.astype(BF16)
    return high, (value - high.astype(F32)).astype(BF16)


def split_f32(value):
    high = value.astype(BF16).astype(F32)
    return high, value - high


def stack_weights(value):
    high, low = split_f32(value)
    return jnp.concatenate([high, low, high], axis=0).T.astype(BF16)


def stack_acts(value):
    high, low = split(value)
    return jnp.concatenate([high, high, low], axis=0)


def stack_acts_f32(value):
    high, low = split_f32(value)
    return jnp.concatenate([high, high, low, jnp.zeros_like(low)], axis=0).astype(BF16)


def iota(shape, dim):
    return lax.broadcasted_iota(jnp.int32, shape, dim)


def sigmoid(value):
    return 0.5 * jnp.tanh(0.5 * value) + 0.5


def axis_steps(size):
    return (0, 1, -1) if size > 2 else tuple(range(size))


class Neighbourhood:
    def __init__(self, sizes):
        self.sizes = sizes
        self.shifts = [
            (dx, dy, dz)
            for dx in axis_steps(sizes[0])
            for dy in axis_steps(sizes[1])
            for dz in axis_steps(sizes[2])
        ]
        self.place = {
            tuple(s % n for s, n in zip(shift, sizes)): b for b, shift in enumerate(self.shifts)
        }
        self.count = len(self.shifts)

    def block(self, *shift):
        return self.place[tuple(s % n for s, n in zip(shift, self.sizes))]

    def opposite(self, block):
        return self.block(*(-s for s in self.shifts[block]))

    def pairs(self, shift):
        nx, ny, nz = self.sizes
        out = []
        for i in range(nx):
            for j in range(ny):
                for k in range(nz):
                    here = (i * ny + j) * nz + k
                    there = ((i + shift[0]) % nx * ny + (j + shift[1]) % ny) * nz + (k + shift[2]) % nz
                    out.append((here, there))
        return out

    def fetch(self, rows):
        got = [rows]
        for shift in self.shifts[1:]:
            pairs = [(there, here) for here, there in self.pairs(shift)]
            got.append(lax.ppermute(rows, ("gx", "gy", "gz"), pairs))
        return got

    def give(self, blocks):
        got = [blocks[0]]
        for block, shift in zip(blocks[1:], self.shifts[1:]):
            got.append(lax.ppermute(block, ("gx", "gy", "gz"), self.pairs(shift)))
        return got


def resolve_kernel(hood, faces, own, edges, *refs):
    count = hood.count
    tables = refs[:count]
    first_ref, second_ref, live_ref, vec_ref, own_out, sent_out, matrix = refs[count:]
    face_z, face_y, face_x = faces
    z_end = own + 2 * face_z
    y_end = z_end + 2 * face_y
    x_end = y_end + 2 * face_x
    width = tables[0].shape[1]
    lane = iota((1, width), 1)
    sub8 = iota((8, width), 0)
    payload = [table[...] for table in tables]

    def rows(block, atom):
        shape = (8, atom.shape[1])
        return jnp.where(
            iota(shape, 0) == 0, jnp.broadcast_to(block, shape), jnp.broadcast_to(atom, shape)
        )

    def z_list(dx, dy):
        plus, minus = hood.block(dx, dy, 1), hood.block(dx, dy, -1)
        in_own, in_plus = lane < own, lane < own + face_z
        atom = jnp.where(
            in_own,
            lane.astype(F32),
            jnp.where(in_plus, payload[plus], payload[minus]),
        )
        block = jnp.where(
            in_own, float(hood.block(dx, dy, 0)), jnp.where(in_plus, float(plus), float(minus))
        )
        return rows(block, atom)

    def lookup(table, index):
        depth = table.shape[1]
        hot = (iota((depth, index.shape[1]), 0) == index).astype(F32).astype(BF16)
        return dot(table.astype(BF16), hot)

    def extend(inner, sides, begin, middle, end, raw_plus, raw_minus):
        low, high = begin // LANES * LANES, round_up(end, LANES)
        spot = lane[:, low:high]
        depth = round_up(begin, LANES)
        raw = jnp.where(spot < middle, raw_plus[:, low:high], raw_minus[:, low:high])
        raw = raw.astype(jnp.int32)
        plus = lookup(sides[0][:, :depth], raw)
        minus = plus if sides[1] is sides[0] else lookup(sides[1][:, :depth], raw)
        section = jnp.where(spot < middle, plus, minus)
        if depth > low:
            head = jnp.where(spot[:, : depth - low] < begin, inner[:, low:depth], section[:, : depth - low])
            section = jnp.concatenate([head, section[:, depth - low :]], axis=1)
        return section if low == 0 else jnp.concatenate([inner[:, :low], section], axis=1)

    z_lists = {}

    def z_cached(dx, dy):
        key = hood.block(dx, dy, 0)
        if key not in z_lists:
            z_lists[key] = z_list(dx, dy)
        return z_lists[key]

    def y_list(dx):
        return extend(
            z_cached(dx, 0),
            (z_cached(dx, 1), z_cached(dx, -1)),
            z_end,
            z_end + face_y,
            y_end,
            payload[hood.block(dx, 1, 0)],
            payload[hood.block(dx, -1, 0)],
        )

    plus_list = y_list(1)
    minus_list = plus_list if hood.block(1, 0, 0) == hood.block(-1, 0, 0) else y_list(-1)
    full = extend(
        y_list(0),
        (plus_list, minus_list),
        y_end,
        y_end + face_x,
        x_end,
        payload[hood.block(1, 0, 0)],
        payload[hood.block(-1, 0, 0)],
    )
    depth = full.shape[1]

    buckets = round_up(count + 1, 8)
    kinds = jnp.concatenate(
        [table[:, x_end : x_end + own] for table in payload]
        + [jnp.zeros((buckets - count, own), F32)],
        axis=0,
    ).astype(BF16)
    before = (iota((BLOCK, BLOCK), 0) < iota((BLOCK, BLOCK), 1)).astype(F32).astype(BF16)
    chunks = range(0, edges, BLOCK)
    spread = []
    seen = jnp.zeros((buckets, 1), F32)
    lower = jnp.zeros((buckets, 1), F32)
    rank_of = []
    bucket_of = []
    for start in chunks:
        at = slice(start, start + BLOCK)
        first = first_ref[:, at]
        live = live_ref[:, at] > 0
        found = lookup(full, second_ref[:, at])
        block, atom = found[0:1], found[1:2]
        hot_block = (iota((buckets, BLOCK), 0) == block.astype(jnp.int32)).astype(F32)
        atom_hot = (iota((own, BLOCK), 0) == atom.astype(jnp.int32)).astype(F32).astype(BF16)
        first_hot = (iota((own, BLOCK), 0) == first).astype(F32).astype(BF16)
        kind_second = jnp.sum(dot(kinds, atom_hot) * hot_block, axis=0, keepdims=True)
        kind_first = dot(kinds[:16], first_hot)[0:1]
        spread.append((first.astype(F32), block, atom, kind_first, kind_second))
        live_f = live.astype(F32)
        hot_live = hot_block * live_f
        rank_of.append(dot(hot_live.astype(BF16), before) + seen)
        bucket_of.append((hot_live, live_f))
        seen = seen + jnp.sum(hot_live, axis=1, keepdims=True)
        smaller = (block.astype(jnp.int32) < iota((buckets, BLOCK), 0)).astype(F32) * live_f
        lower = lower + jnp.sum(smaller, axis=1, keepdims=True)

    meta = jnp.sum(
        jnp.where(iota((buckets, LANES), 0) == iota((buckets, LANES), 1), lower, 0.0),
        axis=0,
        keepdims=True,
    )
    sub = iota((8, BLOCK), 0)
    data = []
    for number, start in enumerate(chunks):
        at = slice(start, start + BLOCK)
        hot_live, live_f = bucket_of[number]
        spot = jnp.sum(hot_live * (rank_of[number] + lower), axis=0, keepdims=True)
        spot = jnp.where(live_f > 0.0, spot, -1.0).astype(jnp.int32)
        matrix[:, at] = (iota((edges, BLOCK), 0) == spot).astype(F32).astype(BF16)
        first, block, atom, kind_first, kind_second = spread[number]
        vec = vec_ref[:, at]
        high, rest = split_f32(vec)
        middle, low = split_f32(rest)
        pad5 = jnp.zeros((5, BLOCK), F32)
        top = jnp.concatenate([high, first, atom, block, kind_first, kind_second], axis=0)
        data.append(
            jnp.concatenate(
                [top, jnp.concatenate([middle, pad5], axis=0), jnp.concatenate([low, pad5], axis=0)],
                axis=0,
            ).astype(BF16)
        )
    data = jnp.concatenate(data, axis=1)
    for number, start in enumerate(chunks):
        at = slice(start, start + BLOCK)
        moved = dot(data, matrix[at, :], NT)
        record = moved[0:8] + moved[8:16] + moved[16:24]
        own_out[:, at] = record
        swapped = jnp.where(
            sub == 3,
            record[4:5],
            jnp.where(sub == 4, record[3:4], jnp.where(sub == 7, record[6:7], 0.0)),
        )
        sent = jnp.where(sub < 3, -record, swapped)
        if start == 0:
            head = jnp.where(sub[:, :LANES] == 6, meta, sent[:, :LANES])
            sent_out[:, :LANES] = head
            sent_out[:, LANES:BLOCK] = sent[:, LANES:]
        else:
            sent_out[:, at] = sent


def prepare_kernel(in_ref, mid_ref, out_ref, *outs):
    for layer in range(in_ref.shape[0]):
        into = in_ref[layer]
        middle = mid_ref[layer]
        last = out_ref[layer]
        in_fw, mid_fw, out_fw, in_bw, mid_bw, out_bw = (out.at[layer] for out in outs)
        high, low = split_f32(into)
        in_fw[...] = (
            jnp.concatenate([high, low, high, jnp.zeros_like(high)], axis=0).T.astype(BF16)
        )
        mid_fw[...] = stack_weights(middle)
        out_fw[...] = stack_weights(last)
        into_t = jnp.concatenate([into, jnp.zeros_like(into)], axis=0).T
        in_bw[...] = stack_weights(into_t)
        mid_bw[...] = stack_weights(middle.T)
        high, low = split(last)
        out_bw[...] = jnp.concatenate([high, low, high], axis=1)


def geometry(chunk, need_slopes):
    vec = [chunk[k : k + 1] for k in range(3)]
    dist = jnp.sqrt(vec[0] * vec[0] + vec[1] * vec[1] + vec[2] * vec[2])
    inv = 1.0 / dist
    ux, uy, uz = (v * inv for v in vec)
    values = [
        jnp.ones_like(dist),
        ROOT3 * ux,
        ROOT3 * uy,
        ROOT3 * uz,
        ROOT15 * ux * uy,
        ROOT15 * uy * uz,
        0.5 * ROOT5 * (3.0 * uz * uz - 1.0),
        ROOT15 * ux * uz,
        0.5 * ROOT15 * (ux * ux - uy * uy),
    ]
    orders = (iota((8, dist.shape[1]), 0) + 1).astype(F32) * (math.pi / CUTOFF)
    angle = orders * dist
    scale = math.sqrt(2.0 / CUTOFF) * inv
    basis = jnp.sin(angle) * scale
    x = dist * (1.0 / CUTOFF)
    x2 = x * x
    x4 = x2 * x2
    envelope = 1.0 + x4 * x * (-21.0 + x * (35.0 - 15.0 * x))
    slopes = None
    if need_slopes:
        d_basis = orders * jnp.cos(angle) * scale - basis * inv
        d_envelope = x4 * (-105.0 + x * (210.0 - 105.0 * x)) * (1.0 / CUTOFF)
        slopes = (d_basis, d_envelope)
    return inv, (ux, uy, uz), values, basis, envelope, slopes


def radial_hidden(basis, in_fw, mid_fw):
    z1 = dot(in_fw, stack_acts_f32(basis))
    gate1 = sigmoid(z1)
    z2 = dot(mid_fw, stack_acts(z1 * gate1))
    return z1, gate1, z2, sigmoid(z2)


def scaled_hots(chunk, own, values):
    target = chunk[3:4].astype(jnp.int32)
    mask = iota((own, target.shape[1]), 0) == target
    highs, lows = [], []
    for begin, size in SPANS:
        high = []
        low = []
        for m in range(begin, begin + size):
            y_high, y_low = split_f32(values[m])
            high.append(jnp.where(mask, y_high, 0.0).astype(BF16))
            low.append(jnp.where(mask, y_low, 0.0).astype(BF16))
        highs.append(jnp.concatenate(high, axis=0))
        lows.append(jnp.concatenate(low, axis=0))
    return mask, highs, lows


def other_hot(chunk, own, total):
    code = (chunk[5:6] * float(own) + chunk[4:5]).astype(jnp.int32)
    return (iota((total, code.shape[1]), 0) == code).astype(F32).astype(BF16)


def read_chunk(edges_ref, step):
    return edges_ref[:, pl.ds(pl.multiple_of(step * BLOCK, BLOCK), BLOCK)]


def kind_features(chunk, columns):
    kind = chunk[7:8]
    out = jnp.where(kind == 0.0, columns[0], 0.0)
    for index in range(1, len(columns)):
        out = out + jnp.where(kind == float(index), columns[index], 0.0)
    return out


def collect(amat, chunk, feat, values, envelope, hidden, out_fw, own):
    z2, gate2 = hidden
    width = feat.shape[0]
    units = z2 * gate2 * (INV_COUNT * envelope)
    weights = dot(out_fw, stack_acts(units))
    _, highs, lows = scaled_hots(chunk, own, values)
    for degree, (begin, size) in enumerate(SPANS):
        high, low = split(weights[degree * width : (degree + 1) * width] * feat)
        left = jnp.concatenate([highs[degree], lows[degree], highs[degree]], axis=1)
        right = jnp.concatenate([high, high, low], axis=1)
        at = slice(begin * own, (begin + size) * own)
        amat[at, :] += dot(left, right, NT)


def node_forward(amat, features, update, own):
    parts = [amat[m * own : (m + 1) * own, :] for m in range(9)]
    inv1 = sum(p * p for p in parts[1:4])
    inv2 = sum(p * p for p in parts[4:9])
    preact = dot_high(jnp.concatenate([parts[0], inv1, inv2], axis=1), update)
    return features + preact * sigmoid(preact), preact


def node_back(amat, d_features, preact, update, own, d_amat, turned):
    width = d_features.shape[1]
    gate = sigmoid(preact)
    d_pre = d_features * gate * (1.0 + preact * (1.0 - gate))
    d_inv = dot_high(d_pre, update, NT)
    for degree, (begin, size) in enumerate(SPANS):
        rows = []
        for m in range(begin, begin + size):
            value = d_inv[:, degree * width : (degree + 1) * width]
            if degree > 0:
                value = 2.0 * amat[m * own : (m + 1) * own, :] * value
            rows.append(value)
        rows = jnp.concatenate(rows, axis=0)
        high, low = split(rows)
        d_amat[begin * own : (begin + size) * own, :] = jnp.concatenate([high, low, high], axis=1)
        turned[degree][...] = stack_weights(rows)


def edge_backward(chunk, feat, own, in_fw, mid_fw, out_fw, in_bw, mid_bw, out_bw, d_amat, turned):
    width = feat.shape[0]
    inv, unit, values, basis, envelope, (d_basis, d_envelope) = geometry(chunk, True)
    z1, gate1, z2, gate2 = radial_hidden(basis, in_fw, mid_fw)
    scale = INV_COUNT * envelope
    units = z2 * gate2
    weights = dot(out_fw, stack_acts(units * scale))
    mask, highs, lows = scaled_hots(chunk, own, values)
    pulled = []
    d_mixed = 0.0
    d_values = []
    for degree, (begin, size) in enumerate(SPANS):
        weight = weights[degree * width : (degree + 1) * width]
        right = jnp.concatenate([highs[degree], highs[degree], lows[degree]], axis=0)
        term = dot(turned[degree][...], right)
        d_mixed = d_mixed + weight * term
        pulled.append(feat * term)
        high, low = split(weight * feat)
        spread = dot(
            d_amat[begin * own : (begin + size) * own, :],
            jnp.concatenate([high, high, low], axis=0),
        )
        for m in range(size):
            d_values.append(
                jnp.sum(jnp.where(mask, spread[m * own : (m + 1) * own], 0.0), axis=0, keepdims=True)
            )
    pulled = jnp.concatenate(pulled, axis=0)
    d_units = dot(out_bw, stack_acts(pulled))
    d_env = INV_COUNT * jnp.sum(units * d_units, axis=0, keepdims=True)
    d_z2 = d_units * scale * gate2 * (1.0 + z2 * (1.0 - gate2))
    d_hidden = dot(mid_bw, stack_acts(d_z2))
    d_z1 = d_hidden * gate1 * (1.0 + z1 * (1.0 - gate1))
    d_b = dot(in_bw, stack_acts(d_z1))[0:8]
    d_dist = jnp.sum(d_b * d_basis, axis=0, keepdims=True) + d_env * d_envelope
    ux, uy, uz = unit
    y = d_values
    dux = ROOT3 * y[1] + ROOT15 * (uy * y[4] + uz * y[7] + ux * y[8])
    duy = ROOT3 * y[2] + ROOT15 * (ux * y[4] + uz * y[5] - uy * y[8])
    duz = ROOT3 * y[3] + ROOT15 * (uy * y[5] + ux * y[7]) + 3.0 * ROOT5 * uz * y[6]
    along = ux * dux + uy * duy + uz * duz
    grad = [(du - u * along) * inv + d_dist * u for u, du in zip(unit, (dux, duy, duz))]
    return grad, d_mixed


def first_kernel(hood, own, edges, *refs):
    count = hood.count
    own_rec = refs[0]
    records = refs[1 : 1 + count]
    (
        species_ref,
        embed_ref,
        mix_ref,
        update_ref,
        in_fw,
        mid_fw,
        out_fw,
        list_out,
        total_out,
        amat_out,
        preact_out,
        h_out,
        w_out,
    ) = refs[1 + count :]
    lane = iota((1, LANES), 1)
    sub = iota((8, LANES), 0)
    dummy = jnp.where(sub == 0, 1.0, jnp.where((sub >= 3) & (sub <= 5), -1.0, 0.0))
    capacity = list_out.shape[1]

    def fill(step, _):
        list_out[:, pl.ds(pl.multiple_of(step * LANES, LANES), LANES)] = dummy
        return 0

    lax.fori_loop(edges // LANES, capacity // LANES, fill, 0)

    def scalar(row, index):
        return jnp.sum(jnp.where(lane == index, row, 0.0)).astype(jnp.int32)

    filled = scalar(records[0][6:7, :LANES], count)
    for start in range(0, edges, LANES):
        at = slice(start, start + LANES)
        list_out[:, at] = jnp.where(lane + start < filled, own_rec[:, at], dummy)
    last = edges // LANES - 1
    for b in range(count):
        record = records[b]
        bucket = hood.opposite(b)
        row = record[6:7, :LANES]
        begin = scalar(row, bucket)
        size = scalar(row, bucket + 1) - begin
        to = filled

        def place(step, _, record=record, begin=begin, size=size, to=to, b=b):
            window = step * LANES - to + begin
            low = lax.shift_right_arithmetic(window, 7)
            turn = jnp.bitwise_and(window, LANES - 1)
            left = jnp.clip(low, 0, last)
            right = jnp.clip(low + 1, 0, last)
            back = jnp.bitwise_and(LANES - turn, LANES - 1)
            one = pltpu.roll(record[:, pl.ds(pl.multiple_of(left * LANES, LANES), LANES)], back, 1)
            two = pltpu.roll(record[:, pl.ds(pl.multiple_of(right * LANES, LANES), LANES)], back, 1)
            rows = jnp.where(lane < LANES - turn, one, two)
            rows = jnp.where(sub == 5, float(b), rows)
            spot = lane + step * LANES
            here = pl.ds(pl.multiple_of(step * LANES, LANES), LANES)
            list_out[:, here] = jnp.where((spot >= to) & (spot < to + size), rows, list_out[:, here])
            return 0

        lax.fori_loop(
            lax.shift_right_arithmetic(to, 7),
            lax.shift_right_arithmetic(to + size + LANES - 1, 7),
            place,
            0,
        )
        filled = to + size
    steps = lax.shift_right_arithmetic(filled + BLOCK - 1, 8)
    total_out[0] = steps

    embed = embed_ref[...]
    mixed = dot_high(embed, mix_ref[0])
    columns = [mixed[k : k + 1].T for k in range(embed.shape[0])]
    amat_out[...] = jnp.zeros_like(amat_out)

    def body(step, _):
        chunk = read_chunk(list_out, step)
        _, _, values, basis, envelope, _ = geometry(chunk, False)
        _, _, z2, gate2 = radial_hidden(basis, in_fw[0], mid_fw[0])
        feat = kind_features(chunk, columns)
        collect(amat_out, chunk, feat, values, envelope, (z2, gate2), out_fw[0], own)
        return 0

    lax.fori_loop(0, steps, body, 0)
    kind = species_ref[...]
    features = jnp.where(kind == 0, embed[0:1], 0.0)
    for k in range(1, embed.shape[0]):
        features = features + jnp.where(kind == k, embed[k : k + 1], 0.0)
    h, preact = node_forward(amat_out, features, update_ref[0], own)
    preact_out[...] = preact
    h_out[...] = h
    w_out[...] = dot_high(h, mix_ref[1])


def second_kernel(count, own, *refs):
    blocks = refs[:count]
    (
        steps_ref,
        list_ref,
        h_ref,
        update_ref,
        readout_ref,
        in_fw,
        mid_fw,
        out_fw,
        in_bw,
        mid_bw,
        out_bw,
        energy_out,
        grad_out,
    ) = refs[count : count + 13]
    d_mixed_outs = refs[count + 13 : count + 13 + count]
    features_t, amat, d_amat, turn0, turn1, turn2, d_mixed_sum = refs[count + 13 + count :]
    turned = (turn0, turn1, turn2)
    total = count * own
    width = h_ref.shape[1]
    steps = steps_ref[0]
    everyone = jnp.concatenate([block[...] for block in blocks], axis=0)
    high, low = split_f32(everyone.T)
    features_t[...] = jnp.concatenate([high, low], axis=0).astype(BF16)
    amat[...] = jnp.zeros_like(amat)
    d_mixed_sum[...] = jnp.zeros_like(d_mixed_sum)

    def gather(hot):
        both = dot(features_t[...], hot)
        return both[:width] + both[width:]

    def forward(step, _):
        chunk = read_chunk(list_ref, step)
        _, _, values, basis, envelope, _ = geometry(chunk, False)
        _, _, z2, gate2 = radial_hidden(basis, in_fw[1], mid_fw[1])
        feat = gather(other_hot(chunk, own, total))
        collect(amat, chunk, feat, values, envelope, (z2, gate2), out_fw[1], own)
        return 0

    lax.fori_loop(0, steps, forward, 0)
    h1 = h_ref[...]
    h2, preact = node_forward(amat, h1, update_ref[1], own)
    readout = readout_ref[...]
    energy_out[...] = dot_high(readout[0:1], h1, NT) + dot_high(readout[1:2], h2, NT)
    d_features = jnp.broadcast_to(readout[1:2], h1.shape)
    node_back(amat, d_features, preact, update_ref[1], own, d_amat, turned)

    def backward(step, _):
        chunk = read_chunk(list_ref, step)
        hot = other_hot(chunk, own, total)
        grad, d_mixed = edge_backward(
            chunk,
            gather(hot),
            own,
            in_fw[1],
            mid_fw[1],
            out_fw[1],
            in_bw[1],
            mid_bw[1],
            out_bw[1],
            d_amat,
            turned,
        )
        at = pl.ds(pl.multiple_of(step * BLOCK, BLOCK), BLOCK)
        grad_out[:, at] = jnp.concatenate(grad + [jnp.zeros((5, BLOCK), F32)], axis=0)
        high, low = split(d_mixed)
        both = dot(hot, jnp.concatenate([high, low], axis=0), NT)
        d_mixed_sum[...] += both[:, :width] + both[:, width:]
        return 0

    lax.fori_loop(0, steps, backward, 0)
    for b, out in enumerate(d_mixed_outs):
        out[...] = d_mixed_sum[b * own : (b + 1) * own, :]


def last_kernel(count, own, *refs):
    blocks = refs[:count]
    (
        steps_ref,
        list_ref,
        grad_ref,
        amat_ref,
        preact_ref,
        embed_ref,
        mix_ref,
        update_ref,
        readout_ref,
        in_fw,
        mid_fw,
        out_fw,
        in_bw,
        mid_bw,
        out_bw,
    ) = refs[count : count + 15]
    force_outs = refs[count + 15 : count + 15 + count]
    d_amat, turn0, turn1, turn2, force = refs[count + 15 + count :]
    turned = (turn0, turn1, turn2)
    total = count * own
    steps = steps_ref[0]
    embed = embed_ref[...]
    mixed = dot_high(embed, mix_ref[0])
    columns = [mixed[k : k + 1].T for k in range(embed.shape[0])]
    d_mixed = sum(block[...] for block in blocks)
    readout = readout_ref[...]
    d_features = readout[0:1] + readout[1:2] + dot_high(d_mixed, mix_ref[1], NT)
    node_back(amat_ref, d_features, preact_ref[...], update_ref[0], own, d_amat, turned)
    force[...] = jnp.zeros_like(force)

    def backward(step, _):
        chunk = read_chunk(list_ref, step)
        grad, _ = edge_backward(
            chunk,
            kind_features(chunk, columns),
            own,
            in_fw[0],
            mid_fw[0],
            out_fw[0],
            in_bw[0],
            mid_bw[0],
            out_bw[0],
            d_amat,
            turned,
        )
        at = pl.ds(pl.multiple_of(step * BLOCK, BLOCK), BLOCK)
        pull = jnp.concatenate(grad + [jnp.zeros((5, BLOCK), F32)], axis=0) + grad_ref[:, at]
        high, rest = split_f32(pull)
        middle, low = split_f32(rest)
        parts = jnp.concatenate([high, middle, low, jnp.zeros_like(low)], axis=0).astype(BF16)
        code = (chunk[5:6] * float(own) + chunk[4:5]).astype(jnp.int32)
        row = iota((total, BLOCK), 0)
        target = chunk[3:4].astype(jnp.int32)
        hot = (row == target).astype(F32) - (row == code).astype(F32)
        moved = dot(parts, hot.astype(BF16), NT)
        force[...] += moved[0:8] + moved[8:16] + moved[16:24]
        return 0

    lax.fori_loop(0, steps, backward, 0)
    for b, out in enumerate(force_outs):
        out[...] = force[:, b * own : (b + 1) * own]


def call(kernel, outs, scratch, args, smem_in=(), smem_out=()):
    vmem = pl.BlockSpec(memory_space=pltpu.VMEM)
    smem = pl.BlockSpec(memory_space=pltpu.SMEM)
    return pl.pallas_call(
        kernel,
        out_shape=outs,
        in_specs=[smem if k in smem_in else vmem for k in range(len(args))],
        out_specs=[smem if k in smem_out else vmem for k in range(len(outs))],
        scratch_shapes=scratch,
        compiler_params=pltpu.CompilerParams(vmem_limit_bytes=40 * 1024 * 1024),
    )(*args)


def shards(
    sizes,
    species,
    send_x,
    send_y,
    send_z,
    edge_first,
    edge_second,
    edge_live,
    edge_vec,
    embed,
    radial_in,
    radial_mid,
    radial_out,
    mix,
    update,
    readout,
):
    hood = Neighbourhood(sizes)
    count = hood.count
    own = species.shape[0]
    width = embed.shape[1]
    layers = readout.shape[0]
    hidden = radial_mid.shape[1]
    slots = edge_first.shape[1]
    edges = round_up(slots, BLOCK)
    extra = edges - slots
    if extra:
        edge_first = jnp.pad(edge_first, ((0, 0), (0, extra)))
        edge_second = jnp.pad(edge_second, ((0, 0), (0, extra)))
        edge_live = jnp.pad(edge_live, ((0, 0), (0, extra)))
        edge_vec = jnp.pad(edge_vec, ((0, 0), (0, extra)), constant_values=1.0)
    faces = tuple(send.shape[2] for send in (send_z, send_y, send_x))
    pieces = [jnp.zeros((own,), jnp.int32)]
    for send in (send_z, send_y, send_x):
        pieces += [send[0, 1], send[0, 0]]
    pieces.append(species)
    length = own * 2 + 2 * sum(faces)
    pieces.append(jnp.zeros((round_up(length, LANES) - length,), jnp.int32))
    payload = jnp.concatenate(pieces).astype(F32)[None, :]

    shape = jax.ShapeDtypeStruct
    weights = call(
        prepare_kernel,
        [
            shape((layers, hidden, 32), BF16),
            shape((layers, hidden, 3 * hidden), BF16),
            shape((layers, 3 * width, 3 * hidden), BF16),
            shape((layers, 16, 3 * hidden), BF16),
            shape((layers, hidden, 3 * hidden), BF16),
            shape((layers, hidden, 9 * width), BF16),
        ],
        [],
        [radial_in, radial_mid, radial_out],
    )
    tables = hood.fetch(payload)
    own_rec, sent = call(
        functools.partial(resolve_kernel, hood, faces, own, edges),
        [shape((8, edges), F32), shape((8, edges), F32)],
        [pltpu.VMEM((edges, edges), BF16)],
        tables + [edge_first, edge_second, edge_live, edge_vec],
    )
    records = hood.fetch(sent)
    capacity = (count + 1) * edges
    edge_list, steps, amat1, preact1, h1, w2 = call(
        functools.partial(first_kernel, hood, own, edges),
        [
            shape((8, capacity), F32),
            shape((1,), jnp.int32),
            shape((9 * own, width), F32),
            shape((own, width), F32),
            shape((own, width), F32),
            shape((own, width), F32),
        ],
        [],
        [own_rec] + records + [species[:, None], embed, mix, update] + list(weights[:3]),
        smem_out=(1,),
    )
    mixed = hood.fetch(w2)
    turned = [pltpu.VMEM((width, 3 * size * own), BF16) for _, size in SPANS]
    results = call(
        functools.partial(second_kernel, count, own),
        [shape((1, own), F32), shape((8, capacity), F32)]
        + [shape((own, width), F32)] * count,
        [
            pltpu.VMEM((2 * width, count * own), BF16),
            pltpu.VMEM((9 * own, width), F32),
            pltpu.VMEM((9 * own, 3 * width), BF16),
        ]
        + turned
        + [pltpu.VMEM((count * own, width), F32)],
        mixed + [steps, edge_list, h1, update, readout] + list(weights),
        smem_in=(count,),
    )
    energies, grads = results[:2]
    d_mixed = hood.give(list(results[2:]))
    forces = call(
        functools.partial(last_kernel, count, own),
        [shape((8, own), F32)] * count,
        [pltpu.VMEM((9 * own, 3 * width), BF16)] + turned + [pltpu.VMEM((8, count * own), F32)],
        d_mixed
        + [steps, edge_list, grads, amat1, preact1, embed, mix, update, readout]
        + list(weights),
        smem_in=(count,),
    )
    forces = sum(part[:3] for part in hood.give(list(forces)))
    return (energies.reshape(own), forces)


def solution(mesh):
    sizes = tuple(mesh.shape[axis] for axis in ("gx", "gy", "gz"))
    split_all = ("parts", "gx", "gy", "gz")
    return jax.shard_map(
        functools.partial(shards, sizes),
        mesh=mesh,
        in_specs=(
            P(split_all),
            P(split_all, None, None),
            P(split_all, None, None),
            P(split_all, None, None),
            P(split_all, None),
            P(split_all, None),
            P(split_all, None),
            P(None, split_all),
            P(),
            P(),
            P(),
            P(),
            P(),
            P(),
            P(),
        ),
        out_specs=(P(split_all), P(None, split_all)),
        check_vma=False,
    )
```

```python
import functools
import math

import jax
import jax.numpy as jnp
from jax import lax
from jax.experimental import pallas as pl
from jax.experimental.pallas import tpu as pltpu
from jax.sharding import PartitionSpec as P

HIGH = lax.Precision.HIGHEST
CUTOFF = 5.0
INV_COUNT = 0.2
ROOT3 = math.sqrt(3.0)
ROOT5 = math.sqrt(5.0)
ROOT15 = math.sqrt(15.0)
SPANS = ((0, 1), (1, 3), (4, 5))
LANES = 128
BLOCK = 256
F32 = jnp.float32
BF16 = jnp.bfloat16
NT = (((1,), (1,)), ((), ()))
NN = (((1,), (0,)), ((), ()))


def round_up(value, unit):
    return -(-value // unit) * unit


def dot(left, right, dims=NN):
    return lax.dot_general(left, right, dims, preferred_element_type=F32)


def dot_high(left, right, dims=NN):
    return lax.dot_general(left, right, dims, preferred_element_type=F32, precision=HIGH)


def split(value):
    high = value.astype(BF16)
    return high, (value - high.astype(F32)).astype(BF16)


def split_f32(value):
    high = value.astype(BF16).astype(F32)
    return high, value - high


def stack_weights(value):
    high, low = split_f32(value)
    return jnp.concatenate([high, low, high], axis=0).T.astype(BF16)


def stack_acts(value):
    high, low = split(value)
    return jnp.concatenate([high, high, low], axis=0)


def stack_acts_f32(value):
    high, low = split_f32(value)
    return jnp.concatenate([high, high, low, jnp.zeros_like(low)], axis=0).astype(BF16)


def iota(shape, dim):
    return lax.broadcasted_iota(jnp.int32, shape, dim)


def sigmoid(value):
    return 0.5 * jnp.tanh(0.5 * value) + 0.5


def axis_steps(size):
    return (0, 1, -1) if size > 2 else tuple(range(size))


class Neighbourhood:
    def __init__(self, sizes):
        self.sizes = sizes
        self.steps = [axis_steps(size) for size in sizes]
        self.shifts = [
            (dx, dy, dz) for dz in self.steps[2] for dy in self.steps[1] for dx in self.steps[0]
        ]
        self.place = {
            tuple(s % n for s, n in zip(shift, sizes)): b for b, shift in enumerate(self.shifts)
        }
        self.count = len(self.shifts)

    def block(self, *shift):
        return self.place.get(tuple(s % n for s, n in zip(shift, self.sizes)))

    def moved(self, rows, axis, step):
        size = self.sizes[axis]
        pairs = [(i, (i + step) % size) for i in range(size)]
        return lax.ppermute(rows, ("gx", "gy", "gz")[axis], pairs)

    def fetch(self, rows):
        for axis in range(3):
            got = [rows] + [self.moved(rows, axis, -step) for step in self.steps[axis][1:]]
            if len(got) > 1:
                rows = jnp.concatenate(got, axis=0)
        return rows

    def give(self, rows):
        for axis in (2, 1, 0):
            steps = self.steps[axis]
            size = rows.shape[0] // len(steps)
            total = rows[:size]
            for index, step in enumerate(steps[1:], 1):
                total = total + self.moved(rows[index * size : (index + 1) * size], axis, step)
            rows = total
        return rows


class Sections:
    def __init__(self, own, faces):
        sizes = [own] + [face for face in faces for _ in range(2)]
        self.starts, self.spots, self.widths = [], [], []
        start = spot = 0
        for size in sizes:
            self.starts.append(start)
            self.spots.append(spot)
            self.widths.append(round_up(size, LANES))
            start += size
            spot += self.widths[-1]
        self.z_end, self.y_end, self.x_end = self.spots[3], self.spots[5], spot

    def align(self, entry):
        out = entry
        for k in range(1, len(self.starts)):
            gap = (self.spots[k] - self.starts[k]) - (self.spots[k - 1] - self.starts[k - 1])
            out = out + jnp.where(entry >= self.starts[k], gap, 0)
        return out


def pack_kernel(species_ref, sx_ref, sy_ref, sz_ref, first_ref, second_ref, live_ref, vec_ref, out):
    out[...] = jnp.zeros_like(out)
    out[0:3, :] = vec_ref[...]
    out[3:4, :] = first_ref[...].astype(F32)
    out[4:5, :] = jnp.where(live_ref[...] > 0, second_ref[...], -1).astype(F32)
    spot = 0
    own = species_ref.shape[1]
    out[5:6, 0:own] = species_ref[...].astype(F32)
    spot = round_up(own, LANES)
    for ref in (sz_ref, sy_ref, sx_ref):
        face = ref.shape[2]
        for side in range(2):
            out[5:6, spot : spot + face] = ref[0, 1 - side : 2 - side, :].astype(F32)
            spot += round_up(face, LANES)


ALONG_LANES = lax.GatherDimensionNumbers(
    offset_dims=(),
    collapsed_slice_dims=(1,),
    start_index_map=(1,),
    operand_batching_dims=(0,),
    start_indices_batching_dims=(0,),
)


def lookup(table, index):
    given = index.shape[0]
    rows = round_up(given, 8)
    if rows != given:
        index = jnp.broadcast_to(index[0:1], (rows, index.shape[1])) if given == 1 else jnp.concatenate(
            [index] + [index[0:1]] * (rows - given), axis=0
        )
        if table.shape[0] != 1:
            table = jnp.concatenate([table] + [table[0:1]] * (rows - given), axis=0)
    table = jnp.broadcast_to(table, (rows, table.shape[1]))
    parts = []
    for start in range(0, index.shape[1], LANES):
        at = index[:, start : start + LANES]
        low = jnp.bitwise_and(at, LANES - 1)
        tile = lax.shift_right_arithmetic(at, 7)
        out = None
        for k in range(table.shape[1] // LANES):
            found = lax.gather(
                table[:, k * LANES : (k + 1) * LANES],
                low[:, :, None],
                ALONG_LANES,
                slice_sizes=(1, 1),
                mode=lax.GatherScatterMode.PROMISE_IN_BOUNDS,
            )
            out = found if out is None else jnp.where(tile == k, found, out)
        parts.append(out)
    out = parts[0] if len(parts) == 1 else jnp.concatenate(parts, axis=1)
    return out[0:given]


def list_tables(hood, sections, own, got):
    def table(block, section):
        at = slice(sections.spots[section], sections.spots[section] + sections.widths[section])
        return got[8 * block + 5 : 8 * block + 6, at].astype(jnp.int32)

    lane = iota((1, sections.widths[0]), 1)
    z_lists = {}

    def z_list(dx, dy):
        block = hood.block(dx, dy, 0)
        if block not in z_lists:
            parts = [block * own + lane]
            for section, step in ((1, 1), (2, -1)):
                other = hood.block(dx, dy, step)
                parts.append(other * own + table(other, section))
            z_lists[block] = jnp.concatenate(parts, axis=1)
        return z_lists[block]

    y_lists = {}

    def y_list(dx):
        block = hood.block(dx, 0, 0)
        if block not in y_lists:
            parts = [z_list(dx, 0)]
            for section, step in ((3, 1), (4, -1)):
                entry = table(hood.block(dx, step, 0), section)
                parts.append(lookup(z_list(dx, step), sections.align(entry)))
            y_lists[block] = jnp.concatenate(parts, axis=1)
        return y_lists[block]

    parts = [y_list(0)]
    for section, step in ((5, 1), (6, -1)):
        entry = table(hood.block(step, 0, 0), section)
        parts.append(lookup(y_list(step), sections.align(entry)))
    mine = jnp.concatenate(parts, axis=1)

    def none(*which):
        return jnp.full((1, sum(sections.widths[k] for k in which)), -1, jnp.int32)

    z_back = {}
    for dz in hood.steps[2]:
        if dz == 0:
            z_back[dz] = jnp.concatenate([jnp.where(lane < own, lane, -1), none(1, 2)], axis=1)
        else:
            parts = [none(0)]
            for section, step in ((1, 1), (2, -1)):
                parts.append(table(0, section) if hood.block(0, 0, dz + step) == 0 else none(section))
            z_back[dz] = jnp.concatenate(parts, axis=1)
    y_back = {}
    for dz in hood.steps[2]:
        for dy in hood.steps[1]:
            if dy == 0:
                y_back[dy, dz] = jnp.concatenate([z_back[dz], none(3, 4)], axis=1)
                continue
            parts = [none(0, 1, 2)]
            for section, step in ((3, 1), (4, -1)):
                if (dy + step) % hood.sizes[1] == 0:
                    entry = table(hood.block(0, 0, dz), section)
                    parts.append(lookup(z_back[dz], sections.align(entry)))
                else:
                    parts.append(none(section))
            y_back[dy, dz] = jnp.concatenate(parts, axis=1)
    wanted = []
    for shift in hood.shifts:
        for section, step in ((5, 1), (6, -1)):
            if shift[0] != 0 and (shift[0] + step) % hood.sizes[0] == 0:
                wanted.append((shift, section))
    found = {}
    if wanted:
        entries = jnp.concatenate(
            [table(hood.block(0, dy, dz), section) for (_, dy, dz), section in wanted], axis=0
        )
        lists = jnp.concatenate([y_back[dy, dz] for (_, dy, dz), _ in wanted], axis=0)
        rows = lookup(lists, sections.align(entries))
        for number, key in enumerate(wanted):
            found[key] = rows[number : number + 1]
    back = []
    for shift in hood.shifts:
        if shift[0] == 0:
            back.append(jnp.concatenate([y_back[shift[1], shift[2]], none(5, 6)], axis=1))
        else:
            tail = [found.get((shift, section), none(section)) for section in (5, 6)]
            back.append(jnp.concatenate([none(0, 1, 2, 3, 4)] + tail, axis=1))
    return mine, back


def build_list(hood, sections, own, edges, got, list_out, fields):
    count = hood.count
    rows = round_up(count + 1, 8)
    pad = rows - count - 1
    mine, back = list_tables(hood, sections, own, got)

    def stacked(field):
        blocks = list(range(count)) + [0] * (1 + pad)
        return jnp.concatenate([got[8 * b + field : 8 * b + field + 1, :] for b in blocks], axis=0)

    second = stacked(4).astype(jnp.int32)
    first = stacked(3).astype(jnp.int32)
    tables = jnp.concatenate(back + [mine] + [mine] * pad, axis=0)
    found = lookup(tables, sections.align(jnp.maximum(second, 0)))
    row = iota((rows, edges), 0)
    chosen = (found >= 0) & (second >= 0) & (row < count)
    kinds = jnp.concatenate(
        [got[8 * b + 5 : 8 * b + 6, 0 : sections.widths[0]] for b in range(count)]
        + [jnp.zeros((rows - count, sections.widths[0]), F32)],
        axis=0,
    ).astype(jnp.int32)
    kind = lookup(kinds, first)

    code = found[count : count + 1]
    block = sum((code >= b * own).astype(jnp.int32) for b in range(1, count))
    atom = code - block * own
    others = lookup(kinds, jnp.broadcast_to(atom, (rows, edges)))
    other_kind = jnp.sum(jnp.where(row == block, others, 0).astype(F32), axis=0, keepdims=True)
    live = second[0:1] >= 0
    sub = iota((8, edges), 0)
    whole = jnp.concatenate(
        [
            got[0:4, :],
            atom.astype(F32),
            block.astype(F32),
            jnp.zeros((1, edges), F32),
            other_kind,
        ],
        axis=0,
    )
    dummy = jnp.where(sub == 0, 1.0, jnp.where((sub >= 3) & (sub <= 5), -1.0, 0.0))
    list_out[:, 0:edges] = jnp.where(live, whole, dummy)
    filled = jnp.sum(live.astype(F32)).astype(jnp.int32)
    capacity = list_out.shape[1]
    tile_dummy = dummy[:, :LANES]

    def fill(step, _):
        list_out[:, pl.ds(pl.multiple_of(step * LANES, LANES), LANES)] = tile_dummy
        return 0

    lax.fori_loop(edges // LANES, capacity // LANES, fill, 0)

    before = (iota((BLOCK, BLOCK), 0) < iota((BLOCK, BLOCK), 1)).astype(F32).astype(BF16)
    taken = chosen.astype(F32)
    seen = jnp.zeros((rows, 1), F32)
    ranks = []
    for start in range(0, edges, BLOCK):
        part = taken[:, start : start + BLOCK]
        ranks.append(dot(part.astype(BF16), before) + seen)
        seen = seen + jnp.sum(part, axis=1, keepdims=True)
    rank = jnp.concatenate(ranks, axis=1).astype(jnp.int32)
    left = jnp.where(chosen, iota((rows, edges), 1) - rank, 0)
    shift_own = (own - 1).bit_length()
    kind_bits = 8
    packed = lax.shift_left(lax.shift_left(found, shift_own) + first, kind_bits) + kind
    values = [stacked(k) for k in range(3)] + [packed]
    for bit in range((edges - 1).bit_length()):
        jump = 1 << bit
        moves = jnp.bitwise_and(lax.shift_right_logical(left, bit), 1)
        arrives = pltpu.roll(moves, edges - jump, 1) > 0
        values = [jnp.where(arrives, pltpu.roll(v, edges - jump, 1), v) for v in values]
        stays = jnp.where(moves > 0, 0, left)
        left = jnp.where(arrives, pltpu.roll(left, edges - jump, 1), stays)
    packed = values[3]
    fields[0] = -values[0]
    fields[1] = -values[1]
    fields[2] = -values[2]
    fields[3] = lax.shift_right_logical(packed, shift_own + kind_bits).astype(F32)
    fields[4] = jnp.bitwise_and(
        lax.shift_right_logical(packed, kind_bits), (1 << shift_own) - 1
    ).astype(F32)
    fields[5] = jnp.bitwise_and(packed, (1 << kind_bits) - 1).astype(F32)

    lane = iota((1, LANES), 1)
    sub = iota((8, LANES), 0)
    row1 = iota((rows, 1), 0)
    last = edges // LANES - 1
    for b in range(count):
        size = jnp.sum(jnp.where(row1 == b, seen, 0.0)).astype(jnp.int32)
        to = filled

        def piece(tile, back, b=b):
            at = pl.ds(pl.multiple_of(jnp.clip(tile, 0, last) * LANES, LANES), LANES)
            rows8 = jnp.concatenate(
                [fields[k, b : b + 1, at] for k in range(5)]
                + [jnp.full((1, LANES), float(b), F32), jnp.zeros((1, LANES), F32)]
                + [fields[5, b : b + 1, at]],
                axis=0,
            )
            return pltpu.roll(rows8, back, 1)

        def place(step, _, size=size, to=to, piece=piece):
            window = step * LANES - to
            low = lax.shift_right_arithmetic(window, 7)
            turn = jnp.bitwise_and(window, LANES - 1)
            back = jnp.bitwise_and(LANES - turn, LANES - 1)
            moved = jnp.where(lane < LANES - turn, piece(low, back), piece(low + 1, back))
            spot = lane + step * LANES
            here = pl.ds(pl.multiple_of(step * LANES, LANES), LANES)
            list_out[:, here] = jnp.where(
                (spot >= to) & (spot < to + size), moved, list_out[:, here]
            )
            return 0

        lax.fori_loop(
            lax.shift_right_arithmetic(to, 7),
            lax.shift_right_arithmetic(to + size + LANES - 1, 7),
            place,
            0,
        )
        filled = to + size
    return filled


def prepare_kernel(in_ref, mid_ref, out_ref, *outs):
    for layer in range(in_ref.shape[0]):
        into = in_ref[layer]
        middle = mid_ref[layer]
        last = out_ref[layer]
        in_fw, mid_fw, out_fw, in_bw, mid_bw, out_bw = (out.at[layer] for out in outs)
        high, low = split_f32(into)
        in_fw[...] = (
            jnp.concatenate([high, low, high, jnp.zeros_like(high)], axis=0).T.astype(BF16)
        )
        mid_fw[...] = stack_weights(middle)
        out_fw[...] = stack_weights(last)
        into_t = jnp.concatenate([into, jnp.zeros_like(into)], axis=0).T
        in_bw[...] = stack_weights(into_t)
        mid_bw[...] = stack_weights(middle.T)
        high, low = split(last)
        out_bw[...] = jnp.concatenate([high, low, high], axis=1)


def geometry(chunk, need_slopes):
    vec = [chunk[k : k + 1] for k in range(3)]
    dist = jnp.sqrt(vec[0] * vec[0] + vec[1] * vec[1] + vec[2] * vec[2])
    inv = 1.0 / dist
    ux, uy, uz = (v * inv for v in vec)
    values = [
        jnp.ones_like(dist),
        ROOT3 * ux,
        ROOT3 * uy,
        ROOT3 * uz,
        ROOT15 * ux * uy,
        ROOT15 * uy * uz,
        0.5 * ROOT5 * (3.0 * uz * uz - 1.0),
        ROOT15 * ux * uz,
        0.5 * ROOT15 * (ux * ux - uy * uy),
    ]
    orders = (iota((8, dist.shape[1]), 0) + 1).astype(F32) * (math.pi / CUTOFF)
    angle = orders * dist
    scale = math.sqrt(2.0 / CUTOFF) * inv
    basis = jnp.sin(angle) * scale
    x = dist * (1.0 / CUTOFF)
    x2 = x * x
    x4 = x2 * x2
    envelope = 1.0 + x4 * x * (-21.0 + x * (35.0 - 15.0 * x))
    slopes = None
    if need_slopes:
        d_basis = orders * jnp.cos(angle) * scale - basis * inv
        d_envelope = x4 * (-105.0 + x * (210.0 - 105.0 * x)) * (1.0 / CUTOFF)
        slopes = (d_basis, d_envelope)
    return inv, (ux, uy, uz), values, basis, envelope, slopes


def radial_hidden(basis, in_fw, mid_fw):
    z1 = dot(in_fw, stack_acts_f32(basis))
    gate1 = sigmoid(z1)
    z2 = dot(mid_fw, stack_acts(z1 * gate1))
    return z1, gate1, z2, sigmoid(z2)


def scaled_hots(chunk, own, values):
    target = chunk[3:4].astype(jnp.int32)
    mask = iota((own, target.shape[1]), 0) == target
    hot = mask.astype(F32).astype(BF16)
    highs, lows = [], []
    for begin, size in SPANS:
        pairs = [split(values[m]) for m in range(begin, begin + size)]
        highs.append(jnp.concatenate([hot * high for high, _ in pairs], axis=0))
        lows.append(jnp.concatenate([hot * low for _, low in pairs], axis=0))
    return mask, highs, lows


def other_hot(chunk, own, total):
    atom = chunk[4:5].astype(jnp.int32)
    hot = (iota((own, atom.shape[1]), 0) == atom).astype(F32).astype(BF16)
    block = chunk[5:6]
    return jnp.concatenate(
        [hot * (block == float(b)).astype(F32).astype(BF16) for b in range(total // own)], axis=0
    )


def read_chunk(edges_ref, step):
    return edges_ref[:, pl.ds(pl.multiple_of(step * BLOCK, BLOCK), BLOCK)]


def kind_features(chunk, columns):
    kind = chunk[7:8]
    out = jnp.where(kind == 0.0, columns[0], 0.0)
    for index in range(1, len(columns)):
        out = out + jnp.where(kind == float(index), columns[index], 0.0)
    return out


def collect(amat, chunk, feat, values, envelope, hidden, out_fw, own):
    z2, gate2 = hidden
    width = feat.shape[0]
    units = z2 * gate2 * (INV_COUNT * envelope)
    weights = dot(out_fw, stack_acts(units))
    _, highs, lows = scaled_hots(chunk, own, values)
    for degree, (begin, size) in enumerate(SPANS):
        high, low = split(weights[degree * width : (degree + 1) * width] * feat)
        left = jnp.concatenate([highs[degree], lows[degree], highs[degree]], axis=1)
        right = jnp.concatenate([high, high, low], axis=1)
        at = slice(begin * own, (begin + size) * own)
        amat[at, :] += dot(left, right, NT)


def node_forward(amat, features, update, own):
    parts = [amat[m * own : (m + 1) * own, :] for m in range(9)]
    inv1 = sum(p * p for p in parts[1:4])
    inv2 = sum(p * p for p in parts[4:9])
    preact = dot_high(jnp.concatenate([parts[0], inv1, inv2], axis=1), update)
    return features + preact * sigmoid(preact), preact


def node_back(amat, d_features, preact, update, own, d_amat, turned):
    width = d_features.shape[1]
    gate = sigmoid(preact)
    d_pre = d_features * gate * (1.0 + preact * (1.0 - gate))
    d_inv = dot_high(d_pre, update, NT)
    for degree, (begin, size) in enumerate(SPANS):
        rows = []
        for m in range(begin, begin + size):
            value = d_inv[:, degree * width : (degree + 1) * width]
            if degree > 0:
                value = 2.0 * amat[m * own : (m + 1) * own, :] * value
            rows.append(value)
        rows = jnp.concatenate(rows, axis=0)
        high, low = split(rows)
        d_amat[begin * own : (begin + size) * own, :] = jnp.concatenate([high, low, high], axis=1)
        turned[degree][...] = stack_weights(rows)


def edge_backward(chunk, feat, own, in_fw, mid_fw, out_fw, in_bw, mid_bw, out_bw, d_amat, turned):
    width = feat.shape[0]
    inv, unit, values, basis, envelope, (d_basis, d_envelope) = geometry(chunk, True)
    z1, gate1, z2, gate2 = radial_hidden(basis, in_fw, mid_fw)
    scale = INV_COUNT * envelope
    units = z2 * gate2
    weights = dot(out_fw, stack_acts(units * scale))
    mask, highs, lows = scaled_hots(chunk, own, values)
    pulled = []
    d_mixed = 0.0
    d_values = []
    for degree, (begin, size) in enumerate(SPANS):
        weight = weights[degree * width : (degree + 1) * width]
        right = jnp.concatenate([highs[degree], highs[degree], lows[degree]], axis=0)
        term = dot(turned[degree][...], right)
        d_mixed = d_mixed + weight * term
        pulled.append(feat * term)
        high, low = split(weight * feat)
        spread = dot(
            d_amat[begin * own : (begin + size) * own, :],
            jnp.concatenate([high, high, low], axis=0),
        )
        for m in range(size):
            d_values.append(
                jnp.sum(jnp.where(mask, spread[m * own : (m + 1) * own], 0.0), axis=0, keepdims=True)
            )
    pulled = jnp.concatenate(pulled, axis=0)
    d_units = dot(out_bw, stack_acts(pulled))
    d_env = INV_COUNT * jnp.sum(units * d_units, axis=0, keepdims=True)
    d_z2 = d_units * scale * gate2 * (1.0 + z2 * (1.0 - gate2))
    d_hidden = dot(mid_bw, stack_acts(d_z2))
    d_z1 = d_hidden * gate1 * (1.0 + z1 * (1.0 - gate1))
    d_b = dot(in_bw, stack_acts(d_z1))[0:8]
    d_dist = jnp.sum(d_b * d_basis, axis=0, keepdims=True) + d_env * d_envelope
    ux, uy, uz = unit
    y = d_values
    dux = ROOT3 * y[1] + ROOT15 * (uy * y[4] + uz * y[7] + ux * y[8])
    duy = ROOT3 * y[2] + ROOT15 * (ux * y[4] + uz * y[5] - uy * y[8])
    duz = ROOT3 * y[3] + ROOT15 * (uy * y[5] + ux * y[7]) + 3.0 * ROOT5 * uz * y[6]
    along = ux * dux + uy * duy + uz * duz
    grad = [(du - u * along) * inv + d_dist * u for u, du in zip(unit, (dux, duy, duz))]
    return grad, d_mixed


def first_kernel(hood, sections, own, edges, *refs):
    (
        got,
        species_ref,
        embed_ref,
        mix_ref,
        update_ref,
        in_fw,
        mid_fw,
        out_fw,
        list_out,
        total_out,
        amat_out,
        preact_out,
        h_out,
        w_out,
        fields,
    ) = refs
    filled = build_list(hood, sections, own, edges, got, list_out, fields)
    steps = lax.shift_right_arithmetic(filled + BLOCK - 1, 8)
    total_out[0] = steps

    embed = embed_ref[...]
    mixed = dot_high(embed, mix_ref[0])
    columns = [mixed[k : k + 1].T for k in range(embed.shape[0])]
    amat_out[...] = jnp.zeros_like(amat_out)

    def body(step, _):
        chunk = read_chunk(list_out, step)
        _, _, values, basis, envelope, _ = geometry(chunk, False)
        _, _, z2, gate2 = radial_hidden(basis, in_fw[0], mid_fw[0])
        feat = kind_features(chunk, columns)
        collect(amat_out, chunk, feat, values, envelope, (z2, gate2), out_fw[0], own)
        return 0

    lax.fori_loop(0, steps, body, 0)
    kind = species_ref[...]
    features = jnp.where(kind == 0, embed[0:1], 0.0)
    for k in range(1, embed.shape[0]):
        features = features + jnp.where(kind == k, embed[k : k + 1], 0.0)
    h, preact = node_forward(amat_out, features, update_ref[0], own)
    preact_out[...] = preact
    h_out[...] = h
    w_out[...] = dot_high(h, mix_ref[1])


def second_kernel(count, own, *refs):
    (
        everyone_ref,
        steps_ref,
        list_ref,
        h_ref,
        update_ref,
        readout_ref,
        in_fw,
        mid_fw,
        out_fw,
        in_bw,
        mid_bw,
        out_bw,
        energy_out,
        grad_out,
        d_mixed_sum,
        features_t,
        amat,
        d_amat,
        turn0,
        turn1,
        turn2,
    ) = refs
    turned = (turn0, turn1, turn2)
    total = count * own
    width = h_ref.shape[1]
    steps = steps_ref[0]
    high, low = split_f32(everyone_ref[...].T)
    features_t[...] = jnp.concatenate([high, low], axis=0).astype(BF16)
    amat[...] = jnp.zeros_like(amat)
    d_mixed_sum[...] = jnp.zeros_like(d_mixed_sum)

    def gather(hot):
        both = dot(features_t[...], hot)
        return both[:width] + both[width:]

    def forward(step, _):
        chunk = read_chunk(list_ref, step)
        _, _, values, basis, envelope, _ = geometry(chunk, False)
        _, _, z2, gate2 = radial_hidden(basis, in_fw[1], mid_fw[1])
        feat = gather(other_hot(chunk, own, total))
        collect(amat, chunk, feat, values, envelope, (z2, gate2), out_fw[1], own)
        return 0

    lax.fori_loop(0, steps, forward, 0)
    h1 = h_ref[...]
    h2, preact = node_forward(amat, h1, update_ref[1], own)
    readout = readout_ref[...]
    energy_out[...] = dot_high(readout[0:1], h1, NT) + dot_high(readout[1:2], h2, NT)
    d_features = jnp.broadcast_to(readout[1:2], h1.shape)
    node_back(amat, d_features, preact, update_ref[1], own, d_amat, turned)

    def backward(step, _):
        chunk = read_chunk(list_ref, step)
        hot = other_hot(chunk, own, total)
        grad, d_mixed = edge_backward(
            chunk,
            gather(hot),
            own,
            in_fw[1],
            mid_fw[1],
            out_fw[1],
            in_bw[1],
            mid_bw[1],
            out_bw[1],
            d_amat,
            turned,
        )
        at = pl.ds(pl.multiple_of(step * BLOCK, BLOCK), BLOCK)
        grad_out[:, at] = jnp.concatenate(grad + [jnp.zeros((5, BLOCK), F32)], axis=0)
        high, low = split(d_mixed)
        both = dot(hot, jnp.concatenate([high, low], axis=0), NT)
        d_mixed_sum[...] += both[:, :width] + both[:, width:]
        return 0

    lax.fori_loop(0, steps, backward, 0)


def last_kernel(count, own, *refs):
    (
        d_mixed_ref,
        steps_ref,
        list_ref,
        grad_ref,
        amat_ref,
        preact_ref,
        embed_ref,
        mix_ref,
        update_ref,
        readout_ref,
        in_fw,
        mid_fw,
        out_fw,
        in_bw,
        mid_bw,
        out_bw,
        force_out,
        d_amat,
        turn0,
        turn1,
        turn2,
        force,
    ) = refs
    turned = (turn0, turn1, turn2)
    total = count * own
    steps = steps_ref[0]
    embed = embed_ref[...]
    mixed = dot_high(embed, mix_ref[0])
    columns = [mixed[k : k + 1].T for k in range(embed.shape[0])]
    readout = readout_ref[...]
    d_features = readout[0:1] + readout[1:2] + dot_high(d_mixed_ref[...], mix_ref[1], NT)
    node_back(amat_ref, d_features, preact_ref[...], update_ref[0], own, d_amat, turned)
    force[...] = jnp.zeros_like(force)

    def backward(step, _):
        chunk = read_chunk(list_ref, step)
        grad, _ = edge_backward(
            chunk,
            kind_features(chunk, columns),
            own,
            in_fw[0],
            mid_fw[0],
            out_fw[0],
            in_bw[0],
            mid_bw[0],
            out_bw[0],
            d_amat,
            turned,
        )
        at = pl.ds(pl.multiple_of(step * BLOCK, BLOCK), BLOCK)
        pull = jnp.concatenate(grad + [jnp.zeros((5, BLOCK), F32)], axis=0) + grad_ref[:, at]
        high, rest = split_f32(pull)
        middle, low = split_f32(rest)
        parts = jnp.concatenate([high, middle, low, jnp.zeros_like(low)], axis=0).astype(BF16)
        target = chunk[3:4].astype(jnp.int32)
        mine = (iota((own, BLOCK), 0) == target).astype(F32).astype(BF16)
        moved = dot(parts, other_hot(chunk, own, total), NT)
        force[...] -= moved[0:8] + moved[8:16] + moved[16:24]
        moved = dot(parts, mine, NT)
        force[:, 0:own] += moved[0:8] + moved[8:16] + moved[16:24]
        return 0

    lax.fori_loop(0, steps, backward, 0)
    for b in range(count):
        force_out[8 * b : 8 * b + 8, :] = force[:, b * own : (b + 1) * own]


def call(kernel, outs, scratch, args, smem_in=(), smem_out=()):
    vmem = pl.BlockSpec(memory_space=pltpu.VMEM)
    smem = pl.BlockSpec(memory_space=pltpu.SMEM)
    return pl.pallas_call(
        kernel,
        out_shape=outs,
        in_specs=[smem if k in smem_in else vmem for k in range(len(args))],
        out_specs=[smem if k in smem_out else vmem for k in range(len(outs))],
        scratch_shapes=scratch,
        compiler_params=pltpu.CompilerParams(vmem_limit_bytes=40 * 1024 * 1024),
    )(*args)


def shards(
    sizes,
    species,
    send_x,
    send_y,
    send_z,
    edge_first,
    edge_second,
    edge_live,
    edge_vec,
    embed,
    radial_in,
    radial_mid,
    radial_out,
    mix,
    update,
    readout,
):
    hood = Neighbourhood(sizes)
    count = hood.count
    own = species.shape[0]
    width = embed.shape[1]
    layers = readout.shape[0]
    hidden = radial_mid.shape[1]
    slots = edge_first.shape[1]
    edges = round_up(slots, BLOCK)
    extra = edges - slots
    if extra:
        edge_first = jnp.pad(edge_first, ((0, 0), (0, extra)))
        edge_second = jnp.pad(edge_second, ((0, 0), (0, extra)))
        edge_live = jnp.pad(edge_live, ((0, 0), (0, extra)))
        edge_vec = jnp.pad(edge_vec, ((0, 0), (0, extra)), constant_values=1.0)
    faces = tuple(send.shape[2] for send in (send_z, send_y, send_x))
    sections = Sections(own, faces)
    shape = jax.ShapeDtypeStruct
    weights = call(
        prepare_kernel,
        [
            shape((layers, hidden, 32), BF16),
            shape((layers, hidden, 3 * hidden), BF16),
            shape((layers, 3 * width, 3 * hidden), BF16),
            shape((layers, 16, 3 * hidden), BF16),
            shape((layers, hidden, 3 * hidden), BF16),
            shape((layers, hidden, 9 * width), BF16),
        ],
        [],
        [radial_in, radial_mid, radial_out],
    )
    packed = call(
        pack_kernel,
        [shape((8, edges), F32)],
        [],
        [species[None, :], send_x, send_y, send_z, edge_first, edge_second, edge_live, edge_vec],
    )[0]
    got = hood.fetch(packed)
    capacity = (count + 1) * edges
    edge_list, steps, amat1, preact1, h1, w2 = call(
        functools.partial(first_kernel, hood, sections, own, edges),
        [
            shape((8, capacity), F32),
            shape((1,), jnp.int32),
            shape((9 * own, width), F32),
            shape((own, width), F32),
            shape((own, width), F32),
            shape((own, width), F32),
        ],
        [pltpu.VMEM((6, round_up(count + 1, 8), edges), F32)],
        [got, species[:, None], embed, mix, update] + list(weights[:3]),
        smem_out=(1,),
    )
    turned = [pltpu.VMEM((width, 3 * size * own), BF16) for _, size in SPANS]
    energies, grads, d_mixed = call(
        functools.partial(second_kernel, count, own),
        [
            shape((1, own), F32),
            shape((8, capacity), F32),
            shape((count * own, width), F32),
        ],
        [
            pltpu.VMEM((2 * width, count * own), BF16),
            pltpu.VMEM((9 * own, width), F32),
            pltpu.VMEM((9 * own, 3 * width), BF16),
        ]
        + turned,
        [hood.fetch(w2), steps, edge_list, h1, update, readout] + list(weights),
        smem_in=(1,),
    )
    forces = call(
        functools.partial(last_kernel, count, own),
        [shape((8 * count, own), F32)],
        [pltpu.VMEM((9 * own, 3 * width), BF16)] + turned + [pltpu.VMEM((8, count * own), F32)],
        [hood.give(d_mixed), steps, edge_list, grads, amat1, preact1, embed, mix, update, readout]
        + list(weights),
        smem_in=(1,),
    )[0]
    return (energies.reshape(own), hood.give(forces)[:3])


def solution(mesh):
    sizes = tuple(mesh.shape[axis] for axis in ("gx", "gy", "gz"))
    split_all = ("parts", "gx", "gy", "gz")
    return jax.shard_map(
        functools.partial(shards, sizes),
        mesh=mesh,
        in_specs=(
            P(split_all),
            P(split_all, None, None),
            P(split_all, None, None),
            P(split_all, None, None),
            P(split_all, None),
            P(split_all, None),
            P(split_all, None),
            P(None, split_all),
            P(),
            P(),
            P(),
            P(),
            P(),
            P(),
            P(),
        ),
        out_specs=(P(split_all), P(None, split_all)),
        check_vma=False,
    )
```

```python
import functools
import math

import jax
import jax.numpy as jnp
from jax import lax
from jax.experimental import pallas as pl
from jax.experimental.pallas import tpu as pltpu
from jax.sharding import PartitionSpec as P

HIGH = lax.Precision.HIGHEST
CUTOFF = 5.0
INV_COUNT = 0.2
ROOT3 = math.sqrt(3.0)
ROOT5 = math.sqrt(5.0)
ROOT15 = math.sqrt(15.0)
SPANS = ((0, 1), (1, 3), (4, 5))
LANES = 128
BLOCK = 256
STEPS = (1024, 512)
F32 = jnp.float32
BF16 = jnp.bfloat16
NT = (((1,), (1,)), ((), ()))
NN = (((1,), (0,)), ((), ()))


def round_up(value, unit):
    return -(-value // unit) * unit


def dot(left, right, dims=NN):
    return lax.dot_general(left, right, dims, preferred_element_type=F32)


def dot_high(left, right, dims=NN):
    return lax.dot_general(left, right, dims, preferred_element_type=F32, precision=HIGH)


def split(value):
    high = value.astype(BF16)
    return high, (value - high.astype(F32)).astype(BF16)


def split_f32(value):
    high = value.astype(BF16).astype(F32)
    return high, value - high


def stack_weights(value):
    high, low = split_f32(value)
    return jnp.concatenate([high, low, high], axis=0).T.astype(BF16)


def stack_acts(value):
    high, low = split(value)
    return jnp.concatenate([high, high, low], axis=0)


def stack_acts_f32(value):
    high, low = split_f32(value)
    return jnp.concatenate([high, high, low, jnp.zeros_like(low)], axis=0).astype(BF16)


def iota(shape, dim):
    return lax.broadcasted_iota(jnp.int32, shape, dim)


def sigmoid(value):
    return 0.5 * jnp.tanh(0.5 * value) + 0.5


def axis_steps(size):
    return (0, 1, -1) if size > 2 else tuple(range(size))


class Neighbourhood:
    def __init__(self, sizes):
        self.sizes = sizes
        self.steps = [axis_steps(size) for size in sizes]
        self.shifts = [
            (dx, dy, dz) for dz in self.steps[2] for dy in self.steps[1] for dx in self.steps[0]
        ]
        self.place = {
            tuple(s % n for s, n in zip(shift, sizes)): b for b, shift in enumerate(self.shifts)
        }
        self.count = len(self.shifts)

    def block(self, *shift):
        return self.place.get(tuple(s % n for s, n in zip(shift, self.sizes)))

    def moved(self, rows, axis, step):
        size = self.sizes[axis]
        pairs = [(i, (i + step) % size) for i in range(size)]
        return lax.ppermute(rows, ("gx", "gy", "gz")[axis], pairs)

    def fetch(self, rows):
        along_x = None
        for axis in range(3):
            got = [rows] + [self.moved(rows, axis, -step) for step in self.steps[axis][1:]]
            if len(got) > 1:
                rows = jnp.concatenate(got, axis=0)
            if axis == 0:
                along_x = rows
        return rows, along_x

    def give(self, rows):
        for axis in (2, 1, 0):
            steps = self.steps[axis]
            size = rows.shape[0] // len(steps)
            total = rows[:size]
            for index, step in enumerate(steps[1:], 1):
                total = total + self.moved(rows[index * size : (index + 1) * size], axis, step)
            rows = total
        return rows


class Sections:
    def __init__(self, own, faces):
        sizes = [own] + [face for face in faces for _ in range(2)]
        self.starts, self.spots, self.widths = [], [], []
        start = spot = 0
        for size in sizes:
            self.starts.append(start)
            self.spots.append(spot)
            self.widths.append(round_up(size, LANES))
            start += size
            spot += self.widths[-1]
        self.z_end, self.y_end, self.x_end = self.spots[3], self.spots[5], spot

    def align(self, entry):
        out = entry
        for k in range(1, len(self.starts)):
            gap = (self.spots[k] - self.starts[k]) - (self.spots[k - 1] - self.starts[k - 1])
            out = out + jnp.where(entry >= self.starts[k], gap, 0)
        return out


def pack_kernel(*refs):
    given, out, held, sems = refs[:8], refs[8], refs[9:17], refs[17]
    copies = [
        pltpu.make_async_copy(source, target, sems.at[k])
        for k, (source, target) in enumerate(zip(given, held))
    ]
    for copy in copies:
        copy.start()
    out[...] = jnp.zeros_like(out)
    for copy in copies:
        copy.wait()
    species_ref, sx_ref, sy_ref, sz_ref, first_ref, second_ref, live_ref, vec_ref = held
    out[0:3, :] = vec_ref[...]
    out[3:4, :] = first_ref[...].astype(F32)
    out[4:5, :] = jnp.where(live_ref[...] > 0, second_ref[...], -1).astype(F32)
    own = species_ref.shape[1]
    out[5:6, 0:own] = species_ref[...].astype(F32)
    spot = round_up(own, LANES)
    for ref in (sz_ref, sy_ref, sx_ref):
        face = ref.shape[2]
        for side in range(2):
            out[5:6, spot : spot + face] = ref[0, 1 - side : 2 - side, :].astype(F32)
            spot += round_up(face, LANES)


ALONG_LANES = lax.GatherDimensionNumbers(
    offset_dims=(),
    collapsed_slice_dims=(1,),
    start_index_map=(1,),
    operand_batching_dims=(0,),
    start_indices_batching_dims=(0,),
)


def lookup(table, index):
    given = index.shape[0]
    rows = round_up(given, 8)
    if rows != given:
        index = jnp.broadcast_to(index[0:1], (rows, index.shape[1])) if given == 1 else jnp.concatenate(
            [index] + [index[0:1]] * (rows - given), axis=0
        )
        if table.shape[0] != 1:
            table = jnp.concatenate([table] + [table[0:1]] * (rows - given), axis=0)
    table = jnp.broadcast_to(table, (rows, table.shape[1]))
    parts = []
    for start in range(0, index.shape[1], LANES):
        at = index[:, start : start + LANES]
        low = jnp.bitwise_and(at, LANES - 1)
        tile = lax.shift_right_arithmetic(at, 7)
        out = None
        for k in range(table.shape[1] // LANES):
            found = lax.gather(
                table[:, k * LANES : (k + 1) * LANES],
                low[:, :, None],
                ALONG_LANES,
                slice_sizes=(1, 1),
                mode=lax.GatherScatterMode.PROMISE_IN_BOUNDS,
            )
            out = found if out is None else jnp.where(tile == k, found, out)
        parts.append(out)
    out = parts[0] if len(parts) == 1 else jnp.concatenate(parts, axis=1)
    return out[0:given]


def list_tables(hood, sections, own, got):
    def table(block, section):
        at = slice(sections.spots[section], sections.spots[section] + sections.widths[section])
        return got[8 * block + 5 : 8 * block + 6, at].astype(jnp.int32)

    lane = iota((1, sections.widths[0]), 1)
    z_lists = {}

    def z_list(dx, dy):
        block = hood.block(dx, dy, 0)
        if block not in z_lists:
            parts = [block * own + lane]
            for section, step in ((1, 1), (2, -1)):
                other = hood.block(dx, dy, step)
                parts.append(other * own + table(other, section))
            z_lists[block] = jnp.concatenate(parts, axis=1)
        return z_lists[block]

    y_lists = {}

    def y_list(dx):
        block = hood.block(dx, 0, 0)
        if block not in y_lists:
            parts = [z_list(dx, 0)]
            for section, step in ((3, 1), (4, -1)):
                entry = table(hood.block(dx, step, 0), section)
                parts.append(lookup(z_list(dx, step), sections.align(entry)))
            y_lists[block] = jnp.concatenate(parts, axis=1)
        return y_lists[block]

    parts = [y_list(0)]
    for section, step in ((5, 1), (6, -1)):
        entry = table(hood.block(step, 0, 0), section)
        parts.append(lookup(y_list(step), sections.align(entry)))
    mine = jnp.concatenate(parts, axis=1)

    def none(*which):
        return jnp.full((1, sum(sections.widths[k] for k in which)), -1, jnp.int32)

    z_back = {}
    for dz in hood.steps[2]:
        if dz == 0:
            z_back[dz] = jnp.concatenate([jnp.where(lane < own, lane, -1), none(1, 2)], axis=1)
        else:
            parts = [none(0)]
            for section, step in ((1, 1), (2, -1)):
                parts.append(table(0, section) if hood.block(0, 0, dz + step) == 0 else none(section))
            z_back[dz] = jnp.concatenate(parts, axis=1)
    y_back = {}
    for dz in hood.steps[2]:
        for dy in hood.steps[1]:
            if dy == 0:
                y_back[dy, dz] = jnp.concatenate([z_back[dz], none(3, 4)], axis=1)
                continue
            parts = [none(0, 1, 2)]
            for section, step in ((3, 1), (4, -1)):
                if (dy + step) % hood.sizes[1] == 0:
                    entry = table(hood.block(0, 0, dz), section)
                    parts.append(lookup(z_back[dz], sections.align(entry)))
                else:
                    parts.append(none(section))
            y_back[dy, dz] = jnp.concatenate(parts, axis=1)
    wanted = []
    for shift in hood.shifts:
        for section, step in ((5, 1), (6, -1)):
            if shift[0] != 0 and (shift[0] + step) % hood.sizes[0] == 0:
                wanted.append((shift, section))
    found = {}
    if wanted:
        entries = jnp.concatenate(
            [table(hood.block(0, dy, dz), section) for (_, dy, dz), section in wanted], axis=0
        )
        lists = jnp.concatenate([y_back[dy, dz] for (_, dy, dz), _ in wanted], axis=0)
        rows = lookup(lists, sections.align(entries))
        for number, key in enumerate(wanted):
            found[key] = rows[number : number + 1]
    back = []
    for shift in hood.shifts:
        if shift[0] == 0:
            back.append(jnp.concatenate([y_back[shift[1], shift[2]], none(5, 6)], axis=1))
        else:
            tail = [found.get((shift, section), none(section)) for section in (5, 6)]
            back.append(jnp.concatenate([none(0, 1, 2, 3, 4)] + tail, axis=1))
    return mine, back


def empty_edges(size):
    sub = iota((8, size), 0)
    return jnp.where(sub == 0, 1.0, jnp.where((sub >= 3) & (sub <= 5), -1.0, 0.0))


def fill_empty(list_out, start):
    tile = empty_edges(LANES)

    def fill(step, _):
        list_out[:, pl.ds(pl.multiple_of(step * LANES, LANES), LANES)] = tile
        return 0

    lax.fori_loop(start // LANES, list_out.shape[1] // LANES, fill, 0)


def put(list_out, piece, to, size):
    lane = iota((1, LANES), 1)
    turn = jnp.bitwise_and(to, LANES - 1)
    piece = pltpu.roll(piece, turn, 1)
    low = lax.shift_right_arithmetic(to, 7)
    stop = turn + size
    for part in range(2):
        here = pl.ds(pl.multiple_of((low + part) * LANES, LANES), LANES)
        if part == 0:
            inside = (lane >= turn) & (lane < stop)
        else:
            inside = (lane < turn) & (lane < stop - LANES)
        list_out[:, here] = jnp.where(inside, piece, list_out[:, here])


def count_true(mask):
    return jnp.sum(mask.astype(F32)).astype(jnp.int32)


def build_inner(own, edges, record, list_out):
    second = record[4:5, :].astype(jnp.int32)
    inner = (second >= 0) & (second < own)
    number = count_true(inner)
    kinds = record[5:6, 0 : round_up(own, LANES)].astype(jnp.int32)
    kind_second = lookup(kinds, jnp.where(inner, second, 0)).astype(F32)
    kind_first = lookup(kinds, record[3:4, :].astype(jnp.int32)).astype(F32)
    zero = jnp.zeros((1, edges), F32)
    vec, first, other = record[0:3, :], record[3:4, :], record[4:5, :]
    forward = jnp.concatenate([vec, first, other, zero, zero, kind_second], axis=0)
    list_out[:, 0:edges] = jnp.where(inner, forward, empty_edges(edges))
    fill_empty(list_out, edges)
    reverse = jnp.concatenate([-vec, other, first, zero, zero, kind_first], axis=0)
    for start in range(0, edges, LANES):
        put(list_out, reverse[:, start : start + LANES], number + start, number - start)
    return 2 * number


def build_outer(hood, sections, own, edges, got, list_out, fields):
    count = hood.count
    rows = round_up(count, 8)
    pad = rows - count
    mine, back = list_tables(hood, sections, own, got)

    def stacked(field):
        blocks = list(range(count)) + [0] * pad
        return jnp.concatenate([got[8 * b + field : 8 * b + field + 1, :] for b in blocks], axis=0)

    second = stacked(4).astype(jnp.int32)
    first = stacked(3).astype(jnp.int32)
    tables = jnp.concatenate([mine] + back[1:] + [mine] * pad, axis=0)
    found = lookup(tables, sections.align(jnp.maximum(second, 0)))
    row = iota((rows, edges), 0)
    chosen = (found >= 0) & (second >= 0) & (row < count) & (row > 0)
    kinds = jnp.concatenate(
        [got[8 * b + 5 : 8 * b + 6, 0 : sections.widths[0]] for b in range(count)]
        + [jnp.zeros((pad, sections.widths[0]), F32)] * (pad > 0),
        axis=0,
    ).astype(jnp.int32)
    kind = lookup(kinds, first)

    code = found[0:1]
    block = sum((code >= b * own).astype(jnp.int32) for b in range(1, count))
    atom = code - block * own
    others = lookup(kinds, jnp.broadcast_to(atom, (rows, edges)))
    other_kind = jnp.sum(jnp.where(row == block, others, 0).astype(F32), axis=0, keepdims=True)
    whole = jnp.concatenate(
        [
            got[0:4, :],
            atom.astype(F32),
            block.astype(F32),
            jnp.zeros((1, edges), F32),
            other_kind,
        ],
        axis=0,
    )
    list_out[:, 0:edges] = jnp.where(second[0:1] >= own, whole, empty_edges(edges))
    fill_empty(list_out, edges)
    filled = count_true(second[0:1] >= 0)
    start = filled - count_true(second[0:1] >= own)

    before = (iota((BLOCK, BLOCK), 0) < iota((BLOCK, BLOCK), 1)).astype(F32).astype(BF16)
    taken = chosen.astype(F32)
    seen = jnp.zeros((rows, 1), F32)
    ranks = []
    for begin in range(0, edges, BLOCK):
        part = taken[:, begin : begin + BLOCK]
        ranks.append(dot(part.astype(BF16), before) + seen)
        seen = seen + jnp.sum(part, axis=1, keepdims=True)
    rank = jnp.concatenate(ranks, axis=1).astype(jnp.int32)
    left = jnp.where(chosen, iota((rows, edges), 1) - rank, 0)
    shift_own = (own - 1).bit_length()
    kind_bits = 8
    packed = lax.shift_left(lax.shift_left(found, shift_own) + first, kind_bits) + kind
    values = [stacked(k) for k in range(3)] + [packed]
    for bit in range((edges - 1).bit_length()):
        jump = 1 << bit
        moves = jnp.bitwise_and(lax.shift_right_logical(left, bit), 1)
        arrives = pltpu.roll(moves, edges - jump, 1) > 0
        values = [jnp.where(arrives, pltpu.roll(v, edges - jump, 1), v) for v in values]
        stays = jnp.where(moves > 0, 0, left)
        left = jnp.where(arrives, pltpu.roll(left, edges - jump, 1), stays)
    packed = values[3]
    fields[0] = -values[0]
    fields[1] = -values[1]
    fields[2] = -values[2]
    fields[3] = lax.shift_right_logical(packed, shift_own + kind_bits).astype(F32)
    fields[4] = jnp.bitwise_and(
        lax.shift_right_logical(packed, kind_bits), (1 << shift_own) - 1
    ).astype(F32)
    fields[5] = jnp.bitwise_and(packed, (1 << kind_bits) - 1).astype(F32)

    row1 = iota((rows, 1), 0)
    sizes = [
        jnp.sum(jnp.where(row1 == b, seen, 0.0)).astype(jnp.int32) for b in range(count)
    ]
    begins = [None]
    for size in sizes[1:]:
        begins.append(filled)
        filled = filled + size

    def place(b, tile):
        if isinstance(tile, int):
            at = slice(tile * LANES, (tile + 1) * LANES)
        else:
            at = pl.ds(pl.multiple_of(tile * LANES, LANES), LANES)
        piece = jnp.concatenate(
            [fields[k, b : b + 1, at] for k in range(5)]
            + [jnp.full((1, LANES), float(b), F32), jnp.zeros((1, LANES), F32)]
            + [fields[5, b : b + 1, at]],
            axis=0,
        )
        put(list_out, piece, begins[b] + tile * LANES, sizes[b] - tile * LANES)

    for b in range(1, count):
        place(b, 0)
    for b in range(1, count):

        def more(tile, _, b=b):
            place(b, tile)
            return 0

        lax.fori_loop(1, (sizes[b] + LANES - 1) // LANES, more, 0)
    return start, filled


def prepare_kernel(*refs):
    given, outs, held, sems = refs[:5], refs[5:12], refs[12:17], refs[17]
    copies = [
        pltpu.make_async_copy(source, target, sems.at[k])
        for k, (source, target) in enumerate(zip(given, held))
    ]
    for copy in copies:
        copy.start()
    for copy in copies:
        copy.wait()
    in_ref, mid_ref, out_ref, embed_ref, readout_ref = held
    rows = jnp.concatenate([embed_ref[...], readout_ref[...]], axis=0)
    small = outs[6]
    small[...] = jnp.zeros_like(small)
    small[0 : rows.shape[0], :] = rows
    for layer in range(in_ref.shape[0]):
        into = in_ref[layer]
        middle = mid_ref[layer]
        last = out_ref[layer]
        in_fw, mid_fw, out_fw, in_bw, mid_bw, out_bw = (out.at[layer] for out in outs[:6])
        high, low = split_f32(into)
        in_fw[...] = (
            jnp.concatenate([high, low, high, jnp.zeros_like(high)], axis=0).T.astype(BF16)
        )
        mid_fw[...] = stack_weights(middle)
        out_fw[...] = stack_weights(last)
        into_t = jnp.concatenate([into, jnp.zeros_like(into)], axis=0).T
        in_bw[...] = stack_weights(into_t)
        mid_bw[...] = stack_weights(middle.T)
        high, low = split(last)
        out_bw[...] = jnp.concatenate([high, low, high], axis=1)


def multiples(dist, count):
    turn = dist * (math.pi / CUTOFF) - 0.5 * math.pi
    square = turn * turn
    high = 1.0 / math.factorial(15)
    sine_turn = -high * square + 1.0 / math.factorial(13)
    for order in (11, 9, 7, 5, 3, 1):
        sign = 1.0 if order % 4 == 1 else -1.0
        sine_turn = sine_turn * square + sign / math.factorial(order)
    cosine_turn = square * (1.0 / math.factorial(16)) - 1.0 / math.factorial(14)
    for order in (12, 10, 8, 6, 4, 2, 0):
        sign = 1.0 if order % 4 == 0 else -1.0
        cosine_turn = cosine_turn * square + sign / math.factorial(order)
    s, c = cosine_turn, -sine_turn * turn
    order = iota((count, dist.shape[1]), 0) + 1
    sine = jnp.zeros(order.shape, F32)
    cosine = jnp.ones(order.shape, F32)
    bit = 1
    while True:
        here = jnp.bitwise_and(order, bit) > 0
        more_s = sine * c + cosine * s
        more_c = cosine * c - sine * s
        sine = jnp.where(here, more_s, sine)
        cosine = jnp.where(here, more_c, cosine)
        bit *= 2
        if bit > count:
            return sine, cosine
        s, c = 2.0 * s * c, 1.0 - 2.0 * s * s


def geometry(chunk, need_slopes):
    vec = [chunk[k : k + 1] for k in range(3)]
    dist = jnp.sqrt(vec[0] * vec[0] + vec[1] * vec[1] + vec[2] * vec[2])
    inv = 1.0 / dist
    ux, uy, uz = (v * inv for v in vec)
    values = [
        jnp.ones_like(dist),
        ROOT3 * ux,
        ROOT3 * uy,
        ROOT3 * uz,
        ROOT15 * ux * uy,
        ROOT15 * uy * uz,
        0.5 * ROOT5 * (3.0 * uz * uz - 1.0),
        ROOT15 * ux * uz,
        0.5 * ROOT15 * (ux * ux - uy * uy),
    ]
    sine, cosine = multiples(dist, 8)
    scale = math.sqrt(2.0 / CUTOFF) * inv
    basis = sine * scale
    x = dist * (1.0 / CUTOFF)
    x2 = x * x
    x4 = x2 * x2
    envelope = 1.0 + x4 * x * (-21.0 + x * (35.0 - 15.0 * x))
    slopes = None
    if need_slopes:
        orders = (iota(sine.shape, 0) + 1).astype(F32) * (math.pi / CUTOFF)
        d_basis = orders * cosine * scale - basis * inv
        d_envelope = x4 * (-105.0 + x * (210.0 - 105.0 * x)) * (1.0 / CUTOFF)
        slopes = (d_basis, d_envelope)
    return inv, (ux, uy, uz), values, basis, envelope, slopes


def radial_hidden(basis, in_fw, mid_fw):
    z1 = dot(in_fw, stack_acts_f32(basis))
    z2 = dot(mid_fw, stack_acts(z1 * sigmoid(z1)))
    return z1, z2


def own_hot(chunk, own):
    target = chunk[3:4].astype(jnp.int32)
    return (iota((own, target.shape[1]), 0) == target).astype(F32).astype(BF16)


def scaled_hots(chunk, own, values):
    hot = own_hot(chunk, own)
    out = []
    for begin, size in SPANS:
        pairs = [split(values[m]) for m in range(begin, begin + size)]
        out.append(
            jnp.concatenate([hot * high for high, _ in pairs] + [hot * low for _, low in pairs], axis=0)
        )
    return out


def other_hot(chunk, own, total):
    atom = chunk[4:5].astype(jnp.int32)
    hot = (iota((own, atom.shape[1]), 0) == atom).astype(F32).astype(BF16)
    block = chunk[5:6]
    return jnp.concatenate(
        [hot * (block == float(b)).astype(F32).astype(BF16) for b in range(total // own)], axis=0
    )


def lanes_at(start, size):
    return pl.ds(pl.multiple_of(start, LANES), size)


def sweep(start, stop, body):
    start = lax.shift_left(lax.shift_right_arithmetic(start, 7), 7)
    for size in STEPS:
        rest = jnp.maximum(stop - start, 0)
        number = (rest + (STEPS[-1] if size != STEPS[-1] else size) - 1) // size

        def step(index, _, start=start, size=size):
            body(lanes_at(start + index * size, size), size)
            return 0

        lax.fori_loop(0, number, step, 0)
        start = start + number * size


def kind_columns(small, kinds, mix):
    mixed = dot_high(small[0:kinds, :], mix)
    return [mixed[k : k + 1].T for k in range(kinds)]


def kind_features(chunk, columns):
    kind = chunk[7:8]
    out = jnp.where(kind == 0.0, columns[0], 0.0)
    for index in range(1, len(columns)):
        out = out + jnp.where(kind == float(index), columns[index], 0.0)
    return out


def collect(amat, chunk, feat, values, envelope, z2, out_fw, own):
    width = feat.shape[0]
    units = z2 * sigmoid(z2) * (INV_COUNT * envelope)
    weights = dot(out_fw, stack_acts(units))
    hots = scaled_hots(chunk, own, values)
    for degree, (begin, size) in enumerate(SPANS):
        high, low = split(weights[degree * width : (degree + 1) * width] * feat)
        parts = dot(hots[degree], jnp.concatenate([high, low], axis=0), NT)
        rows = size * own
        at = slice(begin * own, (begin + size) * own)
        amat[at, :] += (parts[:rows, :width] + parts[:rows, width:]) + (
            parts[rows:, :width] + parts[rows:, width:]
        )


def node_forward(amat, features, update, own):
    parts = [amat[m * own : (m + 1) * own, :] for m in range(9)]
    inv1 = sum(p * p for p in parts[1:4])
    inv2 = sum(p * p for p in parts[4:9])
    preact = dot_high(jnp.concatenate([parts[0], inv1, inv2], axis=1), update)
    return features + preact * sigmoid(preact), preact


def node_back(amat, d_features, preact, update, own, d_amat):
    width = d_features.shape[1]
    gate = sigmoid(preact)
    d_pre = d_features * gate * (1.0 + preact * (1.0 - gate))
    d_inv = dot_high(d_pre, update, NT)
    for degree, (begin, size) in enumerate(SPANS):
        for m in range(begin, begin + size):
            value = d_inv[:, degree * width : (degree + 1) * width]
            if degree > 0:
                value = 2.0 * amat[m * own : (m + 1) * own, :] * value
            high, low = split_f32(value)
            turned = jnp.concatenate([high, low], axis=0).T
            d_amat[m * width : (m + 1) * width, :] = turned.astype(BF16)


def edge_backward(chunk, feat, hidden, own, in_fw, mid_fw, out_fw, in_bw, mid_bw, out_bw, d_amat):
    width = feat.shape[0]
    inv, unit, values, basis, envelope, (d_basis, d_envelope) = geometry(chunk, True)
    z1, z2 = radial_hidden(basis, in_fw, mid_fw) if hidden is None else hidden
    gate1, gate2 = sigmoid(z1), sigmoid(z2)
    scale = INV_COUNT * envelope
    units = z2 * gate2
    weights = dot(out_fw, stack_acts(units * scale))
    hot = own_hot(chunk, own)
    rows = dot(d_amat[...], jnp.concatenate([hot, hot], axis=0))
    pulled = []
    d_mixed = 0.0
    d_values = []
    for degree, (begin, size) in enumerate(SPANS):
        weight = weights[degree * width : (degree + 1) * width]
        product = weight * feat
        term = 0.0
        for m in range(begin, begin + size):
            row = rows[m * width : (m + 1) * width]
            if m == 0:
                term = row
                d_values.append(None)
                continue
            term = term + row * values[m]
            d_values.append(jnp.sum(row * product, axis=0, keepdims=True))
        d_mixed = d_mixed + weight * term
        pulled.append(feat * term)
    pulled = jnp.concatenate(pulled, axis=0)
    d_units = dot(out_bw, stack_acts(pulled))
    d_env = INV_COUNT * jnp.sum(units * d_units, axis=0, keepdims=True)
    d_z2 = d_units * scale * gate2 * (1.0 + z2 * (1.0 - gate2))
    d_hidden = dot(mid_bw, stack_acts(d_z2))
    d_z1 = d_hidden * gate1 * (1.0 + z1 * (1.0 - gate1))
    d_b = dot(in_bw, stack_acts(d_z1))[0:8]
    d_dist = jnp.sum(d_b * d_basis, axis=0, keepdims=True) + d_env * d_envelope
    ux, uy, uz = unit
    y = d_values
    dux = ROOT3 * y[1] + ROOT15 * (uy * y[4] + uz * y[7] + ux * y[8])
    duy = ROOT3 * y[2] + ROOT15 * (ux * y[4] + uz * y[5] - uy * y[8])
    duz = ROOT3 * y[3] + ROOT15 * (uy * y[5] + ux * y[7]) + 3.0 * ROOT5 * uz * y[6]
    along = ux * dux + uy * duy + uz * duz
    grad = [(du - u * along) * inv + d_dist * u for u, du in zip(unit, (dux, duy, duz))]
    return grad, d_mixed


def first_sums(list_ref, start, stop, amat, columns, in_fw, mid_fw, out_fw, own):
    def body(at, _):
        chunk = list_ref[:, at]
        _, _, values, basis, envelope, _ = geometry(chunk, False)
        _, z2 = radial_hidden(basis, in_fw[0], mid_fw[0])
        feat = kind_features(chunk, columns)
        collect(amat, chunk, feat, values, envelope, z2, out_fw[0], own)

    sweep(start, stop, body)


def second_sums(list_ref, start, stop, amat, features_t, in_fw, mid_fw, out_fw, own, keep):
    total = features_t.shape[1]

    def body(at, _):
        chunk = list_ref[:, at]
        _, _, values, basis, envelope, _ = geometry(chunk, False)
        z1, z2 = radial_hidden(basis, in_fw[1], mid_fw[1])
        feat = gather(features_t, other_hot(chunk, own, total))
        if keep is not None:
            for kept, value in zip(keep, (feat, z1, z2)):
                kept[:, at] = value
        collect(amat, chunk, feat, values, envelope, z2, out_fw[1], own)

    sweep(start, stop, body)


def turn_features(features, features_t):
    high, low = split_f32(features.T)
    features_t[...] = jnp.concatenate([high, low], axis=0).astype(BF16)


def gather(features_t, hot):
    both = dot(features_t[...], hot)
    width = both.shape[0] // 2
    return both[:width] + both[width:]


def scatter_back(d_mixed_sum, hot, d_mixed):
    width = d_mixed.shape[0]
    high, low = split(d_mixed)
    both = dot(hot, jnp.concatenate([high, low], axis=0), NT)
    d_mixed_sum[...] += both[:, :width] + both[:, width:]


def rows_of(grad):
    return jnp.concatenate(grad + [jnp.zeros((5, grad[0].shape[1]), F32)], axis=0)


def split_three(pull):
    high, rest = split_f32(pull)
    middle, low = split_f32(rest)
    return jnp.concatenate([high, middle, low, jnp.zeros_like(low)], axis=0).astype(BF16)


def add_three(moved):
    return moved[0:8] + moved[8:16] + moved[16:24]


def inner_first_kernel(own, edges, kinds, *refs):
    (record, small, mix_ref, in_fw, mid_fw, out_fw, list_out, number_out, amat_out) = refs
    number = build_inner(own, edges, record, list_out)
    number_out[0] = number
    amat_out[...] = jnp.zeros_like(amat_out)
    columns = kind_columns(small, kinds, mix_ref[0])
    first_sums(list_out, 0, number, amat_out, columns, in_fw, mid_fw, out_fw, own)


def outer_first_kernel(hood, sections, own, edges, kinds, *refs):
    (
        got,
        inner_amat,
        small,
        mix_ref,
        update_ref,
        in_fw,
        mid_fw,
        out_fw,
        list_out,
        range_out,
        amat_out,
        preact_out,
        h_out,
        w_out,
        fields,
    ) = refs
    start, stop = build_outer(hood, sections, own, edges, got, list_out, fields)
    range_out[0] = start
    range_out[1] = stop
    amat_out[...] = inner_amat[...]
    columns = kind_columns(small, kinds, mix_ref[0])
    first_sums(list_out, start, stop, amat_out, columns, in_fw, mid_fw, out_fw, own)
    kind = got[5:6, 0:own].astype(jnp.int32)
    hot = (iota((8, own), 0) == kind).astype(F32).T
    rows = jnp.where(iota((8, small.shape[1]), 0) < kinds, small[...], 0.0)
    features = dot_high(hot, rows)
    h, preact = node_forward(amat_out, features, update_ref[0], own)
    preact_out[...] = preact
    h_out[...] = h
    w_out[...] = dot_high(h, mix_ref[1])


def inner_second_kernel(own, *refs):
    (number_ref, list_ref, w_ref, in_fw, mid_fw, out_fw, amat_out, features_t) = refs
    amat_out[...] = jnp.zeros_like(amat_out)
    turn_features(w_ref[...], features_t)
    second_sums(
        list_ref, 0, number_ref[0], amat_out, features_t, in_fw, mid_fw, out_fw, own, None
    )


def outer_second_kernel(count, own, kinds, *refs):
    (
        everyone_ref,
        range_ref,
        list_ref,
        inner_amat,
        h_ref,
        update_ref,
        small,
        in_fw,
        mid_fw,
        out_fw,
        in_bw,
        mid_bw,
        out_bw,
        energy_out,
        grad_out,
        d_mixed_sum,
        d_amat,
        features_t,
        amat,
        kept_feat,
        kept_first,
        kept_second,
    ) = refs
    total = count * own
    start, stop = range_ref[0], range_ref[1]
    turn_features(everyone_ref[...], features_t)
    amat[...] = inner_amat[...]
    d_mixed_sum[...] = jnp.zeros_like(d_mixed_sum)
    keep = (kept_feat, kept_first, kept_second)
    second_sums(list_ref, start, stop, amat, features_t, in_fw, mid_fw, out_fw, own, keep)
    h1 = h_ref[...]
    h2, preact = node_forward(amat, h1, update_ref[1], own)
    readout = small[kinds : kinds + 2, :]
    energy_out[...] = dot_high(readout[0:1], h1, NT) + dot_high(readout[1:2], h2, NT)
    d_features = jnp.broadcast_to(readout[1:2], h1.shape)
    node_back(amat, d_features, preact, update_ref[1], own, d_amat)
    weights = [ref[1] for ref in (in_fw, mid_fw, out_fw, in_bw, mid_bw, out_bw)]

    def backward(at, _):
        chunk = list_ref[:, at]
        hidden = (kept_first[:, at], kept_second[:, at])
        grad, d_mixed = edge_backward(chunk, kept_feat[:, at], hidden, own, *weights, d_amat)
        grad_out[:, at] = rows_of(grad)
        scatter_back(d_mixed_sum, other_hot(chunk, own, total), d_mixed)

    sweep(start, stop, backward)


def inner_second_back_kernel(own, *refs):
    (number_ref, list_ref, w_ref, d_amat) = refs[:4]
    weights = [ref[1] for ref in refs[4:10]]
    grad_out, d_mixed_sum, features_t = refs[10:]
    d_mixed_sum[...] = jnp.zeros_like(d_mixed_sum)
    turn_features(w_ref[...], features_t)

    def backward(at, _):
        chunk = list_ref[:, at]
        hot = other_hot(chunk, own, own)
        grad, d_mixed = edge_backward(
            chunk, gather(features_t, hot), None, own, *weights, d_amat
        )
        grad_out[:, at] = rows_of(grad)
        scatter_back(d_mixed_sum, hot, d_mixed)

    sweep(0, number_ref[0], backward)


def outer_first_back_kernel(count, own, kinds, *refs):
    (
        d_mixed_ref,
        inner_d_mixed,
        range_ref,
        list_ref,
        grad_ref,
        amat_ref,
        preact_ref,
        small,
        mix_ref,
        update_ref,
    ) = refs[:10]
    weights = [ref[0] for ref in refs[10:16]]
    force_out, d_amat, force = refs[16:]
    total = count * own
    columns = kind_columns(small, kinds, mix_ref[0])
    readout = small[kinds : kinds + 2, :]
    d_mixed = d_mixed_ref[...] + inner_d_mixed[...]
    d_features = readout[0:1] + readout[1:2] + dot_high(d_mixed, mix_ref[1], NT)
    node_back(amat_ref, d_features, preact_ref[...], update_ref[0], own, d_amat)
    force[...] = jnp.zeros_like(force)

    def backward(at, _):
        chunk = list_ref[:, at]
        feat = kind_features(chunk, columns)
        grad, _ = edge_backward(chunk, feat, None, own, *weights, d_amat)
        parts = split_three(rows_of(grad) + grad_ref[:, at])
        force[...] -= add_three(dot(parts, other_hot(chunk, own, total), NT))
        force[:, 0:own] += add_three(dot(parts, own_hot(chunk, own), NT))

    sweep(range_ref[0], range_ref[1], backward)
    for b in range(count):
        force_out[8 * b : 8 * b + 8, :] = force[:, b * own : (b + 1) * own]


def inner_first_back_kernel(own, kinds, *refs):
    (number_ref, list_ref, grad_ref, d_amat, small, mix_ref) = refs[:6]
    weights = [ref[0] for ref in refs[6:12]]
    force_out = refs[12]
    columns = kind_columns(small, kinds, mix_ref[0])
    force_out[...] = jnp.zeros_like(force_out)

    def backward(at, _):
        chunk = list_ref[:, at]
        feat = kind_features(chunk, columns)
        grad, _ = edge_backward(chunk, feat, None, own, *weights, d_amat)
        parts = split_three(rows_of(grad) + grad_ref[:, at])
        hot = own_hot(chunk, own) - other_hot(chunk, own, own)
        force_out[...] += add_three(dot(parts, hot, NT))

    sweep(0, number_ref[0], backward)


LIMIT = 48 * 1024 * 1024


def call(kernel, outs, scratch, args, smem_in=(), smem_out=(), micros=4):
    vmem = pl.BlockSpec(memory_space=pltpu.VMEM)
    smem = pl.BlockSpec(memory_space=pltpu.SMEM)
    return pl.pallas_call(
        kernel,
        out_shape=outs,
        in_specs=[smem if k in smem_in else vmem for k in range(len(args))],
        out_specs=[smem if k in smem_out else vmem for k in range(len(outs))],
        scratch_shapes=scratch,
        compiler_params=pltpu.CompilerParams(vmem_limit_bytes=LIMIT),
        cost_estimate=pl.CostEstimate(
            flops=micros * 1000 * 1000 * 1000, bytes_accessed=micros * 1000 * 1000, transcendentals=0
        ),
    )(*args)


def call_copying(kernel, outs, args, megabytes):
    vmem = pl.BlockSpec(memory_space=pltpu.VMEM)
    return pl.pallas_call(
        kernel,
        out_shape=outs,
        in_specs=[pl.BlockSpec(memory_space=pltpu.HBM)] * len(args),
        out_specs=[vmem] * len(outs),
        scratch_shapes=[pltpu.VMEM(value.shape, value.dtype) for value in args]
        + [pltpu.SemaphoreType.DMA((len(args),))],
        compiler_params=pltpu.CompilerParams(vmem_limit_bytes=megabytes * 1024 * 1024),
    )(*args)


def shards(
    sizes,
    species,
    send_x,
    send_y,
    send_z,
    edge_first,
    edge_second,
    edge_live,
    edge_vec,
    embed,
    radial_in,
    radial_mid,
    radial_out,
    mix,
    update,
    readout,
):
    hood = Neighbourhood(sizes)
    count = hood.count
    own = species.shape[0]
    width = embed.shape[1]
    layers = readout.shape[0]
    hidden = radial_mid.shape[1]
    slots = edge_first.shape[1]
    edges = round_up(slots, BLOCK)
    extra = edges - slots
    if extra:
        edge_first = jnp.pad(edge_first, ((0, 0), (0, extra)))
        edge_second = jnp.pad(edge_second, ((0, 0), (0, extra)))
        edge_live = jnp.pad(edge_live, ((0, 0), (0, extra)))
        edge_vec = jnp.pad(edge_vec, ((0, 0), (0, extra)), constant_values=1.0)
    faces = tuple(send.shape[2] for send in (send_z, send_y, send_x))
    sections = Sections(own, faces)
    shape = jax.ShapeDtypeStruct
    kinds = embed.shape[0]
    packed = call_copying(
        pack_kernel,
        [shape((8, edges), F32)],
        [species[None, :], send_x, send_y, send_z, edge_first, edge_second, edge_live, edge_vec],
        60,
    )[0]
    *weights, small = call_copying(
        prepare_kernel,
        [
            shape((layers, hidden, 32), BF16),
            shape((layers, hidden, 3 * hidden), BF16),
            shape((layers, 3 * width, 3 * hidden), BF16),
            shape((layers, 16, 3 * hidden), BF16),
            shape((layers, hidden, 3 * hidden), BF16),
            shape((layers, hidden, 9 * width), BF16),
            shape((8, width), F32),
        ],
        [radial_in, radial_mid, radial_out, embed, readout],
        16,
    )
    forward_weights = weights[:3]
    sums = shape((9 * own, width), F32)
    rows = shape((own, width), F32)
    turned = shape((9 * width, 2 * own), BF16)
    inner_size = round_up(2 * edges + LANES, STEPS[0])
    outer_size = round_up((count + 1) * edges + LANES, STEPS[0]) + STEPS[0]

    got, along_x = hood.fetch(packed)
    inner_list, number, inner_amat = call(
        functools.partial(inner_first_kernel, own, edges, kinds),
        [shape((8, inner_size), F32), shape((1,), jnp.int32), sums],
        [],
        [along_x, small, mix] + forward_weights,
        smem_out=(1,),
    )
    outer_list, bounds, amat1, preact1, h1, w2 = call(
        functools.partial(outer_first_kernel, hood, sections, own, edges, kinds),
        [shape((8, outer_size), F32), shape((2,), jnp.int32), sums, rows, rows, rows],
        [pltpu.VMEM((6, round_up(count, 8), edges), F32)],
        [got, inner_amat, small, mix, update] + forward_weights,
        smem_out=(1,),
    )

    everyone, _ = hood.fetch(w2)
    (inner_amat,) = call(
        functools.partial(inner_second_kernel, own),
        [sums],
        [pltpu.VMEM((2 * width, own), BF16)],
        [number, inner_list, w2] + forward_weights,
        smem_in=(0,),
    )
    energies, grads, d_mixed, d_amat2 = call(
        functools.partial(outer_second_kernel, count, own, kinds),
        [shape((1, own), F32), shape((8, outer_size), F32), shape((count * own, width), F32), turned],
        [
            pltpu.VMEM((2 * width, count * own), BF16),
            pltpu.VMEM((9 * own, width), F32),
            pltpu.VMEM((width, outer_size), F32),
            pltpu.VMEM((hidden, outer_size), F32),
            pltpu.VMEM((hidden, outer_size), F32),
        ],
        [everyone, bounds, outer_list, inner_amat, h1, update, small] + weights,
        smem_in=(1,),
    )

    d_mixed = hood.give(d_mixed)
    inner_grads, inner_d_mixed = call(
        functools.partial(inner_second_back_kernel, own),
        [shape((8, inner_size), F32), rows],
        [pltpu.VMEM((2 * width, own), BF16)],
        [number, inner_list, w2, d_amat2] + weights,
        smem_in=(0,),
    )
    forces, d_amat1 = call(
        functools.partial(outer_first_back_kernel, count, own, kinds),
        [shape((8 * count, own), F32), turned],
        [pltpu.VMEM((8, count * own), F32)],
        [d_mixed, inner_d_mixed, bounds, outer_list, grads, amat1, preact1, small, mix, update]
        + weights,
        smem_in=(2,),
    )

    forces = hood.give(forces)
    (inner_forces,) = call(
        functools.partial(inner_first_back_kernel, own, kinds),
        [shape((8, own), F32)],
        [],
        [number, inner_list, inner_grads, d_amat1, small, mix] + weights,
        smem_in=(0,),
    )
    return (energies.reshape(own), forces[:3] + inner_forces[:3])


def solution(mesh):
    sizes = tuple(mesh.shape[axis] for axis in ("gx", "gy", "gz"))
    split_all = ("parts", "gx", "gy", "gz")
    return jax.shard_map(
        functools.partial(shards, sizes),
        mesh=mesh,
        in_specs=(
            P(split_all),
            P(split_all, None, None),
            P(split_all, None, None),
            P(split_all, None, None),
            P(split_all, None),
            P(split_all, None),
            P(split_all, None),
            P(None, split_all),
            P(),
            P(),
            P(),
            P(),
            P(),
            P(),
            P(),
        ),
        out_specs=(P(split_all), P(None, split_all)),
        check_vma=False,
    )
```

```python
import functools
import math

import jax
import jax.numpy as jnp
from jax import lax
from jax.experimental import pallas as pl
from jax.experimental.pallas import tpu as pltpu
from jax.sharding import PartitionSpec as P

HIGH = lax.Precision.HIGHEST
CUTOFF = 5.0
INV_COUNT = 0.2
ROOT3 = math.sqrt(3.0)
ROOT5 = math.sqrt(5.0)
ROOT15 = math.sqrt(15.0)
SPANS = ((0, 1), (1, 3), (4, 5))
LANES = 128
BLOCK = 256
STEPS = (1024, 512)
F32 = jnp.float32
BF16 = jnp.bfloat16
NT = (((1,), (1,)), ((), ()))
NN = (((1,), (0,)), ((), ()))


def round_up(value, unit):
    return -(-value // unit) * unit


def dot(left, right, dims=NN):
    return lax.dot_general(left, right, dims, preferred_element_type=F32)


def dot_high(left, right, dims=NN):
    return lax.dot_general(left, right, dims, preferred_element_type=F32, precision=HIGH)


def split(value):
    high = value.astype(BF16)
    return high, (value - high.astype(F32)).astype(BF16)


def split_f32(value):
    high = value.astype(BF16).astype(F32)
    return high, value - high


def stack_weights(value):
    high, low = split_f32(value)
    return jnp.concatenate([high, low, high, low], axis=0).T.astype(BF16)


def stack_acts(value):
    high, low = split(value)
    return jnp.concatenate([high, high, low, low], axis=0)


def stack_three(value):
    high, low = split(value)
    return jnp.concatenate([high, high, low], axis=0)


def stack_acts_f32(value):
    high, low = split_f32(value)
    return jnp.concatenate([high, high, low, low], axis=0).astype(BF16)


def iota(shape, dim):
    return lax.broadcasted_iota(jnp.int32, shape, dim)


def sigmoid(value):
    return 0.5 * jnp.tanh(0.5 * value) + 0.5


def axis_steps(size):
    return (0, 1, -1) if size > 2 else tuple(range(size))


class Neighbourhood:
    def __init__(self, sizes):
        self.sizes = sizes
        self.steps = [axis_steps(size) for size in sizes]
        self.shifts = [
            (dx, dy, dz) for dz in self.steps[2] for dy in self.steps[1] for dx in self.steps[0]
        ]
        self.place = {
            tuple(s % n for s, n in zip(shift, sizes)): b for b, shift in enumerate(self.shifts)
        }
        self.count = len(self.shifts)

    def block(self, *shift):
        return self.place.get(tuple(s % n for s, n in zip(shift, self.sizes)))

    def moved(self, rows, axis, step):
        size = self.sizes[axis]
        pairs = [(i, (i + step) % size) for i in range(size)]
        return lax.ppermute(rows, ("gx", "gy", "gz")[axis], pairs)

    def fetch(self, rows):
        along_x = None
        for axis in range(3):
            got = [rows] + [self.moved(rows, axis, -step) for step in self.steps[axis][1:]]
            if len(got) > 1:
                rows = jnp.concatenate(got, axis=0)
            if axis == 0:
                along_x = rows
        return rows, along_x

    def give(self, rows, beside):
        for axis in (2, 1, 0):
            if axis == 0:
                rows, beside = lax.optimization_barrier((rows, beside))
            steps = self.steps[axis]
            size = rows.shape[0] // len(steps)
            total = rows[:size]
            for index, step in enumerate(steps[1:], 1):
                total = total + self.moved(rows[index * size : (index + 1) * size], axis, step)
            rows = total
        return rows, beside


class Sections:
    def __init__(self, own, faces):
        sizes = [own] + [face for face in faces for _ in range(2)]
        self.starts, self.spots, self.widths = [], [], []
        start = spot = 0
        for size in sizes:
            self.starts.append(start)
            self.spots.append(spot)
            self.widths.append(round_up(size, LANES))
            start += size
            spot += self.widths[-1]
        self.z_end, self.y_end, self.x_end = self.spots[3], self.spots[5], spot

    def align(self, entry):
        out = entry
        for k in range(1, len(self.starts)):
            gap = (self.spots[k] - self.starts[k]) - (self.spots[k - 1] - self.starts[k - 1])
            out = out + jnp.where(entry >= self.starts[k], gap, 0)
        return out


def pack_kernel(*refs):
    given, out, held, sems = refs[:8], refs[8], refs[9:17], refs[17]
    copies = [
        pltpu.make_async_copy(source, target, sems.at[k])
        for k, (source, target) in enumerate(zip(given, held))
    ]
    for copy in copies:
        copy.start()
    out[...] = jnp.zeros_like(out)
    for copy in copies:
        copy.wait()
    species_ref, sx_ref, sy_ref, sz_ref, first_ref, second_ref, live_ref, vec_ref = held
    out[0:3, :] = vec_ref[...]
    out[3:4, :] = first_ref[...].astype(F32)
    out[4:5, :] = jnp.where(live_ref[...] > 0, second_ref[...], -1).astype(F32)
    own = species_ref.shape[1]
    out[5:6, 0:own] = species_ref[...].astype(F32)
    spot = round_up(own, LANES)
    for ref in (sz_ref, sy_ref, sx_ref):
        face = ref.shape[2]
        for side in range(2):
            out[5:6, spot : spot + face] = ref[0, 1 - side : 2 - side, :].astype(F32)
            spot += round_up(face, LANES)


ALONG_LANES = lax.GatherDimensionNumbers(
    offset_dims=(),
    collapsed_slice_dims=(1,),
    start_index_map=(1,),
    operand_batching_dims=(0,),
    start_indices_batching_dims=(0,),
)


def lookup(table, index):
    given = index.shape[0]
    rows = round_up(given, 8)
    if rows != given:
        index = jnp.broadcast_to(index[0:1], (rows, index.shape[1])) if given == 1 else jnp.concatenate(
            [index] + [index[0:1]] * (rows - given), axis=0
        )
        if table.shape[0] != 1:
            table = jnp.concatenate([table] + [table[0:1]] * (rows - given), axis=0)
    table = jnp.broadcast_to(table, (rows, table.shape[1]))
    parts = []
    for start in range(0, index.shape[1], LANES):
        at = index[:, start : start + LANES]
        low = jnp.bitwise_and(at, LANES - 1)
        tile = lax.shift_right_arithmetic(at, 7)
        out = None
        for k in range(table.shape[1] // LANES):
            found = lax.gather(
                table[:, k * LANES : (k + 1) * LANES],
                low[:, :, None],
                ALONG_LANES,
                slice_sizes=(1, 1),
                mode=lax.GatherScatterMode.PROMISE_IN_BOUNDS,
            )
            out = found if out is None else jnp.where(tile == k, found, out)
        parts.append(out)
    out = parts[0] if len(parts) == 1 else jnp.concatenate(parts, axis=1)
    return out[0:given]


def list_tables(hood, sections, own, got):
    def table(block, section):
        at = slice(sections.spots[section], sections.spots[section] + sections.widths[section])
        return got[8 * block + 5 : 8 * block + 6, at].astype(jnp.int32)

    lane = iota((1, sections.widths[0]), 1)
    z_lists = {}

    def z_list(dx, dy):
        block = hood.block(dx, dy, 0)
        if block not in z_lists:
            parts = [block * own + lane]
            for section, step in ((1, 1), (2, -1)):
                other = hood.block(dx, dy, step)
                parts.append(other * own + table(other, section))
            z_lists[block] = jnp.concatenate(parts, axis=1)
        return z_lists[block]

    y_lists = {}

    def y_list(dx):
        block = hood.block(dx, 0, 0)
        if block not in y_lists:
            parts = [z_list(dx, 0)]
            for section, step in ((3, 1), (4, -1)):
                entry = table(hood.block(dx, step, 0), section)
                parts.append(lookup(z_list(dx, step), sections.align(entry)))
            y_lists[block] = jnp.concatenate(parts, axis=1)
        return y_lists[block]

    parts = [y_list(0)]
    for section, step in ((5, 1), (6, -1)):
        entry = table(hood.block(step, 0, 0), section)
        parts.append(lookup(y_list(step), sections.align(entry)))
    mine = jnp.concatenate(parts, axis=1)

    def none(*which):
        return jnp.full((1, sum(sections.widths[k] for k in which)), -1, jnp.int32)

    z_back = {}
    for dz in hood.steps[2]:
        if dz == 0:
            z_back[dz] = jnp.concatenate([jnp.where(lane < own, lane, -1), none(1, 2)], axis=1)
        else:
            parts = [none(0)]
            for section, step in ((1, 1), (2, -1)):
                parts.append(table(0, section) if hood.block(0, 0, dz + step) == 0 else none(section))
            z_back[dz] = jnp.concatenate(parts, axis=1)
    y_back = {}
    for dz in hood.steps[2]:
        for dy in hood.steps[1]:
            if dy == 0:
                y_back[dy, dz] = jnp.concatenate([z_back[dz], none(3, 4)], axis=1)
                continue
            parts = [none(0, 1, 2)]
            for section, step in ((3, 1), (4, -1)):
                if (dy + step) % hood.sizes[1] == 0:
                    entry = table(hood.block(0, 0, dz), section)
                    parts.append(lookup(z_back[dz], sections.align(entry)))
                else:
                    parts.append(none(section))
            y_back[dy, dz] = jnp.concatenate(parts, axis=1)
    wanted = []
    for shift in hood.shifts:
        for section, step in ((5, 1), (6, -1)):
            if shift[0] != 0 and (shift[0] + step) % hood.sizes[0] == 0:
                wanted.append((shift, section))
    found = {}
    if wanted:
        entries = jnp.concatenate(
            [table(hood.block(0, dy, dz), section) for (_, dy, dz), section in wanted], axis=0
        )
        lists = jnp.concatenate([y_back[dy, dz] for (_, dy, dz), _ in wanted], axis=0)
        rows = lookup(lists, sections.align(entries))
        for number, key in enumerate(wanted):
            found[key] = rows[number : number + 1]
    back = []
    for shift in hood.shifts:
        if shift[0] == 0:
            back.append(jnp.concatenate([y_back[shift[1], shift[2]], none(5, 6)], axis=1))
        else:
            tail = [found.get((shift, section), none(section)) for section in (5, 6)]
            back.append(jnp.concatenate([none(0, 1, 2, 3, 4)] + tail, axis=1))
    return mine, back


def empty_edges(size):
    sub = iota((8, size), 0)
    return jnp.where(sub == 0, 1.0, jnp.where((sub >= 3) & (sub <= 5), -1.0, 0.0))


def fill_empty(list_out, start, stop):
    tile = empty_edges(LANES)
    last = (jnp.maximum(stop, start) + STEPS[0] + LANES - 1) // LANES

    def fill(step, _):
        list_out[:, pl.ds(pl.multiple_of(step * LANES, LANES), LANES)] = tile
        return 0

    lax.fori_loop(start // LANES, last, fill, 0)


def put(list_out, piece, to, size):
    lane = iota((1, LANES), 1)
    turn = jnp.bitwise_and(to, LANES - 1)
    piece = pltpu.roll(piece, turn, 1)
    low = lax.shift_right_arithmetic(to, 7)
    stop = turn + size
    for part in range(2):
        here = pl.ds(pl.multiple_of((low + part) * LANES, LANES), LANES)
        if part == 0:
            inside = (lane >= turn) & (lane < stop)
        else:
            inside = (lane < turn) & (lane < stop - LANES)
        list_out[:, here] = jnp.where(inside, piece, list_out[:, here])


def count_true(mask):
    return jnp.sum(mask.astype(F32)).astype(jnp.int32)


def build_inner(own, edges, record, list_out):
    second = record[4:5, :].astype(jnp.int32)
    inner = (second >= 0) & (second < own)
    number = count_true(inner)
    kinds = record[5:6, 0 : round_up(own, LANES)].astype(jnp.int32)
    kind_second = lookup(kinds, jnp.where(inner, second, 0)).astype(F32)
    kind_first = lookup(kinds, record[3:4, :].astype(jnp.int32)).astype(F32)
    zero = jnp.zeros((1, edges), F32)
    vec, first, other = record[0:3, :], record[3:4, :], record[4:5, :]
    forward = jnp.concatenate([vec, first, other, zero, zero, kind_second], axis=0)
    list_out[:, 0:edges] = jnp.where(inner, forward, empty_edges(edges))
    fill_empty(list_out, edges, 2 * number)
    reverse = jnp.concatenate([-vec, other, first, zero, zero, kind_first], axis=0)
    for start in range(0, edges, LANES):
        put(list_out, reverse[:, start : start + LANES], number + start, number - start)
    return 2 * number


def build_outer(hood, sections, own, edges, got, list_out, fields):
    count = hood.count
    rows = round_up(count, 8)
    pad = rows - count
    mine, back = list_tables(hood, sections, own, got)

    def stacked(field):
        blocks = list(range(count)) + [0] * pad
        return jnp.concatenate([got[8 * b + field : 8 * b + field + 1, :] for b in blocks], axis=0)

    second = stacked(4).astype(jnp.int32)
    first = stacked(3).astype(jnp.int32)
    tables = jnp.concatenate([mine] + back[1:] + [mine] * pad, axis=0)
    found = lookup(tables, sections.align(jnp.maximum(second, 0)))
    row = iota((rows, edges), 0)
    chosen = (found >= 0) & (second >= 0) & (row < count) & (row > 0)
    kinds = jnp.concatenate(
        [got[8 * b + 5 : 8 * b + 6, 0 : sections.widths[0]] for b in range(count)]
        + [jnp.zeros((pad, sections.widths[0]), F32)] * (pad > 0),
        axis=0,
    ).astype(jnp.int32)
    kind = lookup(kinds, first)

    code = found[0:1]
    block = sum((code >= b * own).astype(jnp.int32) for b in range(1, count))
    atom = code - block * own
    others = lookup(kinds, jnp.broadcast_to(atom, (rows, edges)))
    other_kind = jnp.sum(jnp.where(row == block, others, 0).astype(F32), axis=0, keepdims=True)
    whole = jnp.concatenate(
        [
            got[0:4, :],
            atom.astype(F32),
            block.astype(F32),
            jnp.zeros((1, edges), F32),
            other_kind,
        ],
        axis=0,
    )
    list_out[:, 0:edges] = jnp.where(second[0:1] >= own, whole, empty_edges(edges))
    filled = count_true(second[0:1] >= 0)
    start = filled - count_true(second[0:1] >= own)

    before = (iota((BLOCK, BLOCK), 0) < iota((BLOCK, BLOCK), 1)).astype(F32).astype(BF16)
    taken = chosen.astype(F32)
    seen = jnp.zeros((rows, 1), F32)
    ranks = []
    for begin in range(0, edges, BLOCK):
        part = taken[:, begin : begin + BLOCK]
        ranks.append(dot(part.astype(BF16), before) + seen)
        seen = seen + jnp.sum(part, axis=1, keepdims=True)
    rank = jnp.concatenate(ranks, axis=1).astype(jnp.int32)
    left = jnp.where(chosen, iota((rows, edges), 1) - rank, 0)
    shift_own = (own - 1).bit_length()
    kind_bits = 8
    packed = lax.shift_left(lax.shift_left(found, shift_own) + first, kind_bits) + kind
    values = [stacked(k) for k in range(3)] + [packed]
    for bit in range((edges - 1).bit_length()):
        jump = 1 << bit
        moves = jnp.bitwise_and(lax.shift_right_logical(left, bit), 1)
        arrives = pltpu.roll(moves, edges - jump, 1) > 0
        values = [jnp.where(arrives, pltpu.roll(v, edges - jump, 1), v) for v in values]
        stays = jnp.where(moves > 0, 0, left)
        left = jnp.where(arrives, pltpu.roll(left, edges - jump, 1), stays)
    packed = values[3]
    fields[0] = -values[0]
    fields[1] = -values[1]
    fields[2] = -values[2]
    fields[3] = lax.shift_right_logical(packed, shift_own + kind_bits).astype(F32)
    fields[4] = jnp.bitwise_and(
        lax.shift_right_logical(packed, kind_bits), (1 << shift_own) - 1
    ).astype(F32)
    fields[5] = jnp.bitwise_and(packed, (1 << kind_bits) - 1).astype(F32)

    row1 = iota((rows, 1), 0)
    sizes = [
        jnp.sum(jnp.where(row1 == b, seen, 0.0)).astype(jnp.int32) for b in range(count)
    ]
    begins = [None]
    for size in sizes[1:]:
        begins.append(filled)
        filled = filled + size
    fill_empty(list_out, edges, filled)

    def place(b, tile):
        if isinstance(tile, int):
            at = slice(tile * LANES, (tile + 1) * LANES)
        else:
            at = pl.ds(pl.multiple_of(tile * LANES, LANES), LANES)
        piece = jnp.concatenate(
            [fields[k, b : b + 1, at] for k in range(5)]
            + [jnp.full((1, LANES), float(b), F32), jnp.zeros((1, LANES), F32)]
            + [fields[5, b : b + 1, at]],
            axis=0,
        )
        put(list_out, piece, begins[b] + tile * LANES, sizes[b] - tile * LANES)

    for b in range(1, count):
        place(b, 0)
    longest = functools.reduce(jnp.maximum, sizes[1:], jnp.int32(0))

    @pl.when(longest > LANES)
    def _():
        for b in range(1, count):

            def more(tile, _, b=b):
                place(b, tile)
                return 0

            lax.fori_loop(1, (sizes[b] + LANES - 1) // LANES, more, 0)

    return start, filled


def prepare_kernel(*refs):
    given, outs, held, sems = refs[:5], refs[5:12], refs[12:17], refs[17]
    copies = [
        pltpu.make_async_copy(source, target, sems.at[k])
        for k, (source, target) in enumerate(zip(given, held))
    ]
    for copy in copies:
        copy.start()
    for copy in copies:
        copy.wait()
    in_ref, mid_ref, out_ref, embed_ref, readout_ref = held
    rows = jnp.concatenate([embed_ref[...], readout_ref[...]], axis=0)
    small = outs[6]
    small[...] = jnp.zeros_like(small)
    small[0 : rows.shape[0], :] = rows
    for layer in range(in_ref.shape[0]):
        into = in_ref[layer]
        middle = mid_ref[layer]
        last = out_ref[layer]
        in_fw, mid_fw, out_fw, in_bw, mid_bw, out_bw = (out.at[layer] for out in outs[:6])
        in_fw[...] = stack_weights(into)
        mid_fw[...] = stack_weights(middle)
        out_fw[...] = stack_weights(last)
        into_t = jnp.concatenate([into, jnp.zeros_like(into)], axis=0).T
        in_bw[...] = stack_weights(into_t)
        mid_bw[...] = stack_weights(middle.T)
        high, low = split(last)
        out_bw[...] = jnp.concatenate([high, low, high], axis=1)


def multiples(dist, count):
    turn = dist * (math.pi / CUTOFF) - 0.5 * math.pi
    square = turn * turn
    high = 1.0 / math.factorial(15)
    sine_turn = -high * square + 1.0 / math.factorial(13)
    for order in (11, 9, 7, 5, 3, 1):
        sign = 1.0 if order % 4 == 1 else -1.0
        sine_turn = sine_turn * square + sign / math.factorial(order)
    cosine_turn = square * (1.0 / math.factorial(16)) - 1.0 / math.factorial(14)
    for order in (12, 10, 8, 6, 4, 2, 0):
        sign = 1.0 if order % 4 == 0 else -1.0
        cosine_turn = cosine_turn * square + sign / math.factorial(order)
    s, c = cosine_turn, -sine_turn * turn
    order = iota((count, dist.shape[1]), 0) + 1
    sine = jnp.zeros(order.shape, F32)
    cosine = jnp.ones(order.shape, F32)
    bit = 1
    while True:
        here = jnp.bitwise_and(order, bit) > 0
        more_s = sine * c + cosine * s
        more_c = cosine * c - sine * s
        sine = jnp.where(here, more_s, sine)
        cosine = jnp.where(here, more_c, cosine)
        bit *= 2
        if bit > count:
            return sine, cosine
        s, c = 2.0 * s * c, 1.0 - 2.0 * s * s


def geometry(chunk, need_slopes):
    vec = [chunk[k : k + 1] for k in range(3)]
    dist = jnp.sqrt(vec[0] * vec[0] + vec[1] * vec[1] + vec[2] * vec[2])
    inv = 1.0 / dist
    ux, uy, uz = (v * inv for v in vec)
    values = [
        jnp.ones_like(dist),
        ROOT3 * ux,
        ROOT3 * uy,
        ROOT3 * uz,
        ROOT15 * ux * uy,
        ROOT15 * uy * uz,
        0.5 * ROOT5 * (3.0 * uz * uz - 1.0),
        ROOT15 * ux * uz,
        0.5 * ROOT15 * (ux * ux - uy * uy),
    ]
    sine, cosine = multiples(dist, 8)
    scale = math.sqrt(2.0 / CUTOFF) * inv
    basis = sine * scale
    x = dist * (1.0 / CUTOFF)
    x2 = x * x
    x4 = x2 * x2
    envelope = 1.0 + x4 * x * (-21.0 + x * (35.0 - 15.0 * x))
    slopes = None
    if need_slopes:
        orders = (iota(sine.shape, 0) + 1).astype(F32) * (math.pi / CUTOFF)
        d_basis = orders * cosine * scale - basis * inv
        d_envelope = x4 * (-105.0 + x * (210.0 - 105.0 * x)) * (1.0 / CUTOFF)
        slopes = (d_basis, d_envelope)
    return inv, (ux, uy, uz), values, basis, envelope, slopes


def radial_hidden(basis, in_fw, mid_fw):
    z1 = dot(in_fw, stack_acts_f32(basis))
    z2 = dot(mid_fw, stack_acts(z1 * sigmoid(z1)))
    return z1, z2


def own_hot(chunk, own):
    target = chunk[3:4].astype(jnp.int32)
    return (iota((own, target.shape[1]), 0) == target).astype(F32).astype(BF16)


def scaled_hots(chunk, own, values):
    hot = own_hot(chunk, own)
    out = []
    for begin, size in SPANS:
        pairs = [split(values[m]) for m in range(begin, begin + size)]
        out.append(
            jnp.concatenate([hot * high for high, _ in pairs] + [hot * low for _, low in pairs], axis=0)
        )
    return out


def other_hot(chunk, own, total):
    atom = chunk[4:5].astype(jnp.int32)
    hot = (iota((own, atom.shape[1]), 0) == atom).astype(F32).astype(BF16)
    block = chunk[5:6]
    return jnp.concatenate(
        [hot * (block == float(b)).astype(F32).astype(BF16) for b in range(total // own)], axis=0
    )


def lanes_at(start, size):
    return pl.ds(pl.multiple_of(start, LANES), size)


def sweep(start, stop, body):
    start = lax.shift_left(lax.shift_right_arithmetic(start, 7), 7)
    for size in STEPS:
        rest = jnp.maximum(stop - start, 0)
        number = (rest + (STEPS[-1] if size != STEPS[-1] else size) - 1) // size

        def step(index, _, start=start, size=size):
            body(lanes_at(start + index * size, size), size)
            return 0

        lax.fori_loop(0, number, step, 0)
        start = start + number * size


def kind_columns(small, kinds, mix):
    mixed = dot_high(small[0:kinds, :], mix)
    return [mixed[k : k + 1].T for k in range(kinds)]


def kind_features(chunk, columns):
    kind = chunk[7:8]
    out = jnp.where(kind == 0.0, columns[0], 0.0)
    for index in range(1, len(columns)):
        out = out + jnp.where(kind == float(index), columns[index], 0.0)
    return out


def collect(amat, chunk, feat, values, envelope, z2, out_fw, own):
    width = feat.shape[0]
    units = z2 * sigmoid(z2) * (INV_COUNT * envelope)
    weights = dot(out_fw, stack_acts(units))
    hots = scaled_hots(chunk, own, values)
    for degree, (begin, size) in enumerate(SPANS):
        high, low = split(weights[degree * width : (degree + 1) * width] * feat)
        parts = dot(hots[degree], jnp.concatenate([high, low], axis=0), NT)
        rows = size * own
        at = slice(begin * own, (begin + size) * own)
        amat[at, :] += (parts[:rows, :width] + parts[:rows, width:]) + (
            parts[rows:, :width] + parts[rows:, width:]
        )


def node_forward(amat, features, update, own):
    parts = [amat[m * own : (m + 1) * own, :] for m in range(9)]
    inv1 = sum(p * p for p in parts[1:4])
    inv2 = sum(p * p for p in parts[4:9])
    preact = dot_high(jnp.concatenate([parts[0], inv1, inv2], axis=1), update)
    return features + preact * sigmoid(preact), preact


def node_back(amat, d_features, preact, update, own, d_amat):
    width = d_features.shape[1]
    gate = sigmoid(preact)
    d_pre = d_features * gate * (1.0 + preact * (1.0 - gate))
    d_inv = dot_high(d_pre, update, NT)
    for degree, (begin, size) in enumerate(SPANS):
        for m in range(begin, begin + size):
            value = d_inv[:, degree * width : (degree + 1) * width]
            if degree > 0:
                value = 2.0 * amat[m * own : (m + 1) * own, :] * value
            high, low = split_f32(value)
            turned = jnp.concatenate([high, low], axis=0).T
            d_amat[m * width : (m + 1) * width, :] = turned.astype(BF16)


def edge_backward(chunk, feat, hidden, own, in_fw, mid_fw, out_fw, in_bw, mid_bw, out_bw, d_amat):
    width = feat.shape[0]
    inv, unit, values, basis, envelope, (d_basis, d_envelope) = geometry(chunk, True)
    z1, z2 = radial_hidden(basis, in_fw, mid_fw) if hidden is None else hidden
    gate1, gate2 = sigmoid(z1), sigmoid(z2)
    scale = INV_COUNT * envelope
    units = z2 * gate2
    weights = dot(out_fw, stack_acts(units * scale))
    hot = own_hot(chunk, own)
    rows = dot(d_amat[...], jnp.concatenate([hot, hot], axis=0))
    pulled = []
    d_mixed = 0.0
    d_values = []
    for degree, (begin, size) in enumerate(SPANS):
        weight = weights[degree * width : (degree + 1) * width]
        product = weight * feat
        term = 0.0
        for m in range(begin, begin + size):
            row = rows[m * width : (m + 1) * width]
            if m == 0:
                term = row
                d_values.append(None)
                continue
            term = term + row * values[m]
            d_values.append(jnp.sum(row * product, axis=0, keepdims=True))
        d_mixed = d_mixed + weight * term
        pulled.append(feat * term)
    pulled = jnp.concatenate(pulled, axis=0)
    d_units = dot(out_bw, stack_three(pulled))
    d_env = INV_COUNT * jnp.sum(units * d_units, axis=0, keepdims=True)
    d_z2 = d_units * scale * gate2 * (1.0 + z2 * (1.0 - gate2))
    d_hidden = dot(mid_bw, stack_acts(d_z2))
    d_z1 = d_hidden * gate1 * (1.0 + z1 * (1.0 - gate1))
    d_b = dot(in_bw, stack_acts(d_z1))[0:8]
    d_dist = jnp.sum(d_b * d_basis, axis=0, keepdims=True) + d_env * d_envelope
    ux, uy, uz = unit
    y = d_values
    dux = ROOT3 * y[1] + ROOT15 * (uy * y[4] + uz * y[7] + ux * y[8])
    duy = ROOT3 * y[2] + ROOT15 * (ux * y[4] + uz * y[5] - uy * y[8])
    duz = ROOT3 * y[3] + ROOT15 * (uy * y[5] + ux * y[7]) + 3.0 * ROOT5 * uz * y[6]
    along = ux * dux + uy * duy + uz * duz
    grad = [(du - u * along) * inv + d_dist * u for u, du in zip(unit, (dux, duy, duz))]
    return grad, d_mixed


def first_sums(list_ref, start, stop, amat, columns, in_fw, mid_fw, out_fw, own):
    def body(at, _):
        chunk = list_ref[:, at]
        _, _, values, basis, envelope, _ = geometry(chunk, False)
        _, z2 = radial_hidden(basis, in_fw[0], mid_fw[0])
        feat = kind_features(chunk, columns)
        collect(amat, chunk, feat, values, envelope, z2, out_fw[0], own)

    sweep(start, stop, body)


def second_sums(list_ref, start, stop, amat, features_t, in_fw, mid_fw, out_fw, own, keep):
    total = features_t.shape[1]

    def body(at, _):
        chunk = list_ref[:, at]
        _, _, values, basis, envelope, _ = geometry(chunk, False)
        z1, z2 = radial_hidden(basis, in_fw[1], mid_fw[1])
        feat = gather(features_t, other_hot(chunk, own, total))
        if keep is not None:
            for kept, value in zip(keep, (feat, z1, z2)):
                kept[:, at] = value
        collect(amat, chunk, feat, values, envelope, z2, out_fw[1], own)

    sweep(start, stop, body)


def turn_features(features, features_t):
    high, low = split_f32(features.T)
    features_t[...] = jnp.concatenate([high, low], axis=0).astype(BF16)


def gather(features_t, hot):
    both = dot(features_t[...], hot)
    width = both.shape[0] // 2
    return both[:width] + both[width:]


def scatter_back(d_mixed_sum, hot, d_mixed):
    width = d_mixed.shape[0]
    high, low = split(d_mixed)
    both = dot(hot, jnp.concatenate([high, low], axis=0), NT)
    d_mixed_sum[...] += both[:, :width] + both[:, width:]


def rows_of(grad):
    return jnp.concatenate(grad + [jnp.zeros((5, grad[0].shape[1]), F32)], axis=0)


def split_three(pull):
    high, rest = split_f32(pull)
    middle, low = split_f32(rest)
    return jnp.concatenate([high, middle, low, jnp.zeros_like(low)], axis=0).astype(BF16)


def add_three(moved):
    return moved[0:8] + moved[8:16] + moved[16:24]


def inner_first_kernel(own, edges, kinds, *refs):
    (record, small, mix_ref, in_fw, mid_fw, out_fw, list_out, number_out, amat_out) = refs
    number = build_inner(own, edges, record, list_out)
    number_out[0] = number
    amat_out[...] = jnp.zeros_like(amat_out)
    columns = kind_columns(small, kinds, mix_ref[0])
    first_sums(list_out, 0, number, amat_out, columns, in_fw, mid_fw, out_fw, own)


def outer_first_kernel(hood, sections, own, edges, kinds, *refs):
    (
        got,
        inner_amat,
        small,
        mix_ref,
        update_ref,
        in_fw,
        mid_fw,
        out_fw,
        list_out,
        range_out,
        amat_out,
        preact_out,
        h_out,
        w_out,
        fields,
    ) = refs
    start, stop = build_outer(hood, sections, own, edges, got, list_out, fields)
    range_out[0] = start
    range_out[1] = stop
    amat_out[...] = inner_amat[...]
    columns = kind_columns(small, kinds, mix_ref[0])
    first_sums(list_out, start, stop, amat_out, columns, in_fw, mid_fw, out_fw, own)
    kind = got[5:6, 0:own].astype(jnp.int32)
    hot = (iota((8, own), 0) == kind).astype(F32).T
    rows = jnp.where(iota((8, small.shape[1]), 0) < kinds, small[...], 0.0)
    features = dot_high(hot, rows)
    h, preact = node_forward(amat_out, features, update_ref[0], own)
    preact_out[...] = preact
    h_out[...] = h
    w_out[...] = dot_high(h, mix_ref[1])


def inner_second_kernel(own, *refs):
    (number_ref, list_ref, w_ref, in_fw, mid_fw, out_fw, amat_out, features_t) = refs
    amat_out[...] = jnp.zeros_like(amat_out)
    turn_features(w_ref[...], features_t)
    second_sums(
        list_ref, 0, number_ref[0], amat_out, features_t, in_fw, mid_fw, out_fw, own, None
    )


def outer_second_kernel(count, own, kinds, *refs):
    (
        everyone_ref,
        range_ref,
        list_ref,
        inner_amat,
        h_ref,
        update_ref,
        small,
        in_fw,
        mid_fw,
        out_fw,
        in_bw,
        mid_bw,
        out_bw,
        energy_out,
        grad_out,
        d_mixed_sum,
        d_amat,
        features_t,
        amat,
        kept_feat,
        kept_first,
        kept_second,
    ) = refs
    total = count * own
    start, stop = range_ref[0], range_ref[1]
    turn_features(everyone_ref[...], features_t)
    amat[...] = inner_amat[...]
    d_mixed_sum[...] = jnp.zeros_like(d_mixed_sum)
    keep = (kept_feat, kept_first, kept_second)
    second_sums(list_ref, start, stop, amat, features_t, in_fw, mid_fw, out_fw, own, keep)
    h1 = h_ref[...]
    h2, preact = node_forward(amat, h1, update_ref[1], own)
    readout = small[kinds : kinds + 2, :]
    energy_out[...] = dot_high(readout[0:1], h1, NT) + dot_high(readout[1:2], h2, NT)
    d_features = jnp.broadcast_to(readout[1:2], h1.shape)
    node_back(amat, d_features, preact, update_ref[1], own, d_amat)
    weights = [ref[1] for ref in (in_fw, mid_fw, out_fw, in_bw, mid_bw, out_bw)]

    def backward(at, _):
        chunk = list_ref[:, at]
        hidden = (kept_first[:, at], kept_second[:, at])
        grad, d_mixed = edge_backward(chunk, kept_feat[:, at], hidden, own, *weights, d_amat)
        grad_out[:, at] = rows_of(grad)
        scatter_back(d_mixed_sum, other_hot(chunk, own, total), d_mixed)

    sweep(start, stop, backward)


def inner_second_back_kernel(own, *refs):
    (number_ref, list_ref, w_ref, d_amat) = refs[:4]
    weights = [ref[1] for ref in refs[4:10]]
    grad_out, d_mixed_sum, features_t = refs[10:]
    d_mixed_sum[...] = jnp.zeros_like(d_mixed_sum)
    turn_features(w_ref[...], features_t)

    def backward(at, _):
        chunk = list_ref[:, at]
        hot = other_hot(chunk, own, own)
        grad, d_mixed = edge_backward(
            chunk, gather(features_t, hot), None, own, *weights, d_amat
        )
        grad_out[:, at] = rows_of(grad)
        scatter_back(d_mixed_sum, hot, d_mixed)

    sweep(0, number_ref[0], backward)


def outer_first_back_kernel(count, own, kinds, *refs):
    (
        d_mixed_ref,
        inner_d_mixed,
        range_ref,
        list_ref,
        grad_ref,
        amat_ref,
        preact_ref,
        small,
        mix_ref,
        update_ref,
    ) = refs[:10]
    weights = [ref[0] for ref in refs[10:16]]
    force_out, d_amat, force = refs[16:]
    total = count * own
    columns = kind_columns(small, kinds, mix_ref[0])
    readout = small[kinds : kinds + 2, :]
    d_mixed = d_mixed_ref[...] + inner_d_mixed[...]
    d_features = readout[0:1] + readout[1:2] + dot_high(d_mixed, mix_ref[1], NT)
    node_back(amat_ref, d_features, preact_ref[...], update_ref[0], own, d_amat)
    force[...] = jnp.zeros_like(force)

    def backward(at, _):
        chunk = list_ref[:, at]
        feat = kind_features(chunk, columns)
        grad, _ = edge_backward(chunk, feat, None, own, *weights, d_amat)
        parts = split_three(rows_of(grad) + grad_ref[:, at])
        force[...] -= add_three(dot(parts, other_hot(chunk, own, total), NT))
        force[:, 0:own] += add_three(dot(parts, own_hot(chunk, own), NT))

    sweep(range_ref[0], range_ref[1], backward)
    for b in range(count):
        force_out[8 * b : 8 * b + 8, :] = force[:, b * own : (b + 1) * own]


def inner_first_back_kernel(own, kinds, *refs):
    (number_ref, list_ref, grad_ref, d_amat, small, mix_ref) = refs[:6]
    weights = [ref[0] for ref in refs[6:12]]
    force_out = refs[12]
    columns = kind_columns(small, kinds, mix_ref[0])
    force_out[...] = jnp.zeros_like(force_out)

    def backward(at, _):
        chunk = list_ref[:, at]
        feat = kind_features(chunk, columns)
        grad, _ = edge_backward(chunk, feat, None, own, *weights, d_amat)
        parts = split_three(rows_of(grad) + grad_ref[:, at])
        hot = own_hot(chunk, own) - other_hot(chunk, own, own)
        force_out[...] += add_three(dot(parts, hot, NT))

    sweep(0, number_ref[0], backward)


LIMIT = 48 * 1024 * 1024


def call(kernel, outs, scratch, args, smem_in=(), smem_out=(), micros=4):
    vmem = pl.BlockSpec(memory_space=pltpu.VMEM)
    smem = pl.BlockSpec(memory_space=pltpu.SMEM)
    return pl.pallas_call(
        kernel,
        out_shape=outs,
        in_specs=[smem if k in smem_in else vmem for k in range(len(args))],
        out_specs=[smem if k in smem_out else vmem for k in range(len(outs))],
        scratch_shapes=scratch,
        compiler_params=pltpu.CompilerParams(vmem_limit_bytes=LIMIT),
        cost_estimate=pl.CostEstimate(
            flops=micros * 1000 * 1000 * 1000, bytes_accessed=micros * 1000 * 1000, transcendentals=0
        ),
    )(*args)


def call_copying(kernel, outs, args, megabytes):
    vmem = pl.BlockSpec(memory_space=pltpu.VMEM)
    return pl.pallas_call(
        kernel,
        out_shape=outs,
        in_specs=[pl.BlockSpec(memory_space=pltpu.HBM)] * len(args),
        out_specs=[vmem] * len(outs),
        scratch_shapes=[pltpu.VMEM(value.shape, value.dtype) for value in args]
        + [pltpu.SemaphoreType.DMA((len(args),))],
        compiler_params=pltpu.CompilerParams(vmem_limit_bytes=megabytes * 1024 * 1024),
    )(*args)


def shards(
    sizes,
    species,
    send_x,
    send_y,
    send_z,
    edge_first,
    edge_second,
    edge_live,
    edge_vec,
    embed,
    radial_in,
    radial_mid,
    radial_out,
    mix,
    update,
    readout,
):
    hood = Neighbourhood(sizes)
    count = hood.count
    own = species.shape[0]
    width = embed.shape[1]
    layers = readout.shape[0]
    hidden = radial_mid.shape[1]
    slots = edge_first.shape[1]
    edges = round_up(slots, BLOCK)
    extra = edges - slots
    if extra:
        edge_first = jnp.pad(edge_first, ((0, 0), (0, extra)))
        edge_second = jnp.pad(edge_second, ((0, 0), (0, extra)))
        edge_live = jnp.pad(edge_live, ((0, 0), (0, extra)))
        edge_vec = jnp.pad(edge_vec, ((0, 0), (0, extra)), constant_values=1.0)
    faces = tuple(send.shape[2] for send in (send_z, send_y, send_x))
    sections = Sections(own, faces)
    shape = jax.ShapeDtypeStruct
    kinds = embed.shape[0]
    packed = call_copying(
        pack_kernel,
        [shape((8, edges), F32)],
        [species[None, :], send_x, send_y, send_z, edge_first, edge_second, edge_live, edge_vec],
        60,
    )[0]
    *weights, small = call_copying(
        prepare_kernel,
        [
            shape((layers, hidden, 32), BF16),
            shape((layers, hidden, 4 * hidden), BF16),
            shape((layers, 3 * width, 4 * hidden), BF16),
            shape((layers, 16, 4 * hidden), BF16),
            shape((layers, hidden, 4 * hidden), BF16),
            shape((layers, hidden, 9 * width), BF16),
            shape((8, width), F32),
        ],
        [radial_in, radial_mid, radial_out, embed, readout],
        16,
    )
    forward_weights = weights[:3]
    sums = shape((9 * own, width), F32)
    rows = shape((own, width), F32)
    turned = shape((9 * width, 2 * own), BF16)
    inner_size = round_up(2 * edges + LANES, STEPS[0]) + STEPS[0]
    outer_size = round_up((count + 1) * edges + LANES, STEPS[0]) + STEPS[0]

    got, along_x = hood.fetch(packed)
    inner_list, number, inner_amat = call(
        functools.partial(inner_first_kernel, own, edges, kinds),
        [shape((8, inner_size), F32), shape((1,), jnp.int32), sums],
        [],
        [along_x, small, mix] + forward_weights,
        smem_out=(1,),
    )
    outer_list, bounds, amat1, preact1, h1, w2 = call(
        functools.partial(outer_first_kernel, hood, sections, own, edges, kinds),
        [shape((8, outer_size), F32), shape((2,), jnp.int32), sums, rows, rows, rows],
        [pltpu.VMEM((6, round_up(count, 8), edges), F32)],
        [got, inner_amat, small, mix, update] + forward_weights,
        smem_out=(1,),
    )

    everyone, _ = hood.fetch(w2)
    (inner_amat,) = call(
        functools.partial(inner_second_kernel, own),
        [sums],
        [pltpu.VMEM((2 * width, own), BF16)],
        [number, inner_list, w2] + forward_weights,
        smem_in=(0,),
    )
    energies, grads, d_mixed, d_amat2 = call(
        functools.partial(outer_second_kernel, count, own, kinds),
        [shape((1, own), F32), shape((8, outer_size), F32), shape((count * own, width), F32), turned],
        [
            pltpu.VMEM((2 * width, count * own), BF16),
            pltpu.VMEM((9 * own, width), F32),
            pltpu.VMEM((width, outer_size), F32),
            pltpu.VMEM((hidden, outer_size), F32),
            pltpu.VMEM((hidden, outer_size), F32),
        ],
        [everyone, bounds, outer_list, inner_amat, h1, update, small] + weights,
        smem_in=(1,),
    )

    inner_grads, inner_d_mixed = call(
        functools.partial(inner_second_back_kernel, own),
        [shape((8, inner_size), F32), rows],
        [pltpu.VMEM((2 * width, own), BF16)],
        [number, inner_list, w2, d_amat2] + weights,
        smem_in=(0,),
    )
    d_mixed, inner_d_mixed = hood.give(d_mixed, inner_d_mixed)
    forces, d_amat1 = call(
        functools.partial(outer_first_back_kernel, count, own, kinds),
        [shape((8 * count, own), F32), turned],
        [pltpu.VMEM((8, count * own), F32)],
        [d_mixed, inner_d_mixed, bounds, outer_list, grads, amat1, preact1, small, mix, update]
        + weights,
        smem_in=(2,),
    )

    (inner_forces,) = call(
        functools.partial(inner_first_back_kernel, own, kinds),
        [shape((8, own), F32)],
        [],
        [number, inner_list, inner_grads, d_amat1, small, mix] + weights,
        smem_in=(0,),
    )
    forces, inner_forces = hood.give(forces, inner_forces)
    return (energies.reshape(own), forces[:3] + inner_forces[:3])


def solution(mesh):
    sizes = tuple(mesh.shape[axis] for axis in ("gx", "gy", "gz"))
    split_all = ("parts", "gx", "gy", "gz")
    return jax.shard_map(
        functools.partial(shards, sizes),
        mesh=mesh,
        in_specs=(
            P(split_all),
            P(split_all, None, None),
            P(split_all, None, None),
            P(split_all, None, None),
            P(split_all, None),
            P(split_all, None),
            P(split_all, None),
            P(None, split_all),
            P(),
            P(),
            P(),
            P(),
            P(),
            P(),
            P(),
        ),
        out_specs=(P(split_all), P(None, split_all)),
        check_vma=False,
    )
```

```python
import functools
import math

import jax
import jax.numpy as jnp
from jax import lax
from jax.experimental import pallas as pl
from jax.experimental.pallas import tpu as pltpu
from jax.sharding import PartitionSpec as P

HIGH = lax.Precision.HIGHEST
CUTOFF = 5.0
INV_COUNT = 0.2
ROOT3 = math.sqrt(3.0)
ROOT5 = math.sqrt(5.0)
ROOT15 = math.sqrt(15.0)
SPANS = ((0, 1), (1, 3), (4, 5))
LANES = 128
BLOCK = 256
STEPS = (1024, 512)
F32 = jnp.float32
BF16 = jnp.bfloat16
NT = (((1,), (1,)), ((), ()))
NN = (((1,), (0,)), ((), ()))


def round_up(value, unit):
    return -(-value // unit) * unit


def dot(left, right, dims=NN):
    return lax.dot_general(left, right, dims, preferred_element_type=F32)


def dot_high(left, right, dims=NN):
    return lax.dot_general(left, right, dims, preferred_element_type=F32, precision=HIGH)


def split(value):
    high = value.astype(BF16)
    return high, (value - high.astype(F32)).astype(BF16)


def split_f32(value):
    high = value.astype(BF16).astype(F32)
    return high, value - high


def stack_weights(value):
    high, low = split_f32(value)
    return jnp.concatenate([high, low, high, low], axis=0).T.astype(BF16)


def stack_acts(value):
    high, low = split(value)
    return jnp.concatenate([high, high, low, low], axis=0)


def stack_three(value):
    high, low = split(value)
    return jnp.concatenate([high, high, low], axis=0)


def stack_acts_f32(value):
    high, low = split_f32(value)
    return jnp.concatenate([high, high, low, low], axis=0).astype(BF16)


def iota(shape, dim):
    return lax.broadcasted_iota(jnp.int32, shape, dim)


def sigmoid(value):
    return 0.5 * jnp.tanh(0.5 * value) + 0.5


def axis_steps(size):
    return (0, 1, -1) if size > 2 else tuple(range(size))


class Neighbourhood:
    def __init__(self, sizes):
        self.sizes = sizes
        self.steps = [axis_steps(size) for size in sizes]
        self.shifts = [
            (dx, dy, dz) for dz in self.steps[2] for dy in self.steps[1] for dx in self.steps[0]
        ]
        self.place = {
            tuple(s % n for s, n in zip(shift, sizes)): b for b, shift in enumerate(self.shifts)
        }
        self.count = len(self.shifts)

    def block(self, *shift):
        return self.place.get(tuple(s % n for s, n in zip(shift, self.sizes)))

    def moved(self, rows, axis, step):
        size = self.sizes[axis]
        pairs = [(i, (i + step) % size) for i in range(size)]
        return lax.ppermute(rows, ("gx", "gy", "gz")[axis], pairs)

    def fetch(self, rows):
        along_x = None
        for axis in range(3):
            got = [rows] + [self.moved(rows, axis, -step) for step in self.steps[axis][1:]]
            if len(got) > 1:
                rows = jnp.concatenate(got, axis=0)
            if axis == 0:
                along_x = rows
        return rows, along_x

    def give(self, rows, beside):
        for axis in (2, 1, 0):
            if axis == 0:
                rows, beside = lax.optimization_barrier((rows, beside))
            steps = self.steps[axis]
            size = rows.shape[0] // len(steps)
            total = rows[:size]
            for index, step in enumerate(steps[1:], 1):
                total = total + self.moved(rows[index * size : (index + 1) * size], axis, step)
            rows = total
        return rows, beside


class Sections:
    def __init__(self, own, faces):
        sizes = [own] + [face for face in faces for _ in range(2)]
        self.starts, self.spots, self.widths = [], [], []
        start = spot = 0
        for size in sizes:
            self.starts.append(start)
            self.spots.append(spot)
            self.widths.append(round_up(size, LANES))
            start += size
            spot += self.widths[-1]
        self.z_end, self.y_end, self.x_end = self.spots[3], self.spots[5], spot

    def align(self, entry):
        out = entry
        for k in range(1, len(self.starts)):
            gap = (self.spots[k] - self.starts[k]) - (self.spots[k - 1] - self.starts[k - 1])
            out = out + jnp.where(entry >= self.starts[k], gap, 0)
        return out


def pack_kernel(*refs):
    given, out, held, sems = refs[:8], refs[8], refs[9:17], refs[17]
    copies = [
        pltpu.make_async_copy(source, target, sems.at[k])
        for k, (source, target) in enumerate(zip(given, held))
    ]
    for copy in copies:
        copy.start()
    out[...] = jnp.zeros_like(out)
    for copy in copies:
        copy.wait()
    species_ref, sx_ref, sy_ref, sz_ref, first_ref, second_ref, live_ref, vec_ref = held
    out[0:3, :] = vec_ref[...]
    out[3:4, :] = first_ref[...].astype(F32)
    out[4:5, :] = jnp.where(live_ref[...] > 0, second_ref[...], -1).astype(F32)
    own = species_ref.shape[1]
    out[5:6, 0:own] = species_ref[...].astype(F32)
    spot = round_up(own, LANES)
    for ref in (sz_ref, sy_ref, sx_ref):
        face = ref.shape[2]
        for side in range(2):
            out[5:6, spot : spot + face] = ref[0, 1 - side : 2 - side, :].astype(F32)
            spot += round_up(face, LANES)


ALONG_LANES = lax.GatherDimensionNumbers(
    offset_dims=(),
    collapsed_slice_dims=(1,),
    start_index_map=(1,),
    operand_batching_dims=(0,),
    start_indices_batching_dims=(0,),
)


def lookup(table, index):
    given = index.shape[0]
    rows = round_up(given, 8)
    if rows != given:
        index = jnp.broadcast_to(index[0:1], (rows, index.shape[1])) if given == 1 else jnp.concatenate(
            [index] + [index[0:1]] * (rows - given), axis=0
        )
        if table.shape[0] != 1:
            table = jnp.concatenate([table] + [table[0:1]] * (rows - given), axis=0)
    table = jnp.broadcast_to(table, (rows, table.shape[1]))
    parts = []
    for start in range(0, index.shape[1], LANES):
        at = index[:, start : start + LANES]
        low = jnp.bitwise_and(at, LANES - 1)
        tile = lax.shift_right_arithmetic(at, 7)
        out = None
        for k in range(table.shape[1] // LANES):
            found = lax.gather(
                table[:, k * LANES : (k + 1) * LANES],
                low[:, :, None],
                ALONG_LANES,
                slice_sizes=(1, 1),
                mode=lax.GatherScatterMode.PROMISE_IN_BOUNDS,
            )
            out = found if out is None else jnp.where(tile == k, found, out)
        parts.append(out)
    out = parts[0] if len(parts) == 1 else jnp.concatenate(parts, axis=1)
    return out[0:given]


def list_tables(hood, sections, own, got):
    def table(block, section):
        at = slice(sections.spots[section], sections.spots[section] + sections.widths[section])
        return got[8 * block + 5 : 8 * block + 6, at].astype(jnp.int32)

    lane = iota((1, sections.widths[0]), 1)
    z_lists = {}

    def z_list(dx, dy):
        block = hood.block(dx, dy, 0)
        if block not in z_lists:
            parts = [block * own + lane]
            for section, step in ((1, 1), (2, -1)):
                other = hood.block(dx, dy, step)
                parts.append(other * own + table(other, section))
            z_lists[block] = jnp.concatenate(parts, axis=1)
        return z_lists[block]

    y_lists = {}

    def y_list(dx):
        block = hood.block(dx, 0, 0)
        if block not in y_lists:
            parts = [z_list(dx, 0)]
            for section, step in ((3, 1), (4, -1)):
                entry = table(hood.block(dx, step, 0), section)
                parts.append(lookup(z_list(dx, step), sections.align(entry)))
            y_lists[block] = jnp.concatenate(parts, axis=1)
        return y_lists[block]

    parts = [y_list(0)]
    for section, step in ((5, 1), (6, -1)):
        entry = table(hood.block(step, 0, 0), section)
        parts.append(lookup(y_list(step), sections.align(entry)))
    mine = jnp.concatenate(parts, axis=1)

    def none(*which):
        return jnp.full((1, sum(sections.widths[k] for k in which)), -1, jnp.int32)

    z_back = {}
    for dz in hood.steps[2]:
        if dz == 0:
            z_back[dz] = jnp.concatenate([jnp.where(lane < own, lane, -1), none(1, 2)], axis=1)
        else:
            parts = [none(0)]
            for section, step in ((1, 1), (2, -1)):
                parts.append(table(0, section) if hood.block(0, 0, dz + step) == 0 else none(section))
            z_back[dz] = jnp.concatenate(parts, axis=1)
    y_back = {}
    for dz in hood.steps[2]:
        for dy in hood.steps[1]:
            if dy == 0:
                y_back[dy, dz] = jnp.concatenate([z_back[dz], none(3, 4)], axis=1)
                continue
            parts = [none(0, 1, 2)]
            for section, step in ((3, 1), (4, -1)):
                if (dy + step) % hood.sizes[1] == 0:
                    entry = table(hood.block(0, 0, dz), section)
                    parts.append(lookup(z_back[dz], sections.align(entry)))
                else:
                    parts.append(none(section))
            y_back[dy, dz] = jnp.concatenate(parts, axis=1)
    wanted = []
    for shift in hood.shifts:
        for section, step in ((5, 1), (6, -1)):
            if shift[0] != 0 and (shift[0] + step) % hood.sizes[0] == 0:
                wanted.append((shift, section))
    found = {}
    if wanted:
        entries = jnp.concatenate(
            [table(hood.block(0, dy, dz), section) for (_, dy, dz), section in wanted], axis=0
        )
        lists = jnp.concatenate([y_back[dy, dz] for (_, dy, dz), _ in wanted], axis=0)
        rows = lookup(lists, sections.align(entries))
        for number, key in enumerate(wanted):
            found[key] = rows[number : number + 1]
    back = []
    for shift in hood.shifts:
        if shift[0] == 0:
            back.append(jnp.concatenate([y_back[shift[1], shift[2]], none(5, 6)], axis=1))
        else:
            tail = [found.get((shift, section), none(section)) for section in (5, 6)]
            back.append(jnp.concatenate([none(0, 1, 2, 3, 4)] + tail, axis=1))
    return mine, back


def empty_edges(size):
    sub = iota((8, size), 0)
    return jnp.where(sub == 0, 1.0, jnp.where((sub >= 3) & (sub <= 5), -1.0, 0.0))


def fill_empty(list_out, start, stop):
    tile = empty_edges(LANES)
    last = (jnp.maximum(stop, start) + STEPS[0] + LANES - 1) // LANES

    def fill(step, _):
        list_out[:, pl.ds(pl.multiple_of(step * LANES, LANES), LANES)] = tile
        return 0

    lax.fori_loop(start // LANES, last, fill, 0)


def put(list_out, piece, to, size):
    lane = iota((1, LANES), 1)
    turn = jnp.bitwise_and(to, LANES - 1)
    piece = pltpu.roll(piece, turn, 1)
    low = lax.shift_right_arithmetic(to, 7)
    stop = turn + size
    for part in range(2):
        here = pl.ds(pl.multiple_of((low + part) * LANES, LANES), LANES)
        if part == 0:
            inside = (lane >= turn) & (lane < stop)
        else:
            inside = (lane < turn) & (lane < stop - LANES)
        list_out[:, here] = jnp.where(inside, piece, list_out[:, here])


def count_true(mask):
    return jnp.sum(mask.astype(F32)).astype(jnp.int32)


def build_inner(own, edges, record, list_out):
    second = record[4:5, :].astype(jnp.int32)
    inner = (second >= 0) & (second < own)
    number = count_true(inner)
    kinds = record[5:6, 0 : round_up(own, LANES)].astype(jnp.int32)
    kind_second = lookup(kinds, jnp.where(inner, second, 0)).astype(F32)
    kind_first = lookup(kinds, record[3:4, :].astype(jnp.int32)).astype(F32)
    zero = jnp.zeros((1, edges), F32)
    vec, first, other = record[0:3, :], record[3:4, :], record[4:5, :]
    forward = jnp.concatenate([vec, first, other, zero, zero, kind_second], axis=0)
    list_out[:, 0:edges] = jnp.where(inner, forward, empty_edges(edges))
    fill_empty(list_out, edges, 2 * number)
    reverse = jnp.concatenate([-vec, other, first, zero, zero, kind_first], axis=0)
    for start in range(0, edges, LANES):
        put(list_out, reverse[:, start : start + LANES], number + start, number - start)
    return 2 * number


def build_outer(hood, sections, own, edges, got, list_out, fields, sources):
    count = hood.count
    rows = round_up(count, 8)
    pad = rows - count
    mine, back = list_tables(hood, sections, own, got)

    def stacked(field):
        blocks = list(range(count)) + [0] * pad
        return jnp.concatenate([got[8 * b + field : 8 * b + field + 1, :] for b in blocks], axis=0)

    second = stacked(4).astype(jnp.int32)
    first = stacked(3).astype(jnp.int32)
    tables = jnp.concatenate([mine] + back[1:] + [mine] * pad, axis=0)
    found = lookup(tables, sections.align(jnp.maximum(second, 0)))
    row = iota((rows, edges), 0)
    chosen = (found >= 0) & (second >= 0) & (row < count) & (row > 0)
    kinds = jnp.concatenate(
        [got[8 * b + 5 : 8 * b + 6, 0 : sections.widths[0]] for b in range(count)]
        + [jnp.zeros((pad, sections.widths[0]), F32)] * (pad > 0),
        axis=0,
    ).astype(jnp.int32)
    kind = lookup(kinds, first)

    code = found[0:1]
    block = sum((code >= b * own).astype(jnp.int32) for b in range(1, count))
    atom = code - block * own
    others = lookup(kinds, jnp.broadcast_to(atom, (rows, edges)))
    other_kind = jnp.sum(jnp.where(row == block, others, 0).astype(F32), axis=0, keepdims=True)
    whole = jnp.concatenate(
        [
            got[0:4, :],
            atom.astype(F32),
            block.astype(F32),
            jnp.zeros((1, edges), F32),
            other_kind,
        ],
        axis=0,
    )
    list_out[:, 0:edges] = jnp.where(second[0:1] >= own, whole, empty_edges(edges))
    filled = count_true(second[0:1] >= 0)
    start = filled - count_true(second[0:1] >= own)

    before = (iota((BLOCK, BLOCK), 0) < iota((BLOCK, BLOCK), 1)).astype(F32).astype(BF16)
    taken = chosen.astype(F32)
    seen = jnp.zeros((rows, 1), F32)
    ranks = []
    for begin in range(0, edges, BLOCK):
        part = taken[:, begin : begin + BLOCK]
        ranks.append(dot(part.astype(BF16), before) + seen)
        seen = seen + jnp.sum(part, axis=1, keepdims=True)
    rank = jnp.concatenate(ranks, axis=1).astype(jnp.int32)
    bits = (edges - 1).bit_length()
    lanes = iota((rows, edges), 1)
    moving = jnp.where(chosen, lax.shift_left(lanes - rank, bits) + lanes, 0)
    for bit in range(bits):
        here = 1 << (bits + bit)
        shifted = pltpu.roll(moving, edges - (1 << bit), 1)
        stays = jnp.where(jnp.bitwise_and(moving, here) > 0, 0, moving)
        moving = jnp.where(jnp.bitwise_and(shifted, here) > 0, shifted, stays)
    sources[...] = jnp.minimum(jnp.bitwise_and(moving, (1 << bits) - 1), edges - 1)
    shift_own = (own - 1).bit_length()
    kind_bits = 8
    packed = lax.shift_left(lax.shift_left(found, shift_own) + first, kind_bits) + kind
    vectors = [stacked(k) for k in range(3)]

    def bring(at):
        source = sources[:, at]
        for k in range(3):
            fields[k, :, at] = -lookup(vectors[k], source)
        values = lookup(packed, source)
        fields[3, :, at] = lax.shift_right_logical(values, shift_own + kind_bits).astype(F32)
        fields[4, :, at] = jnp.bitwise_and(
            lax.shift_right_logical(values, kind_bits), (1 << shift_own) - 1
        ).astype(F32)
        fields[5, :, at] = jnp.bitwise_and(values, (1 << kind_bits) - 1).astype(F32)

    bring(slice(0, LANES))

    row1 = iota((rows, 1), 0)
    sizes = [
        jnp.sum(jnp.where(row1 == b, seen, 0.0)).astype(jnp.int32) for b in range(count)
    ]
    begins = [None]
    for size in sizes[1:]:
        begins.append(filled)
        filled = filled + size
    fill_empty(list_out, edges, filled)

    def place(b, tile):
        if isinstance(tile, int):
            at = slice(tile * LANES, (tile + 1) * LANES)
        else:
            at = pl.ds(pl.multiple_of(tile * LANES, LANES), LANES)
        piece = jnp.concatenate(
            [fields[k, b : b + 1, at] for k in range(5)]
            + [jnp.full((1, LANES), float(b), F32), jnp.zeros((1, LANES), F32)]
            + [fields[5, b : b + 1, at]],
            axis=0,
        )
        put(list_out, piece, begins[b] + tile * LANES, sizes[b] - tile * LANES)

    for b in range(1, count):
        place(b, 0)
    longest = functools.reduce(jnp.maximum, sizes[1:], jnp.int32(0))

    @pl.when(longest > LANES)
    def _():
        def bring_more(tile, _):
            bring(pl.ds(pl.multiple_of(tile * LANES, LANES), LANES))
            return 0

        lax.fori_loop(1, (longest + LANES - 1) // LANES, bring_more, 0)
        for b in range(1, count):

            def more(tile, _, b=b):
                place(b, tile)
                return 0

            lax.fori_loop(1, (sizes[b] + LANES - 1) // LANES, more, 0)

    return start, filled


def prepare_kernel(*refs):
    given, outs, held, sems = refs[:5], refs[5:12], refs[12:17], refs[17]
    copies = [
        pltpu.make_async_copy(source, target, sems.at[k])
        for k, (source, target) in enumerate(zip(given, held))
    ]
    for copy in copies:
        copy.start()
    for copy in copies:
        copy.wait()
    in_ref, mid_ref, out_ref, embed_ref, readout_ref = held
    rows = jnp.concatenate([embed_ref[...], readout_ref[...]], axis=0)
    small = outs[6]
    small[...] = jnp.zeros_like(small)
    small[0 : rows.shape[0], :] = rows
    for layer in range(in_ref.shape[0]):
        into = in_ref[layer]
        middle = mid_ref[layer]
        last = out_ref[layer]
        in_fw, mid_fw, out_fw, in_bw, mid_bw, out_bw = (out.at[layer] for out in outs[:6])
        in_fw[...] = stack_weights(into)
        mid_fw[...] = stack_weights(middle)
        out_fw[...] = stack_weights(last)
        into_t = jnp.concatenate([into, jnp.zeros_like(into)], axis=0).T
        in_bw[...] = stack_weights(into_t)
        mid_bw[...] = stack_weights(middle.T)
        high, low = split(last)
        out_bw[...] = jnp.concatenate([high, low, high], axis=1)


def multiples(dist, count):
    turn = dist * (math.pi / CUTOFF) - 0.5 * math.pi
    square = turn * turn
    high = 1.0 / math.factorial(15)
    sine_turn = -high * square + 1.0 / math.factorial(13)
    for order in (11, 9, 7, 5, 3, 1):
        sign = 1.0 if order % 4 == 1 else -1.0
        sine_turn = sine_turn * square + sign / math.factorial(order)
    cosine_turn = square * (1.0 / math.factorial(16)) - 1.0 / math.factorial(14)
    for order in (12, 10, 8, 6, 4, 2, 0):
        sign = 1.0 if order % 4 == 0 else -1.0
        cosine_turn = cosine_turn * square + sign / math.factorial(order)
    s, c = cosine_turn, -sine_turn * turn
    order = iota((count, dist.shape[1]), 0) + 1
    sine = jnp.zeros(order.shape, F32)
    cosine = jnp.ones(order.shape, F32)
    bit = 1
    while True:
        here = jnp.bitwise_and(order, bit) > 0
        more_s = sine * c + cosine * s
        more_c = cosine * c - sine * s
        sine = jnp.where(here, more_s, sine)
        cosine = jnp.where(here, more_c, cosine)
        bit *= 2
        if bit > count:
            return sine, cosine
        s, c = 2.0 * s * c, 1.0 - 2.0 * s * s


def geometry(chunk, need_slopes):
    vec = [chunk[k : k + 1] for k in range(3)]
    dist = jnp.sqrt(vec[0] * vec[0] + vec[1] * vec[1] + vec[2] * vec[2])
    inv = 1.0 / dist
    ux, uy, uz = (v * inv for v in vec)
    values = [
        jnp.ones_like(dist),
        ROOT3 * ux,
        ROOT3 * uy,
        ROOT3 * uz,
        ROOT15 * ux * uy,
        ROOT15 * uy * uz,
        0.5 * ROOT5 * (3.0 * uz * uz - 1.0),
        ROOT15 * ux * uz,
        0.5 * ROOT15 * (ux * ux - uy * uy),
    ]
    sine, cosine = multiples(dist, 8)
    scale = math.sqrt(2.0 / CUTOFF) * inv
    basis = sine * scale
    x = dist * (1.0 / CUTOFF)
    x2 = x * x
    x4 = x2 * x2
    envelope = 1.0 + x4 * x * (-21.0 + x * (35.0 - 15.0 * x))
    slopes = None
    if need_slopes:
        orders = (iota(sine.shape, 0) + 1).astype(F32) * (math.pi / CUTOFF)
        d_basis = orders * cosine * scale - basis * inv
        d_envelope = x4 * (-105.0 + x * (210.0 - 105.0 * x)) * (1.0 / CUTOFF)
        slopes = (d_basis, d_envelope)
    return inv, (ux, uy, uz), values, basis, envelope, slopes


def radial_hidden(basis, in_fw, mid_fw):
    z1 = dot(in_fw, stack_acts_f32(basis))
    z2 = dot(mid_fw, stack_acts(z1 * sigmoid(z1)))
    return z1, z2


def own_hot(chunk, own):
    target = chunk[3:4].astype(jnp.int32)
    return (iota((own, target.shape[1]), 0) == target).astype(F32).astype(BF16)


def scaled_hots(chunk, own, values):
    hot = own_hot(chunk, own)
    out = []
    for begin, size in SPANS:
        pairs = [split(values[m]) for m in range(begin, begin + size)]
        out.append(
            jnp.concatenate([hot * high for high, _ in pairs] + [hot * low for _, low in pairs], axis=0)
        )
    return out


def other_hot(chunk, own, total):
    atom = chunk[4:5].astype(jnp.int32)
    hot = (iota((own, atom.shape[1]), 0) == atom).astype(F32).astype(BF16)
    block = chunk[5:6]
    return jnp.concatenate(
        [hot * (block == float(b)).astype(F32).astype(BF16) for b in range(total // own)], axis=0
    )


def lanes_at(start, size):
    return pl.ds(pl.multiple_of(start, LANES), size)


def sweep(start, stop, body):
    start = lax.shift_left(lax.shift_right_arithmetic(start, 7), 7)
    for size in STEPS:
        rest = jnp.maximum(stop - start, 0)
        number = (rest + (STEPS[-1] if size != STEPS[-1] else size) - 1) // size

        def step(index, _, start=start, size=size):
            body(lanes_at(start + index * size, size), size)
            return 0

        lax.fori_loop(0, number, step, 0)
        start = start + number * size


def kind_columns(small, kinds, mix):
    mixed = dot_high(small[0:kinds, :], mix)
    return [mixed[k : k + 1].T for k in range(kinds)]


def kind_features(chunk, columns):
    kind = chunk[7:8]
    out = jnp.where(kind == 0.0, columns[0], 0.0)
    for index in range(1, len(columns)):
        out = out + jnp.where(kind == float(index), columns[index], 0.0)
    return out


def collect(amat, chunk, feat, values, envelope, z2, out_fw, own):
    width = feat.shape[0]
    units = z2 * sigmoid(z2) * (INV_COUNT * envelope)
    weights = dot(out_fw, stack_acts(units))
    hots = scaled_hots(chunk, own, values)
    for degree, (begin, size) in enumerate(SPANS):
        high, low = split(weights[degree * width : (degree + 1) * width] * feat)
        parts = dot(hots[degree], jnp.concatenate([high, low], axis=0), NT)
        rows = size * own
        at = slice(begin * own, (begin + size) * own)
        amat[at, :] += (parts[:rows, :width] + parts[:rows, width:]) + (
            parts[rows:, :width] + parts[rows:, width:]
        )


def node_forward(amat, features, update, own):
    parts = [amat[m * own : (m + 1) * own, :] for m in range(9)]
    inv1 = sum(p * p for p in parts[1:4])
    inv2 = sum(p * p for p in parts[4:9])
    preact = dot_high(jnp.concatenate([parts[0], inv1, inv2], axis=1), update)
    return features + preact * sigmoid(preact), preact


def node_back(amat, d_features, preact, update, own, d_amat):
    width = d_features.shape[1]
    gate = sigmoid(preact)
    d_pre = d_features * gate * (1.0 + preact * (1.0 - gate))
    d_inv = dot_high(d_pre, update, NT)
    for degree, (begin, size) in enumerate(SPANS):
        for m in range(begin, begin + size):
            value = d_inv[:, degree * width : (degree + 1) * width]
            if degree > 0:
                value = 2.0 * amat[m * own : (m + 1) * own, :] * value
            high, low = split_f32(value)
            turned = jnp.concatenate([high, low], axis=0).T
            d_amat[m * width : (m + 1) * width, :] = turned.astype(BF16)


def edge_backward(chunk, feat, hidden, own, in_fw, mid_fw, out_fw, in_bw, mid_bw, out_bw, d_amat):
    width = feat.shape[0]
    inv, unit, values, basis, envelope, (d_basis, d_envelope) = geometry(chunk, True)
    z1, z2 = radial_hidden(basis, in_fw, mid_fw) if hidden is None else hidden
    gate1, gate2 = sigmoid(z1), sigmoid(z2)
    scale = INV_COUNT * envelope
    units = z2 * gate2
    weights = dot(out_fw, stack_acts(units * scale))
    hot = own_hot(chunk, own)
    rows = dot(d_amat[...], jnp.concatenate([hot, hot], axis=0))
    pulled = []
    d_mixed = 0.0
    d_values = []
    for degree, (begin, size) in enumerate(SPANS):
        weight = weights[degree * width : (degree + 1) * width]
        product = weight * feat
        term = 0.0
        for m in range(begin, begin + size):
            row = rows[m * width : (m + 1) * width]
            if m == 0:
                term = row
                d_values.append(None)
                continue
            term = term + row * values[m]
            d_values.append(jnp.sum(row * product, axis=0, keepdims=True))
        d_mixed = d_mixed + weight * term
        pulled.append(feat * term)
    pulled = jnp.concatenate(pulled, axis=0)
    d_units = dot(out_bw, stack_three(pulled))
    d_env = INV_COUNT * jnp.sum(units * d_units, axis=0, keepdims=True)
    d_z2 = d_units * scale * gate2 * (1.0 + z2 * (1.0 - gate2))
    d_hidden = dot(mid_bw, stack_acts(d_z2))
    d_z1 = d_hidden * gate1 * (1.0 + z1 * (1.0 - gate1))
    d_b = dot(in_bw, stack_acts(d_z1))[0:8]
    d_dist = jnp.sum(d_b * d_basis, axis=0, keepdims=True) + d_env * d_envelope
    ux, uy, uz = unit
    y = d_values
    dux = ROOT3 * y[1] + ROOT15 * (uy * y[4] + uz * y[7] + ux * y[8])
    duy = ROOT3 * y[2] + ROOT15 * (ux * y[4] + uz * y[5] - uy * y[8])
    duz = ROOT3 * y[3] + ROOT15 * (uy * y[5] + ux * y[7]) + 3.0 * ROOT5 * uz * y[6]
    along = ux * dux + uy * duy + uz * duz
    grad = [(du - u * along) * inv + d_dist * u for u, du in zip(unit, (dux, duy, duz))]
    return grad, d_mixed


def first_sums(list_ref, start, stop, amat, columns, in_fw, mid_fw, out_fw, own):
    def body(at, _):
        chunk = list_ref[:, at]
        _, _, values, basis, envelope, _ = geometry(chunk, False)
        _, z2 = radial_hidden(basis, in_fw[0], mid_fw[0])
        feat = kind_features(chunk, columns)
        collect(amat, chunk, feat, values, envelope, z2, out_fw[0], own)

    sweep(start, stop, body)


def second_sums(list_ref, start, stop, amat, features_t, in_fw, mid_fw, out_fw, own, keep):
    total = features_t.shape[1]

    def body(at, _):
        chunk = list_ref[:, at]
        _, _, values, basis, envelope, _ = geometry(chunk, False)
        z1, z2 = radial_hidden(basis, in_fw[1], mid_fw[1])
        feat = gather(features_t, other_hot(chunk, own, total))
        if keep is not None:
            for kept, value in zip(keep, (feat, z1, z2)):
                kept[:, at] = value
        collect(amat, chunk, feat, values, envelope, z2, out_fw[1], own)

    sweep(start, stop, body)


def turn_features(features, features_t):
    high, low = split_f32(features.T)
    features_t[...] = jnp.concatenate([high, low], axis=0).astype(BF16)


def gather(features_t, hot):
    both = dot(features_t[...], hot)
    width = both.shape[0] // 2
    return both[:width] + both[width:]


def scatter_back(d_mixed_sum, hot, d_mixed):
    width = d_mixed.shape[0]
    high, low = split(d_mixed)
    both = dot(hot, jnp.concatenate([high, low], axis=0), NT)
    d_mixed_sum[...] += both[:, :width] + both[:, width:]


def rows_of(grad):
    return jnp.concatenate(grad + [jnp.zeros((5, grad[0].shape[1]), F32)], axis=0)


def split_three(pull):
    high, rest = split_f32(pull)
    middle, low = split_f32(rest)
    return jnp.concatenate([high, middle, low, jnp.zeros_like(low)], axis=0).astype(BF16)


def add_three(moved):
    return moved[0:8] + moved[8:16] + moved[16:24]


def inner_first_kernel(own, edges, kinds, *refs):
    (record, small, mix_ref, in_fw, mid_fw, out_fw, list_out, number_out, amat_out) = refs
    number = build_inner(own, edges, record, list_out)
    number_out[0] = number
    amat_out[...] = jnp.zeros_like(amat_out)
    columns = kind_columns(small, kinds, mix_ref[0])
    first_sums(list_out, 0, number, amat_out, columns, in_fw, mid_fw, out_fw, own)


def outer_first_kernel(hood, sections, own, edges, kinds, *refs):
    (
        got,
        inner_amat,
        small,
        mix_ref,
        update_ref,
        in_fw,
        mid_fw,
        out_fw,
        list_out,
        range_out,
        amat_out,
        preact_out,
        h_out,
        w_out,
        fields,
        sources,
    ) = refs
    start, stop = build_outer(hood, sections, own, edges, got, list_out, fields, sources)
    range_out[0] = start
    range_out[1] = stop
    amat_out[...] = inner_amat[...]
    columns = kind_columns(small, kinds, mix_ref[0])
    first_sums(list_out, start, stop, amat_out, columns, in_fw, mid_fw, out_fw, own)
    kind = got[5:6, 0:own].astype(jnp.int32)
    hot = (iota((8, own), 0) == kind).astype(F32).T
    rows = jnp.where(iota((8, small.shape[1]), 0) < kinds, small[...], 0.0)
    features = dot_high(hot, rows)
    h, preact = node_forward(amat_out, features, update_ref[0], own)
    preact_out[...] = preact
    h_out[...] = h
    w_out[...] = dot_high(h, mix_ref[1])


def inner_second_kernel(own, *refs):
    (number_ref, list_ref, w_ref, in_fw, mid_fw, out_fw, amat_out, features_t) = refs
    amat_out[...] = jnp.zeros_like(amat_out)
    turn_features(w_ref[...], features_t)
    second_sums(
        list_ref, 0, number_ref[0], amat_out, features_t, in_fw, mid_fw, out_fw, own, None
    )


def outer_second_kernel(count, own, kinds, *refs):
    (
        everyone_ref,
        range_ref,
        list_ref,
        inner_amat,
        h_ref,
        update_ref,
        small,
        in_fw,
        mid_fw,
        out_fw,
        in_bw,
        mid_bw,
        out_bw,
        energy_out,
        grad_out,
        d_mixed_sum,
        d_amat,
        features_t,
        amat,
        kept_feat,
        kept_first,
        kept_second,
    ) = refs
    total = count * own
    start, stop = range_ref[0], range_ref[1]
    turn_features(everyone_ref[...], features_t)
    amat[...] = inner_amat[...]
    d_mixed_sum[...] = jnp.zeros_like(d_mixed_sum)
    keep = (kept_feat, kept_first, kept_second)
    second_sums(list_ref, start, stop, amat, features_t, in_fw, mid_fw, out_fw, own, keep)
    h1 = h_ref[...]
    h2, preact = node_forward(amat, h1, update_ref[1], own)
    readout = small[kinds : kinds + 2, :]
    energy_out[...] = dot_high(readout[0:1], h1, NT) + dot_high(readout[1:2], h2, NT)
    d_features = jnp.broadcast_to(readout[1:2], h1.shape)
    node_back(amat, d_features, preact, update_ref[1], own, d_amat)
    weights = [ref[1] for ref in (in_fw, mid_fw, out_fw, in_bw, mid_bw, out_bw)]

    def backward(at, _):
        chunk = list_ref[:, at]
        hidden = (kept_first[:, at], kept_second[:, at])
        grad, d_mixed = edge_backward(chunk, kept_feat[:, at], hidden, own, *weights, d_amat)
        grad_out[:, at] = rows_of(grad)
        scatter_back(d_mixed_sum, other_hot(chunk, own, total), d_mixed)

    sweep(start, stop, backward)


def inner_second_back_kernel(own, *refs):
    (number_ref, list_ref, w_ref, d_amat) = refs[:4]
    weights = [ref[1] for ref in refs[4:10]]
    grad_out, d_mixed_sum, features_t = refs[10:]
    d_mixed_sum[...] = jnp.zeros_like(d_mixed_sum)
    turn_features(w_ref[...], features_t)

    def backward(at, _):
        chunk = list_ref[:, at]
        hot = other_hot(chunk, own, own)
        grad, d_mixed = edge_backward(
            chunk, gather(features_t, hot), None, own, *weights, d_amat
        )
        grad_out[:, at] = rows_of(grad)
        scatter_back(d_mixed_sum, hot, d_mixed)

    sweep(0, number_ref[0], backward)


def outer_first_back_kernel(count, own, kinds, *refs):
    (
        d_mixed_ref,
        inner_d_mixed,
        range_ref,
        list_ref,
        grad_ref,
        amat_ref,
        preact_ref,
        small,
        mix_ref,
        update_ref,
    ) = refs[:10]
    weights = [ref[0] for ref in refs[10:16]]
    force_out, d_amat, force = refs[16:]
    total = count * own
    columns = kind_columns(small, kinds, mix_ref[0])
    readout = small[kinds : kinds + 2, :]
    d_mixed = d_mixed_ref[...] + inner_d_mixed[...]
    d_features = readout[0:1] + readout[1:2] + dot_high(d_mixed, mix_ref[1], NT)
    node_back(amat_ref, d_features, preact_ref[...], update_ref[0], own, d_amat)
    force[...] = jnp.zeros_like(force)

    def backward(at, _):
        chunk = list_ref[:, at]
        feat = kind_features(chunk, columns)
        grad, _ = edge_backward(chunk, feat, None, own, *weights, d_amat)
        parts = split_three(rows_of(grad) + grad_ref[:, at])
        force[...] -= add_three(dot(parts, other_hot(chunk, own, total), NT))
        force[:, 0:own] += add_three(dot(parts, own_hot(chunk, own), NT))

    sweep(range_ref[0], range_ref[1], backward)
    for b in range(count):
        force_out[8 * b : 8 * b + 8, :] = force[:, b * own : (b + 1) * own]


def inner_first_back_kernel(own, kinds, *refs):
    (number_ref, list_ref, grad_ref, d_amat, small, mix_ref) = refs[:6]
    weights = [ref[0] for ref in refs[6:12]]
    force_out = refs[12]
    columns = kind_columns(small, kinds, mix_ref[0])
    force_out[...] = jnp.zeros_like(force_out)

    def backward(at, _):
        chunk = list_ref[:, at]
        feat = kind_features(chunk, columns)
        grad, _ = edge_backward(chunk, feat, None, own, *weights, d_amat)
        parts = split_three(rows_of(grad) + grad_ref[:, at])
        hot = own_hot(chunk, own) - other_hot(chunk, own, own)
        force_out[...] += add_three(dot(parts, hot, NT))

    sweep(0, number_ref[0], backward)


LIMIT = 48 * 1024 * 1024


def call(kernel, outs, scratch, args, smem_in=(), smem_out=(), micros=4):
    vmem = pl.BlockSpec(memory_space=pltpu.VMEM)
    smem = pl.BlockSpec(memory_space=pltpu.SMEM)
    return pl.pallas_call(
        kernel,
        out_shape=outs,
        in_specs=[smem if k in smem_in else vmem for k in range(len(args))],
        out_specs=[smem if k in smem_out else vmem for k in range(len(outs))],
        scratch_shapes=scratch,
        compiler_params=pltpu.CompilerParams(vmem_limit_bytes=LIMIT),
        cost_estimate=pl.CostEstimate(
            flops=micros * 1000 * 1000 * 1000, bytes_accessed=micros * 1000 * 1000, transcendentals=0
        ),
    )(*args)


def call_copying(kernel, outs, args, megabytes):
    vmem = pl.BlockSpec(memory_space=pltpu.VMEM)
    return pl.pallas_call(
        kernel,
        out_shape=outs,
        in_specs=[pl.BlockSpec(memory_space=pltpu.HBM)] * len(args),
        out_specs=[vmem] * len(outs),
        scratch_shapes=[pltpu.VMEM(value.shape, value.dtype) for value in args]
        + [pltpu.SemaphoreType.DMA((len(args),))],
        compiler_params=pltpu.CompilerParams(vmem_limit_bytes=megabytes * 1024 * 1024),
    )(*args)


def shards(
    sizes,
    species,
    send_x,
    send_y,
    send_z,
    edge_first,
    edge_second,
    edge_live,
    edge_vec,
    embed,
    radial_in,
    radial_mid,
    radial_out,
    mix,
    update,
    readout,
):
    hood = Neighbourhood(sizes)
    count = hood.count
    own = species.shape[0]
    width = embed.shape[1]
    layers = readout.shape[0]
    hidden = radial_mid.shape[1]
    slots = edge_first.shape[1]
    edges = round_up(slots, BLOCK)
    extra = edges - slots
    if extra:
        edge_first = jnp.pad(edge_first, ((0, 0), (0, extra)))
        edge_second = jnp.pad(edge_second, ((0, 0), (0, extra)))
        edge_live = jnp.pad(edge_live, ((0, 0), (0, extra)))
        edge_vec = jnp.pad(edge_vec, ((0, 0), (0, extra)), constant_values=1.0)
    faces = tuple(send.shape[2] for send in (send_z, send_y, send_x))
    sections = Sections(own, faces)
    shape = jax.ShapeDtypeStruct
    kinds = embed.shape[0]
    packed = call_copying(
        pack_kernel,
        [shape((8, edges), F32)],
        [species[None, :], send_x, send_y, send_z, edge_first, edge_second, edge_live, edge_vec],
        60,
    )[0]
    *weights, small = call_copying(
        prepare_kernel,
        [
            shape((layers, hidden, 32), BF16),
            shape((layers, hidden, 4 * hidden), BF16),
            shape((layers, 3 * width, 4 * hidden), BF16),
            shape((layers, 16, 4 * hidden), BF16),
            shape((layers, hidden, 4 * hidden), BF16),
            shape((layers, hidden, 9 * width), BF16),
            shape((8, width), F32),
        ],
        [radial_in, radial_mid, radial_out, embed, readout],
        16,
    )
    forward_weights = weights[:3]
    sums = shape((9 * own, width), F32)
    rows = shape((own, width), F32)
    turned = shape((9 * width, 2 * own), BF16)
    inner_size = round_up(2 * edges + LANES, STEPS[0]) + STEPS[0]
    outer_size = round_up((count + 1) * edges + LANES, STEPS[0]) + STEPS[0]

    got, along_x = hood.fetch(packed)
    inner_list, number, inner_amat = call(
        functools.partial(inner_first_kernel, own, edges, kinds),
        [shape((8, inner_size), F32), shape((1,), jnp.int32), sums],
        [],
        [along_x, small, mix] + forward_weights,
        smem_out=(1,),
    )
    outer_list, bounds, amat1, preact1, h1, w2 = call(
        functools.partial(outer_first_kernel, hood, sections, own, edges, kinds),
        [shape((8, outer_size), F32), shape((2,), jnp.int32), sums, rows, rows, rows],
        [
            pltpu.VMEM((6, round_up(count, 8), edges), F32),
            pltpu.VMEM((round_up(count, 8), edges), jnp.int32),
        ],
        [got, inner_amat, small, mix, update] + forward_weights,
        smem_out=(1,),
    )

    everyone, _ = hood.fetch(w2)
    (inner_amat,) = call(
        functools.partial(inner_second_kernel, own),
        [sums],
        [pltpu.VMEM((2 * width, own), BF16)],
        [number, inner_list, w2] + forward_weights,
        smem_in=(0,),
    )
    energies, grads, d_mixed, d_amat2 = call(
        functools.partial(outer_second_kernel, count, own, kinds),
        [shape((1, own), F32), shape((8, outer_size), F32), shape((count * own, width), F32), turned],
        [
            pltpu.VMEM((2 * width, count * own), BF16),
            pltpu.VMEM((9 * own, width), F32),
            pltpu.VMEM((width, outer_size), F32),
            pltpu.VMEM((hidden, outer_size), F32),
            pltpu.VMEM((hidden, outer_size), F32),
        ],
        [everyone, bounds, outer_list, inner_amat, h1, update, small] + weights,
        smem_in=(1,),
    )

    inner_grads, inner_d_mixed = call(
        functools.partial(inner_second_back_kernel, own),
        [shape((8, inner_size), F32), rows],
        [pltpu.VMEM((2 * width, own), BF16)],
        [number, inner_list, w2, d_amat2] + weights,
        smem_in=(0,),
    )
    d_mixed, inner_d_mixed = hood.give(d_mixed, inner_d_mixed)
    forces, d_amat1 = call(
        functools.partial(outer_first_back_kernel, count, own, kinds),
        [shape((8 * count, own), F32), turned],
        [pltpu.VMEM((8, count * own), F32)],
        [d_mixed, inner_d_mixed, bounds, outer_list, grads, amat1, preact1, small, mix, update]
        + weights,
        smem_in=(2,),
    )

    (inner_forces,) = call(
        functools.partial(inner_first_back_kernel, own, kinds),
        [shape((8, own), F32)],
        [],
        [number, inner_list, inner_grads, d_amat1, small, mix] + weights,
        smem_in=(0,),
    )
    forces, inner_forces = hood.give(forces, inner_forces)
    return (energies.reshape(own), forces[:3] + inner_forces[:3])


def solution(mesh):
    sizes = tuple(mesh.shape[axis] for axis in ("gx", "gy", "gz"))
    split_all = ("parts", "gx", "gy", "gz")
    return jax.shard_map(
        functools.partial(shards, sizes),
        mesh=mesh,
        in_specs=(
            P(split_all),
            P(split_all, None, None),
            P(split_all, None, None),
            P(split_all, None, None),
            P(split_all, None),
            P(split_all, None),
            P(split_all, None),
            P(None, split_all),
            P(),
            P(),
            P(),
            P(),
            P(),
            P(),
            P(),
        ),
        out_specs=(P(split_all), P(None, split_all)),
        check_vma=False,
    )
```

```python
import functools
import math

import jax
import jax.numpy as jnp
from jax import lax
from jax.experimental import pallas as pl
from jax.experimental.pallas import tpu as pltpu
from jax.sharding import PartitionSpec as P

HIGH = lax.Precision.HIGHEST
CUTOFF = 5.0
INV_COUNT = 0.2
ROOT3 = math.sqrt(3.0)
ROOT5 = math.sqrt(5.0)
ROOT15 = math.sqrt(15.0)
SPANS = ((0, 1), (1, 3), (4, 5))
LANES = 128
BLOCK = 256
STEPS = (1536, 512)
F32 = jnp.float32
BF16 = jnp.bfloat16
NT = (((1,), (1,)), ((), ()))
NN = (((1,), (0,)), ((), ()))


def round_up(value, unit):
    return -(-value // unit) * unit


def dot(left, right, dims=NN):
    return lax.dot_general(left, right, dims, preferred_element_type=F32)


def dot_high(left, right, dims=NN):
    return lax.dot_general(left, right, dims, preferred_element_type=F32, precision=HIGH)


def split(value):
    high = value.astype(BF16)
    return high, (value - high.astype(F32)).astype(BF16)


def split_f32(value):
    high = value.astype(BF16).astype(F32)
    return high, value - high


def stack_weights(value):
    high, low = split_f32(value)
    return jnp.concatenate([high, low, high, low], axis=0).T.astype(BF16)


def stack_acts(value):
    high, low = split(value)
    return jnp.concatenate([high, high, low, low], axis=0)


def stack_three(value):
    high, low = split(value)
    return jnp.concatenate([high, high, low], axis=0)


def stack_acts_f32(value):
    high, low = split_f32(value)
    return jnp.concatenate([high, high, low, low], axis=0).astype(BF16)


def iota(shape, dim):
    return lax.broadcasted_iota(jnp.int32, shape, dim)


def sigmoid(value):
    return 0.5 * jnp.tanh(0.5 * value) + 0.5


def axis_steps(size):
    return (0, 1, -1) if size > 2 else tuple(range(size))


class Neighbourhood:
    def __init__(self, sizes):
        self.sizes = sizes
        self.steps = [axis_steps(size) for size in sizes]
        self.shifts = [
            (dx, dy, dz) for dz in self.steps[2] for dy in self.steps[1] for dx in self.steps[0]
        ]
        self.place = {
            tuple(s % n for s, n in zip(shift, sizes)): b for b, shift in enumerate(self.shifts)
        }
        self.count = len(self.shifts)

    def block(self, *shift):
        return self.place.get(tuple(s % n for s, n in zip(shift, self.sizes)))

    def moved(self, rows, axis, step):
        size = self.sizes[axis]
        pairs = [(i, (i + step) % size) for i in range(size)]
        return lax.ppermute(rows, ("gx", "gy", "gz")[axis], pairs)

    def fetch(self, rows):
        along_x = None
        for axis in range(3):
            got = [rows] + [self.moved(rows, axis, -step) for step in self.steps[axis][1:]]
            if len(got) > 1:
                rows = jnp.concatenate(got, axis=0)
            if axis == 0:
                along_x = rows
        return rows, along_x

    def give(self, rows, beside):
        for axis in (2, 1, 0):
            if axis == 0:
                rows, beside = lax.optimization_barrier((rows, beside))
            steps = self.steps[axis]
            size = rows.shape[0] // len(steps)
            total = rows[:size]
            for index, step in enumerate(steps[1:], 1):
                total = total + self.moved(rows[index * size : (index + 1) * size], axis, step)
            rows = total
        return rows, beside


class Sections:
    def __init__(self, own, faces):
        sizes = [own] + [face for face in faces for _ in range(2)]
        self.starts, self.spots, self.widths = [], [], []
        start = spot = 0
        for size in sizes:
            self.starts.append(start)
            self.spots.append(spot)
            self.widths.append(round_up(size, LANES))
            start += size
            spot += self.widths[-1]
        self.z_end, self.y_end, self.x_end = self.spots[3], self.spots[5], spot

    def align(self, entry):
        out = entry
        for k in range(1, len(self.starts)):
            gap = (self.spots[k] - self.starts[k]) - (self.spots[k - 1] - self.starts[k - 1])
            out = out + jnp.where(entry >= self.starts[k], gap, 0)
        return out


def pack_kernel(*refs):
    given, out, held, sems = refs[:8], refs[8], refs[9:17], refs[17]
    copies = [
        pltpu.make_async_copy(source, target, sems.at[k])
        for k, (source, target) in enumerate(zip(given, held))
    ]
    for copy in copies:
        copy.start()
    out[...] = jnp.zeros_like(out)
    for copy in copies:
        copy.wait()
    species_ref, sx_ref, sy_ref, sz_ref, first_ref, second_ref, live_ref, vec_ref = held
    out[0:3, :] = vec_ref[...]
    out[3:4, :] = first_ref[...].astype(F32)
    out[4:5, :] = jnp.where(live_ref[...] > 0, second_ref[...], -1).astype(F32)
    own = species_ref.shape[1]
    out[5:6, 0:own] = species_ref[...].astype(F32)
    spot = round_up(own, LANES)
    for ref in (sz_ref, sy_ref, sx_ref):
        face = ref.shape[2]
        for side in range(2):
            out[5:6, spot : spot + face] = ref[0, 1 - side : 2 - side, :].astype(F32)
            spot += round_up(face, LANES)


ALONG_LANES = lax.GatherDimensionNumbers(
    offset_dims=(),
    collapsed_slice_dims=(1,),
    start_index_map=(1,),
    operand_batching_dims=(0,),
    start_indices_batching_dims=(0,),
)


def lookup(table, index):
    given = index.shape[0]
    rows = round_up(given, 8)
    if rows != given:
        index = jnp.broadcast_to(index[0:1], (rows, index.shape[1])) if given == 1 else jnp.concatenate(
            [index] + [index[0:1]] * (rows - given), axis=0
        )
        if table.shape[0] != 1:
            table = jnp.concatenate([table] + [table[0:1]] * (rows - given), axis=0)
    table = jnp.broadcast_to(table, (rows, table.shape[1]))
    parts = []
    for start in range(0, index.shape[1], LANES):
        at = index[:, start : start + LANES]
        low = jnp.bitwise_and(at, LANES - 1)
        tile = lax.shift_right_arithmetic(at, 7)
        out = None
        for k in range(table.shape[1] // LANES):
            found = lax.gather(
                table[:, k * LANES : (k + 1) * LANES],
                low[:, :, None],
                ALONG_LANES,
                slice_sizes=(1, 1),
                mode=lax.GatherScatterMode.PROMISE_IN_BOUNDS,
            )
            out = found if out is None else jnp.where(tile == k, found, out)
        parts.append(out)
    out = parts[0] if len(parts) == 1 else jnp.concatenate(parts, axis=1)
    return out[0:given]


def list_tables(hood, sections, own, got):
    def table(block, section):
        at = slice(sections.spots[section], sections.spots[section] + sections.widths[section])
        return got[8 * block + 5 : 8 * block + 6, at].astype(jnp.int32)

    lane = iota((1, sections.widths[0]), 1)
    z_lists = {}

    def z_list(dx, dy):
        block = hood.block(dx, dy, 0)
        if block not in z_lists:
            parts = [block * own + lane]
            for section, step in ((1, 1), (2, -1)):
                other = hood.block(dx, dy, step)
                parts.append(other * own + table(other, section))
            z_lists[block] = jnp.concatenate(parts, axis=1)
        return z_lists[block]

    y_lists = {}

    def y_list(dx):
        block = hood.block(dx, 0, 0)
        if block not in y_lists:
            parts = [z_list(dx, 0)]
            for section, step in ((3, 1), (4, -1)):
                entry = table(hood.block(dx, step, 0), section)
                parts.append(lookup(z_list(dx, step), sections.align(entry)))
            y_lists[block] = jnp.concatenate(parts, axis=1)
        return y_lists[block]

    parts = [y_list(0)]
    for section, step in ((5, 1), (6, -1)):
        entry = table(hood.block(step, 0, 0), section)
        parts.append(lookup(y_list(step), sections.align(entry)))
    mine = jnp.concatenate(parts, axis=1)

    def none(*which):
        return jnp.full((1, sum(sections.widths[k] for k in which)), -1, jnp.int32)

    z_back = {}
    for dz in hood.steps[2]:
        if dz == 0:
            z_back[dz] = jnp.concatenate([jnp.where(lane < own, lane, -1), none(1, 2)], axis=1)
        else:
            parts = [none(0)]
            for section, step in ((1, 1), (2, -1)):
                parts.append(table(0, section) if hood.block(0, 0, dz + step) == 0 else none(section))
            z_back[dz] = jnp.concatenate(parts, axis=1)
    y_back = {}
    for dz in hood.steps[2]:
        for dy in hood.steps[1]:
            if dy == 0:
                y_back[dy, dz] = jnp.concatenate([z_back[dz], none(3, 4)], axis=1)
                continue
            parts = [none(0, 1, 2)]
            for section, step in ((3, 1), (4, -1)):
                if (dy + step) % hood.sizes[1] == 0:
                    entry = table(hood.block(0, 0, dz), section)
                    parts.append(lookup(z_back[dz], sections.align(entry)))
                else:
                    parts.append(none(section))
            y_back[dy, dz] = jnp.concatenate(parts, axis=1)
    wanted = []
    for shift in hood.shifts:
        for section, step in ((5, 1), (6, -1)):
            if shift[0] != 0 and (shift[0] + step) % hood.sizes[0] == 0:
                wanted.append((shift, section))
    found = {}
    if wanted:
        entries = jnp.concatenate(
            [table(hood.block(0, dy, dz), section) for (_, dy, dz), section in wanted], axis=0
        )
        lists = jnp.concatenate([y_back[dy, dz] for (_, dy, dz), _ in wanted], axis=0)
        rows = lookup(lists, sections.align(entries))
        for number, key in enumerate(wanted):
            found[key] = rows[number : number + 1]
    back = []
    for shift in hood.shifts:
        if shift[0] == 0:
            back.append(jnp.concatenate([y_back[shift[1], shift[2]], none(5, 6)], axis=1))
        else:
            tail = [found.get((shift, section), none(section)) for section in (5, 6)]
            back.append(jnp.concatenate([none(0, 1, 2, 3, 4)] + tail, axis=1))
    return mine, back


def empty_edges(size):
    sub = iota((8, size), 0)
    return jnp.where(sub == 0, 1.0, jnp.where((sub >= 3) & (sub <= 5), -1.0, 0.0))


def fill_empty(list_out, start, stop):
    tile = empty_edges(LANES)
    last = (jnp.maximum(stop, start) + STEPS[0] + LANES - 1) // LANES

    def fill(step, _):
        list_out[:, pl.ds(pl.multiple_of(step * LANES, LANES), LANES)] = tile
        return 0

    lax.fori_loop(start // LANES, last, fill, 0)


def put(list_out, piece, to, size):
    lane = iota((1, LANES), 1)
    turn = jnp.bitwise_and(to, LANES - 1)
    piece = pltpu.roll(piece, turn, 1)
    low = lax.shift_right_arithmetic(to, 7)
    stop = turn + size
    for part in range(2):
        here = pl.ds(pl.multiple_of((low + part) * LANES, LANES), LANES)
        if part == 0:
            inside = (lane >= turn) & (lane < stop)
        else:
            inside = (lane < turn) & (lane < stop - LANES)
        list_out[:, here] = jnp.where(inside, piece, list_out[:, here])


def count_true(mask):
    return jnp.sum(mask.astype(F32)).astype(jnp.int32)


def build_inner(own, edges, record, list_out):
    second = record[4:5, :].astype(jnp.int32)
    inner = (second >= 0) & (second < own)
    number = count_true(inner)
    kinds = record[5:6, 0 : round_up(own, LANES)].astype(jnp.int32)
    kind_second = lookup(kinds, jnp.where(inner, second, 0)).astype(F32)
    kind_first = lookup(kinds, record[3:4, :].astype(jnp.int32)).astype(F32)
    zero = jnp.zeros((1, edges), F32)
    vec, first, other = record[0:3, :], record[3:4, :], record[4:5, :]
    forward = jnp.concatenate([vec, first, other, zero, zero, kind_second], axis=0)
    list_out[:, 0:edges] = jnp.where(inner, forward, empty_edges(edges))
    fill_empty(list_out, edges, 2 * number)
    reverse = jnp.concatenate([-vec, other, first, zero, zero, kind_first], axis=0)
    for start in range(0, edges, LANES):
        put(list_out, reverse[:, start : start + LANES], number + start, number - start)
    return 2 * number


def build_outer(hood, sections, own, edges, got, list_out, fields, sources):
    count = hood.count
    rows = round_up(count, 8)
    pad = rows - count
    mine, back = list_tables(hood, sections, own, got)

    def stacked(field):
        blocks = list(range(count)) + [0] * pad
        return jnp.concatenate([got[8 * b + field : 8 * b + field + 1, :] for b in blocks], axis=0)

    second = stacked(4).astype(jnp.int32)
    first = stacked(3).astype(jnp.int32)
    tables = jnp.concatenate([mine] + back[1:] + [mine] * pad, axis=0)
    found = lookup(tables, sections.align(jnp.maximum(second, 0)))
    row = iota((rows, edges), 0)
    chosen = (found >= 0) & (second >= 0) & (row < count) & (row > 0)
    kinds = jnp.concatenate(
        [got[8 * b + 5 : 8 * b + 6, 0 : sections.widths[0]] for b in range(count)]
        + [jnp.zeros((pad, sections.widths[0]), F32)] * (pad > 0),
        axis=0,
    ).astype(jnp.int32)
    kind = lookup(kinds, first)

    code = found[0:1]
    block = sum((code >= b * own).astype(jnp.int32) for b in range(1, count))
    atom = code - block * own
    others = lookup(kinds, jnp.broadcast_to(atom, (rows, edges)))
    other_kind = jnp.sum(jnp.where(row == block, others, 0).astype(F32), axis=0, keepdims=True)
    whole = jnp.concatenate(
        [
            got[0:4, :],
            atom.astype(F32),
            block.astype(F32),
            jnp.zeros((1, edges), F32),
            other_kind,
        ],
        axis=0,
    )
    list_out[:, 0:edges] = jnp.where(second[0:1] >= own, whole, empty_edges(edges))
    filled = count_true(second[0:1] >= 0)
    start = filled - count_true(second[0:1] >= own)

    before = (iota((BLOCK, BLOCK), 0) < iota((BLOCK, BLOCK), 1)).astype(F32).astype(BF16)
    taken = chosen.astype(F32)
    seen = jnp.zeros((rows, 1), F32)
    ranks = []
    for begin in range(0, edges, BLOCK):
        part = taken[:, begin : begin + BLOCK]
        ranks.append(dot(part.astype(BF16), before) + seen)
        seen = seen + jnp.sum(part, axis=1, keepdims=True)
    rank = jnp.concatenate(ranks, axis=1).astype(jnp.int32)
    bits = (edges - 1).bit_length()
    lanes = iota((rows, edges), 1)
    moving = jnp.where(chosen, lax.shift_left(lanes - rank, bits) + lanes, 0)
    for bit in range(bits):
        here = 1 << (bits + bit)
        shifted = pltpu.roll(moving, edges - (1 << bit), 1)
        stays = jnp.where(jnp.bitwise_and(moving, here) > 0, 0, moving)
        moving = jnp.where(jnp.bitwise_and(shifted, here) > 0, shifted, stays)
    sources[...] = jnp.minimum(jnp.bitwise_and(moving, (1 << bits) - 1), edges - 1)
    shift_own = (own - 1).bit_length()
    kind_bits = 8
    packed = lax.shift_left(lax.shift_left(found, shift_own) + first, kind_bits) + kind
    vectors = [stacked(k) for k in range(3)]

    def bring(at):
        source = sources[:, at]
        for k in range(3):
            fields[k, :, at] = -lookup(vectors[k], source)
        values = lookup(packed, source)
        fields[3, :, at] = lax.shift_right_logical(values, shift_own + kind_bits).astype(F32)
        fields[4, :, at] = jnp.bitwise_and(
            lax.shift_right_logical(values, kind_bits), (1 << shift_own) - 1
        ).astype(F32)
        fields[5, :, at] = jnp.bitwise_and(values, (1 << kind_bits) - 1).astype(F32)

    bring(slice(0, LANES))

    row1 = iota((rows, 1), 0)
    sizes = [
        jnp.sum(jnp.where(row1 == b, seen, 0.0)).astype(jnp.int32) for b in range(count)
    ]
    begins = [None]
    for size in sizes[1:]:
        begins.append(filled)
        filled = filled + size
    fill_empty(list_out, edges, filled)

    def place(b, tile):
        if isinstance(tile, int):
            at = slice(tile * LANES, (tile + 1) * LANES)
        else:
            at = pl.ds(pl.multiple_of(tile * LANES, LANES), LANES)
        piece = jnp.concatenate(
            [fields[k, b : b + 1, at] for k in range(5)]
            + [jnp.full((1, LANES), float(b), F32), jnp.zeros((1, LANES), F32)]
            + [fields[5, b : b + 1, at]],
            axis=0,
        )
        put(list_out, piece, begins[b] + tile * LANES, sizes[b] - tile * LANES)

    for b in range(1, count):
        place(b, 0)
    longest = functools.reduce(jnp.maximum, sizes[1:], jnp.int32(0))

    @pl.when(longest > LANES)
    def _():
        def bring_more(tile, _):
            bring(pl.ds(pl.multiple_of(tile * LANES, LANES), LANES))
            return 0

        lax.fori_loop(1, (longest + LANES - 1) // LANES, bring_more, 0)
        for b in range(1, count):

            def more(tile, _, b=b):
                place(b, tile)
                return 0

            lax.fori_loop(1, (sizes[b] + LANES - 1) // LANES, more, 0)

    return start, filled


def prepare_kernel(*refs):
    given, outs, held, sems = refs[:5], refs[5:12], refs[12:17], refs[17]
    copies = [
        pltpu.make_async_copy(source, target, sems.at[k])
        for k, (source, target) in enumerate(zip(given, held))
    ]
    for copy in copies:
        copy.start()
    for copy in copies:
        copy.wait()
    in_ref, mid_ref, out_ref, embed_ref, readout_ref = held
    rows = jnp.concatenate([embed_ref[...], readout_ref[...]], axis=0)
    small = outs[6]
    small[...] = jnp.zeros_like(small)
    small[0 : rows.shape[0], :] = rows
    for layer in range(in_ref.shape[0]):
        into = in_ref[layer]
        middle = mid_ref[layer]
        last = out_ref[layer]
        in_fw, mid_fw, out_fw, in_bw, mid_bw, out_bw = (out.at[layer] for out in outs[:6])
        in_fw[...] = stack_weights(into)
        mid_fw[...] = stack_weights(middle)
        out_fw[...] = stack_weights(last)
        into_t = jnp.concatenate([into, jnp.zeros_like(into)], axis=0).T
        in_bw[...] = stack_weights(into_t)
        mid_bw[...] = stack_weights(middle.T)
        high, low = split(last)
        out_bw[...] = jnp.concatenate([high, low, high], axis=1)


def multiples(dist, count):
    turn = dist * (math.pi / CUTOFF) - 0.5 * math.pi
    square = turn * turn
    high = 1.0 / math.factorial(15)
    sine_turn = -high * square + 1.0 / math.factorial(13)
    for order in (11, 9, 7, 5, 3, 1):
        sign = 1.0 if order % 4 == 1 else -1.0
        sine_turn = sine_turn * square + sign / math.factorial(order)
    cosine_turn = square * (1.0 / math.factorial(16)) - 1.0 / math.factorial(14)
    for order in (12, 10, 8, 6, 4, 2, 0):
        sign = 1.0 if order % 4 == 0 else -1.0
        cosine_turn = cosine_turn * square + sign / math.factorial(order)
    s, c = cosine_turn, -sine_turn * turn
    order = iota((count, dist.shape[1]), 0) + 1
    sine = jnp.zeros(order.shape, F32)
    cosine = jnp.ones(order.shape, F32)
    bit = 1
    while True:
        here = jnp.bitwise_and(order, bit) > 0
        more_s = sine * c + cosine * s
        more_c = cosine * c - sine * s
        sine = jnp.where(here, more_s, sine)
        cosine = jnp.where(here, more_c, cosine)
        bit *= 2
        if bit > count:
            return sine, cosine
        s, c = 2.0 * s * c, 1.0 - 2.0 * s * s


def geometry(chunk, need_slopes):
    vec = [chunk[k : k + 1] for k in range(3)]
    dist = jnp.sqrt(vec[0] * vec[0] + vec[1] * vec[1] + vec[2] * vec[2])
    inv = 1.0 / dist
    ux, uy, uz = (v * inv for v in vec)
    values = [
        jnp.ones_like(dist),
        ROOT3 * ux,
        ROOT3 * uy,
        ROOT3 * uz,
        ROOT15 * ux * uy,
        ROOT15 * uy * uz,
        0.5 * ROOT5 * (3.0 * uz * uz - 1.0),
        ROOT15 * ux * uz,
        0.5 * ROOT15 * (ux * ux - uy * uy),
    ]
    sine, cosine = multiples(dist, 8)
    scale = math.sqrt(2.0 / CUTOFF) * inv
    basis = sine * scale
    x = dist * (1.0 / CUTOFF)
    x2 = x * x
    x4 = x2 * x2
    envelope = 1.0 + x4 * x * (-21.0 + x * (35.0 - 15.0 * x))
    slopes = None
    if need_slopes:
        orders = (iota(sine.shape, 0) + 1).astype(F32) * (math.pi / CUTOFF)
        d_basis = orders * cosine * scale - basis * inv
        d_envelope = x4 * (-105.0 + x * (210.0 - 105.0 * x)) * (1.0 / CUTOFF)
        slopes = (d_basis, d_envelope)
    return inv, (ux, uy, uz), values, basis, envelope, slopes


def radial_hidden(basis, in_fw, mid_fw):
    z1 = dot(in_fw, stack_acts_f32(basis))
    z2 = dot(mid_fw, stack_acts(z1 * sigmoid(z1)))
    return z1, z2


def own_hot(chunk, own):
    target = chunk[3:4].astype(jnp.int32)
    return (iota((own, target.shape[1]), 0) == target).astype(F32).astype(BF16)


def scaled_hots(chunk, own, values):
    hot = own_hot(chunk, own)
    out = []
    for begin, size in SPANS:
        pairs = [split(values[m]) for m in range(begin, begin + size)]
        out.append(
            jnp.concatenate([hot * high for high, _ in pairs] + [hot * low for _, low in pairs], axis=0)
        )
    return out


def other_hot(chunk, own, total):
    atom = chunk[4:5].astype(jnp.int32)
    hot = (iota((own, atom.shape[1]), 0) == atom).astype(F32).astype(BF16)
    block = chunk[5:6]
    return jnp.concatenate(
        [hot * (block == float(b)).astype(F32).astype(BF16) for b in range(total // own)], axis=0
    )


def lanes_at(start, size):
    return pl.ds(pl.multiple_of(start, LANES), size)


def sweep(start, stop, body):
    start = lax.shift_left(lax.shift_right_arithmetic(start, 7), 7)
    for size in STEPS:
        rest = jnp.maximum(stop - start, 0)
        number = (rest + (STEPS[-1] if size != STEPS[-1] else size) - 1) // size

        def step(index, _, start=start, size=size):
            body(lanes_at(start + index * size, size), size)
            return 0

        lax.fori_loop(0, number, step, 0)
        start = start + number * size


def kind_columns(small, kinds, mix):
    mixed = dot_high(small[0:kinds, :], mix)
    return [mixed[k : k + 1].T for k in range(kinds)]


def kind_features(chunk, columns):
    kind = chunk[7:8]
    out = jnp.where(kind == 0.0, columns[0], 0.0)
    for index in range(1, len(columns)):
        out = out + jnp.where(kind == float(index), columns[index], 0.0)
    return out


def collect(amat, chunk, feat, values, envelope, z2, out_fw, own):
    width = feat.shape[0]
    units = z2 * sigmoid(z2) * (INV_COUNT * envelope)
    weights = dot(out_fw, stack_acts(units))
    hots = scaled_hots(chunk, own, values)
    for degree, (begin, size) in enumerate(SPANS):
        high, low = split(weights[degree * width : (degree + 1) * width] * feat)
        parts = dot(hots[degree], jnp.concatenate([high, low], axis=0), NT)
        rows = size * own
        at = slice(begin * own, (begin + size) * own)
        amat[at, :] += (parts[:rows, :width] + parts[:rows, width:]) + (
            parts[rows:, :width] + parts[rows:, width:]
        )


def node_forward(amat, features, update, own):
    parts = [amat[m * own : (m + 1) * own, :] for m in range(9)]
    inv1 = sum(p * p for p in parts[1:4])
    inv2 = sum(p * p for p in parts[4:9])
    preact = dot_high(jnp.concatenate([parts[0], inv1, inv2], axis=1), update)
    return features + preact * sigmoid(preact), preact


def node_back(amat, d_features, preact, update, own, d_amat):
    width = d_features.shape[1]
    gate = sigmoid(preact)
    d_pre = d_features * gate * (1.0 + preact * (1.0 - gate))
    d_inv = dot_high(d_pre, update, NT)
    for degree, (begin, size) in enumerate(SPANS):
        for m in range(begin, begin + size):
            value = d_inv[:, degree * width : (degree + 1) * width]
            if degree > 0:
                value = 2.0 * amat[m * own : (m + 1) * own, :] * value
            high, low = split_f32(value)
            turned = jnp.concatenate([high, low], axis=0).T
            d_amat[m * width : (m + 1) * width, :] = turned.astype(BF16)


def edge_backward(chunk, feat, hidden, own, in_fw, mid_fw, out_fw, in_bw, mid_bw, out_bw, d_amat):
    width = feat.shape[0]
    inv, unit, values, basis, envelope, (d_basis, d_envelope) = geometry(chunk, True)
    z1, z2 = radial_hidden(basis, in_fw, mid_fw) if hidden is None else hidden
    gate1, gate2 = sigmoid(z1), sigmoid(z2)
    scale = INV_COUNT * envelope
    units = z2 * gate2
    weights = dot(out_fw, stack_acts(units * scale))
    hot = own_hot(chunk, own)
    rows = dot(d_amat[...], jnp.concatenate([hot, hot], axis=0))
    pulled = []
    d_mixed = 0.0
    d_values = []
    for degree, (begin, size) in enumerate(SPANS):
        weight = weights[degree * width : (degree + 1) * width]
        product = weight * feat
        term = 0.0
        for m in range(begin, begin + size):
            row = rows[m * width : (m + 1) * width]
            if m == 0:
                term = row
                d_values.append(None)
                continue
            term = term + row * values[m]
            d_values.append(jnp.sum(row * product, axis=0, keepdims=True))
        d_mixed = d_mixed + weight * term
        pulled.append(feat * term)
    pulled = jnp.concatenate(pulled, axis=0)
    d_units = dot(out_bw, stack_three(pulled))
    d_env = INV_COUNT * jnp.sum(units * d_units, axis=0, keepdims=True)
    d_z2 = d_units * scale * gate2 * (1.0 + z2 * (1.0 - gate2))
    d_hidden = dot(mid_bw, stack_acts(d_z2))
    d_z1 = d_hidden * gate1 * (1.0 + z1 * (1.0 - gate1))
    d_b = dot(in_bw, stack_acts(d_z1))[0:8]
    d_dist = jnp.sum(d_b * d_basis, axis=0, keepdims=True) + d_env * d_envelope
    ux, uy, uz = unit
    y = d_values
    dux = ROOT3 * y[1] + ROOT15 * (uy * y[4] + uz * y[7] + ux * y[8])
    duy = ROOT3 * y[2] + ROOT15 * (ux * y[4] + uz * y[5] - uy * y[8])
    duz = ROOT3 * y[3] + ROOT15 * (uy * y[5] + ux * y[7]) + 3.0 * ROOT5 * uz * y[6]
    along = ux * dux + uy * duy + uz * duz
    grad = [(du - u * along) * inv + d_dist * u for u, du in zip(unit, (dux, duy, duz))]
    return grad, d_mixed


def first_sums(list_ref, start, stop, amat, columns, in_fw, mid_fw, out_fw, own):
    def body(at, _):
        chunk = list_ref[:, at]
        _, _, values, basis, envelope, _ = geometry(chunk, False)
        _, z2 = radial_hidden(basis, in_fw[0], mid_fw[0])
        feat = kind_features(chunk, columns)
        collect(amat, chunk, feat, values, envelope, z2, out_fw[0], own)

    sweep(start, stop, body)


def second_sums(list_ref, start, stop, amat, features_t, in_fw, mid_fw, out_fw, own, keep):
    total = features_t.shape[1]

    def body(at, _):
        chunk = list_ref[:, at]
        _, _, values, basis, envelope, _ = geometry(chunk, False)
        z1, z2 = radial_hidden(basis, in_fw[1], mid_fw[1])
        feat = gather(features_t, other_hot(chunk, own, total))
        if keep is not None:
            for kept, value in zip(keep, (feat, z1, z2)):
                kept[:, at] = value
        collect(amat, chunk, feat, values, envelope, z2, out_fw[1], own)

    sweep(start, stop, body)


def turn_features(features, features_t):
    high, low = split_f32(features.T)
    features_t[...] = jnp.concatenate([high, low], axis=0).astype(BF16)


def gather(features_t, hot):
    both = dot(features_t[...], hot)
    width = both.shape[0] // 2
    return both[:width] + both[width:]


def scatter_back(d_mixed_sum, hot, d_mixed):
    width = d_mixed.shape[0]
    high, low = split(d_mixed)
    both = dot(hot, jnp.concatenate([high, low], axis=0), NT)
    d_mixed_sum[...] += both[:, :width] + both[:, width:]


def rows_of(grad):
    return jnp.concatenate(grad + [jnp.zeros((5, grad[0].shape[1]), F32)], axis=0)


def split_three(pull):
    high, rest = split_f32(pull)
    middle, low = split_f32(rest)
    return jnp.concatenate([high, middle, low, jnp.zeros_like(low)], axis=0).astype(BF16)


def add_three(moved):
    return moved[0:8] + moved[8:16] + moved[16:24]


def inner_first_kernel(own, edges, kinds, *refs):
    (record, small, mix_ref, in_fw, mid_fw, out_fw, list_out, number_out, amat_out) = refs
    number = build_inner(own, edges, record, list_out)
    number_out[0] = number
    amat_out[...] = jnp.zeros_like(amat_out)
    columns = kind_columns(small, kinds, mix_ref[0])
    first_sums(list_out, 0, number, amat_out, columns, in_fw, mid_fw, out_fw, own)


def outer_first_kernel(hood, sections, own, edges, kinds, *refs):
    (
        got,
        inner_amat,
        small,
        mix_ref,
        update_ref,
        in_fw,
        mid_fw,
        out_fw,
        list_out,
        range_out,
        amat_out,
        preact_out,
        h_out,
        w_out,
        fields,
        sources,
    ) = refs
    start, stop = build_outer(hood, sections, own, edges, got, list_out, fields, sources)
    range_out[0] = start
    range_out[1] = stop
    amat_out[...] = inner_amat[...]
    columns = kind_columns(small, kinds, mix_ref[0])
    first_sums(list_out, start, stop, amat_out, columns, in_fw, mid_fw, out_fw, own)
    kind = got[5:6, 0:own].astype(jnp.int32)
    hot = (iota((8, own), 0) == kind).astype(F32).T
    rows = jnp.where(iota((8, small.shape[1]), 0) < kinds, small[...], 0.0)
    features = dot_high(hot, rows)
    h, preact = node_forward(amat_out, features, update_ref[0], own)
    preact_out[...] = preact
    h_out[...] = h
    w_out[...] = dot_high(h, mix_ref[1])


def inner_second_kernel(own, *refs):
    (number_ref, list_ref, w_ref, in_fw, mid_fw, out_fw, amat_out, features_t) = refs
    amat_out[...] = jnp.zeros_like(amat_out)
    turn_features(w_ref[...], features_t)
    second_sums(
        list_ref, 0, number_ref[0], amat_out, features_t, in_fw, mid_fw, out_fw, own, None
    )


def outer_second_kernel(count, own, kinds, *refs):
    (
        everyone_ref,
        range_ref,
        list_ref,
        inner_amat,
        h_ref,
        update_ref,
        small,
        in_fw,
        mid_fw,
        out_fw,
        in_bw,
        mid_bw,
        out_bw,
        energy_out,
        grad_out,
        d_mixed_sum,
        d_amat,
        features_t,
        amat,
        kept_feat,
        kept_first,
        kept_second,
    ) = refs
    total = count * own
    start, stop = range_ref[0], range_ref[1]
    turn_features(everyone_ref[...], features_t)
    amat[...] = inner_amat[...]
    d_mixed_sum[...] = jnp.zeros_like(d_mixed_sum)
    keep = (kept_feat, kept_first, kept_second)
    second_sums(list_ref, start, stop, amat, features_t, in_fw, mid_fw, out_fw, own, keep)
    h1 = h_ref[...]
    h2, preact = node_forward(amat, h1, update_ref[1], own)
    readout = small[kinds : kinds + 2, :]
    energy_out[...] = dot_high(readout[0:1], h1, NT) + dot_high(readout[1:2], h2, NT)
    d_features = jnp.broadcast_to(readout[1:2], h1.shape)
    node_back(amat, d_features, preact, update_ref[1], own, d_amat)
    weights = [ref[1] for ref in (in_fw, mid_fw, out_fw, in_bw, mid_bw, out_bw)]

    def backward(at, _):
        chunk = list_ref[:, at]
        hidden = (kept_first[:, at], kept_second[:, at])
        grad, d_mixed = edge_backward(chunk, kept_feat[:, at], hidden, own, *weights, d_amat)
        grad_out[:, at] = rows_of(grad)
        scatter_back(d_mixed_sum, other_hot(chunk, own, total), d_mixed)

    sweep(start, stop, backward)


def inner_second_back_kernel(own, *refs):
    (number_ref, list_ref, w_ref, d_amat) = refs[:4]
    weights = [ref[1] for ref in refs[4:10]]
    grad_out, d_mixed_sum, features_t = refs[10:]
    d_mixed_sum[...] = jnp.zeros_like(d_mixed_sum)
    turn_features(w_ref[...], features_t)

    def backward(at, _):
        chunk = list_ref[:, at]
        hot = other_hot(chunk, own, own)
        grad, d_mixed = edge_backward(
            chunk, gather(features_t, hot), None, own, *weights, d_amat
        )
        grad_out[:, at] = rows_of(grad)
        scatter_back(d_mixed_sum, hot, d_mixed)

    sweep(0, number_ref[0], backward)


def outer_first_back_kernel(count, own, kinds, *refs):
    (
        d_mixed_ref,
        inner_d_mixed,
        range_ref,
        list_ref,
        grad_ref,
        amat_ref,
        preact_ref,
        small,
        mix_ref,
        update_ref,
    ) = refs[:10]
    weights = [ref[0] for ref in refs[10:16]]
    force_out, d_amat, force = refs[16:]
    total = count * own
    columns = kind_columns(small, kinds, mix_ref[0])
    readout = small[kinds : kinds + 2, :]
    d_mixed = d_mixed_ref[...] + inner_d_mixed[...]
    d_features = readout[0:1] + readout[1:2] + dot_high(d_mixed, mix_ref[1], NT)
    node_back(amat_ref, d_features, preact_ref[...], update_ref[0], own, d_amat)
    force[...] = jnp.zeros_like(force)

    def backward(at, _):
        chunk = list_ref[:, at]
        feat = kind_features(chunk, columns)
        grad, _ = edge_backward(chunk, feat, None, own, *weights, d_amat)
        parts = split_three(rows_of(grad) + grad_ref[:, at])
        force[...] -= add_three(dot(parts, other_hot(chunk, own, total), NT))
        force[:, 0:own] += add_three(dot(parts, own_hot(chunk, own), NT))

    sweep(range_ref[0], range_ref[1], backward)
    for b in range(count):
        force_out[8 * b : 8 * b + 8, :] = force[:, b * own : (b + 1) * own]


def inner_first_back_kernel(own, kinds, *refs):
    (number_ref, list_ref, grad_ref, d_amat, small, mix_ref) = refs[:6]
    weights = [ref[0] for ref in refs[6:12]]
    force_out = refs[12]
    columns = kind_columns(small, kinds, mix_ref[0])
    force_out[...] = jnp.zeros_like(force_out)

    def backward(at, _):
        chunk = list_ref[:, at]
        feat = kind_features(chunk, columns)
        grad, _ = edge_backward(chunk, feat, None, own, *weights, d_amat)
        parts = split_three(rows_of(grad) + grad_ref[:, at])
        hot = own_hot(chunk, own) - other_hot(chunk, own, own)
        force_out[...] += add_three(dot(parts, hot, NT))

    sweep(0, number_ref[0], backward)


LIMIT = 48 * 1024 * 1024


def call(kernel, outs, scratch, args, smem_in=(), smem_out=(), micros=4):
    vmem = pl.BlockSpec(memory_space=pltpu.VMEM)
    smem = pl.BlockSpec(memory_space=pltpu.SMEM)
    return pl.pallas_call(
        kernel,
        out_shape=outs,
        in_specs=[smem if k in smem_in else vmem for k in range(len(args))],
        out_specs=[smem if k in smem_out else vmem for k in range(len(outs))],
        scratch_shapes=scratch,
        compiler_params=pltpu.CompilerParams(vmem_limit_bytes=LIMIT),
        cost_estimate=pl.CostEstimate(
            flops=micros * 1000 * 1000 * 1000, bytes_accessed=micros * 1000 * 1000, transcendentals=0
        ),
    )(*args)


def call_copying(kernel, outs, args, megabytes):
    vmem = pl.BlockSpec(memory_space=pltpu.VMEM)
    return pl.pallas_call(
        kernel,
        out_shape=outs,
        in_specs=[pl.BlockSpec(memory_space=pltpu.HBM)] * len(args),
        out_specs=[vmem] * len(outs),
        scratch_shapes=[pltpu.VMEM(value.shape, value.dtype) for value in args]
        + [pltpu.SemaphoreType.DMA((len(args),))],
        compiler_params=pltpu.CompilerParams(vmem_limit_bytes=megabytes * 1024 * 1024),
    )(*args)


def shards(
    sizes,
    species,
    send_x,
    send_y,
    send_z,
    edge_first,
    edge_second,
    edge_live,
    edge_vec,
    embed,
    radial_in,
    radial_mid,
    radial_out,
    mix,
    update,
    readout,
):
    hood = Neighbourhood(sizes)
    count = hood.count
    own = species.shape[0]
    width = embed.shape[1]
    layers = readout.shape[0]
    hidden = radial_mid.shape[1]
    slots = edge_first.shape[1]
    edges = round_up(slots, BLOCK)
    extra = edges - slots
    if extra:
        edge_first = jnp.pad(edge_first, ((0, 0), (0, extra)))
        edge_second = jnp.pad(edge_second, ((0, 0), (0, extra)))
        edge_live = jnp.pad(edge_live, ((0, 0), (0, extra)))
        edge_vec = jnp.pad(edge_vec, ((0, 0), (0, extra)), constant_values=1.0)
    faces = tuple(send.shape[2] for send in (send_z, send_y, send_x))
    sections = Sections(own, faces)
    shape = jax.ShapeDtypeStruct
    kinds = embed.shape[0]
    packed = call_copying(
        pack_kernel,
        [shape((8, edges), F32)],
        [species[None, :], send_x, send_y, send_z, edge_first, edge_second, edge_live, edge_vec],
        60,
    )[0]
    *weights, small = call_copying(
        prepare_kernel,
        [
            shape((layers, hidden, 32), BF16),
            shape((layers, hidden, 4 * hidden), BF16),
            shape((layers, 3 * width, 4 * hidden), BF16),
            shape((layers, 16, 4 * hidden), BF16),
            shape((layers, hidden, 4 * hidden), BF16),
            shape((layers, hidden, 9 * width), BF16),
            shape((8, width), F32),
        ],
        [radial_in, radial_mid, radial_out, embed, readout],
        16,
    )
    forward_weights = weights[:3]
    sums = shape((9 * own, width), F32)
    rows = shape((own, width), F32)
    turned = shape((9 * width, 2 * own), BF16)
    inner_size = round_up(2 * edges + LANES, STEPS[0]) + STEPS[0]
    outer_size = round_up((count + 1) * edges + LANES, STEPS[0]) + STEPS[0]

    got, along_x = hood.fetch(packed)
    inner_list, number, inner_amat = call(
        functools.partial(inner_first_kernel, own, edges, kinds),
        [shape((8, inner_size), F32), shape((1,), jnp.int32), sums],
        [],
        [along_x, small, mix] + forward_weights,
        smem_out=(1,),
    )
    outer_list, bounds, amat1, preact1, h1, w2 = call(
        functools.partial(outer_first_kernel, hood, sections, own, edges, kinds),
        [shape((8, outer_size), F32), shape((2,), jnp.int32), sums, rows, rows, rows],
        [
            pltpu.VMEM((6, round_up(count, 8), edges), F32),
            pltpu.VMEM((round_up(count, 8), edges), jnp.int32),
        ],
        [got, inner_amat, small, mix, update] + forward_weights,
        smem_out=(1,),
    )

    everyone, _ = hood.fetch(w2)
    (inner_amat,) = call(
        functools.partial(inner_second_kernel, own),
        [sums],
        [pltpu.VMEM((2 * width, own), BF16)],
        [number, inner_list, w2] + forward_weights,
        smem_in=(0,),
    )
    energies, grads, d_mixed, d_amat2 = call(
        functools.partial(outer_second_kernel, count, own, kinds),
        [shape((1, own), F32), shape((8, outer_size), F32), shape((count * own, width), F32), turned],
        [
            pltpu.VMEM((2 * width, count * own), BF16),
            pltpu.VMEM((9 * own, width), F32),
            pltpu.VMEM((width, outer_size), F32),
            pltpu.VMEM((hidden, outer_size), F32),
            pltpu.VMEM((hidden, outer_size), F32),
        ],
        [everyone, bounds, outer_list, inner_amat, h1, update, small] + weights,
        smem_in=(1,),
    )

    inner_grads, inner_d_mixed = call(
        functools.partial(inner_second_back_kernel, own),
        [shape((8, inner_size), F32), rows],
        [pltpu.VMEM((2 * width, own), BF16)],
        [number, inner_list, w2, d_amat2] + weights,
        smem_in=(0,),
    )
    d_mixed, inner_d_mixed = hood.give(d_mixed, inner_d_mixed)
    forces, d_amat1 = call(
        functools.partial(outer_first_back_kernel, count, own, kinds),
        [shape((8 * count, own), F32), turned],
        [pltpu.VMEM((8, count * own), F32)],
        [d_mixed, inner_d_mixed, bounds, outer_list, grads, amat1, preact1, small, mix, update]
        + weights,
        smem_in=(2,),
    )

    (inner_forces,) = call(
        functools.partial(inner_first_back_kernel, own, kinds),
        [shape((8, own), F32)],
        [],
        [number, inner_list, inner_grads, d_amat1, small, mix] + weights,
        smem_in=(0,),
    )
    forces, inner_forces = hood.give(forces, inner_forces)
    return (energies.reshape(own), forces[:3] + inner_forces[:3])


def solution(mesh):
    sizes = tuple(mesh.shape[axis] for axis in ("gx", "gy", "gz"))
    split_all = ("parts", "gx", "gy", "gz")
    return jax.shard_map(
        functools.partial(shards, sizes),
        mesh=mesh,
        in_specs=(
            P(split_all),
            P(split_all, None, None),
            P(split_all, None, None),
            P(split_all, None, None),
            P(split_all, None),
            P(split_all, None),
            P(split_all, None),
            P(None, split_all),
            P(),
            P(),
            P(),
            P(),
            P(),
            P(),
            P(),
        ),
        out_specs=(P(split_all), P(None, split_all)),
        check_vma=False,
    )
```
